32 devices in a mesh: row: 8 (over z, core), col: 4 (over y, x).
Axes of the slice: x: 2, y: 2, z: 4, core: 2. Of those that a mesh axis runs over, the one named last changes fastest.
Arguments:
- spans: bfloat16 [4096, 768], P(('row', 'col')), may hold values from -10 to 10
- centroids: bfloat16 [2048, 768], P(('col', 'row')), may hold values from -10 to 10
- pattern: int32 [32, 4], P('row'), may hold values from 0 to 15, as said below
Outputs:
- new_centroids: bfloat16 [2048, 768], P(('col', 'row'))
- row_potential: float32 [4096], P('row')
- col_potential: float32 [2048], P('col')
The draws below stay inside these ranges and needn't reach their ends.
Inputs may be any that keep to these rules, and one draw needn't show every extreme that they name: `pattern`: each row lists 4 distinct centroid blocks in rising order; row b always lists block b % 16; every centroid block is listed by some row.
All inputs are finite; a program needn't handle non-finite values.
Results may differ from the reference program's by a relative error of at most 0.0095.
Values may be sent and summed in bfloat16 or wider, within the bound.
No kernel may reach another device: no remote copies, remote signals or barrier semaphores. Data moves between devices by JAX's collectives and lax.ppermute only.
A program may use at most 64 MiB of HBM per device.

```python
import math
import jax
import jax.numpy as jnp
from jax import lax

E = 768
ITERS = 3
NCH = 4096
K = 2048
RB = 32
CB = 16
NNZ = 4


def pair_signs(key):
    flips = jax.random.bernoulli(jax.random.fold_in(key, 21), 0.5, (K // 2, E))
    return jnp.where(flips, 1.0, -1.0).astype(jnp.float32)


def lead_magnitude():
    return math.sqrt(16.0 * 170.0 / E)


def centroid_table(key):
    base = jax.random.truncated_normal(jax.random.fold_in(key, 12), -4.0, 4.0, (K, E), jnp.float32)
    signs = jnp.repeat(pair_signs(key), 2, axis=0)
    index = jnp.arange(K, dtype=jnp.int32)
    local = index % 128
    leading = local % 16 == 0
    partner = local % 16 == 1
    magnitude = lead_magnitude()
    table = jnp.where(leading[:, None], magnitude * signs, base)
    table = jnp.where(partner[:, None], 0.99 * magnitude * signs, table)
    return table


def draw_centroids(key, part):
    return centroid_table(key).astype(jnp.bfloat16)


def draw_spans(key, part):
    signs = pair_signs(key)
    values = jax.random.truncated_normal(jax.random.fold_in(key, 15), -4.0, 4.0, (NCH, E), jnp.float32)
    index = jnp.arange(NCH, dtype=jnp.int32)
    target_block = index // 128 % CB
    target = target_block * 128 + 16 * (index * 37 % 8)
    level = index // 61 % 3
    strength = jnp.where(level == 0, 130.0, jnp.where(level == 1, 180.0, 240.0)).astype(jnp.float32)
    amount = strength * 16.0 / (E * lead_magnitude())
    chosen = index % 61 == 0
    aligned = amount[:, None] * signs[target // 2]
    return jnp.where(chosen[:, None], aligned, values).astype(jnp.bfloat16)


def draw_pattern(key, part):
    columns = jnp.arange(CB, dtype=jnp.int32)
    raw_scores = jax.random.randint(jax.random.fold_in(key, 16), (RB, CB), 0, 65536, jnp.int32) * CB + columns[None, :]
    home = jnp.arange(RB, dtype=jnp.int32) % CB
    raw_scores = jnp.where(columns[None, :] == home[:, None], 65536 * CB + CB, raw_scores)
    unused, picked = lax.top_k(raw_scores, NNZ)
    return jnp.sort(picked, axis=1).astype(jnp.int32)


def setup_inputs(seed: int = 0) -> dict:
    splits = jax.random.split(jax.random.key(seed), 4)
    return {
        "spans": draw_spans(jax.random.fold_in(splits[3], 71), 0),
        "centroids": draw_centroids(jax.random.fold_in(splits[3], 71), 0),
        "pattern": draw_pattern(jax.random.fold_in(splits[3], 71), 0),
    }


def reference(spans, centroids, pattern):
    span_blocks = spans.reshape(RB, 128, E)
    centroid_blocks = centroids.reshape(CB, 128, E)

    def block_scores(inputs):
        span_block, listed = inputs
        picked = centroid_blocks[listed]
        return jnp.einsum("ie,nje->nij", span_block.astype(jnp.float32), picked.astype(jnp.float32)) * 0.0625

    scores = lax.map(block_scores, (span_blocks, pattern))
    flat_ids = pattern.reshape(-1)
    col_pot = jnp.zeros((CB, 128), jnp.float32)
    row_pot = jnp.zeros((RB, 128), jnp.float32)
    log_target = jnp.log(jnp.float32(NCH) / jnp.float32(K))
    for sweep in range(ITERS):
        shifted = scores + col_pot[pattern][:, :, None, :]
        row_high = jnp.max(shifted, axis=(1, 3))
        row_sum = jnp.sum(jnp.exp(shifted - row_high[:, None, :, None]), axis=(1, 3))
        row_pot = -(row_high + jnp.log(row_sum))
        shifted = scores + row_pot[:, None, :, None]
        block_high = jnp.max(shifted, axis=2).reshape(-1, 128)
        col_high = jax.ops.segment_max(block_high, flat_ids, num_segments=CB)
        block_sum = jnp.sum(jnp.exp(shifted - col_high[pattern][:, :, None, :]), axis=2).reshape(-1, 128)
        col_sum = jax.ops.segment_sum(block_sum, flat_ids, num_segments=CB)
        col_pot = log_target - (col_high + jnp.log(col_sum))
    plan = jnp.exp(scores + row_pot[:, None, :, None] + col_pot[pattern][:, :, None, :]).astype(jnp.bfloat16)

    def accumulate(running, inputs):
        plan_block, span_block, listed = inputs
        term = jnp.einsum("nij,ie->nje", plan_block.astype(jnp.float32), span_block.astype(jnp.float32))
        return running.at[listed].add(term), None

    start_sum = jnp.zeros((CB, 128, E), jnp.float32)
    summed, unused = lax.scan(accumulate, start_sum, (plan, span_blocks, pattern))
    mass_ratio = jnp.float32(K) / jnp.float32(NCH)
    new_centroids = (summed.reshape(K, E) * mass_ratio).astype(jnp.bfloat16)
    return new_centroids, row_pot.reshape(NCH), col_pot.reshape(K)
```

```python
import math

import jax
import jax.numpy as jnp
from jax import lax
from jax.sharding import PartitionSpec as P

ITERS = 3


logit_scale = 0.0625
floor_value = -1e30


def stages_of(n):
    bits = n.bit_length() - 1
    out = []
    shift = 0
    while shift < bits:
        width = min(3, bits - shift)
        out.append((shift, width))
        shift += width
    return out


def swap(x, axis, k):
    n = lax.axis_size(axis)
    return lax.ppermute(x, axis, [(i, i ^ k) for i in range(n)])


def digit(axis, shift, width):
    return (lax.axis_index(axis) >> shift) & ((1 << width) - 1)


def gather_rows(x, axis):
    for shift, width in stages_of(lax.axis_size(axis)):
        parts = [x] + [swap(x, axis, k << shift) for k in range(1, 1 << width)]
        me = digit(axis, shift, width)
        whole = jnp.zeros((1 << width,) + x.shape, x.dtype)
        for k, part in enumerate(parts):
            whole = lax.dynamic_update_index_in_dim(whole, part, me ^ k, 0)
        x = whole.reshape((-1,) + x.shape[1:])
    return x


def tree(op, parts):
    while len(parts) > 1:
        parts = [op(parts[i], parts[i + 1]) for i in range(0, len(parts), 2)]
    return parts[0]


def log_sum_over(x, axis):
    for shift, width in stages_of(lax.axis_size(axis)):
        parts = [x] + [swap(x, axis, k << shift) for k in range(1, 1 << width)]
        high = tree(jnp.maximum, parts)
        total = tree(jnp.add, [jnp.exp(part - high) for part in parts])
        x = high + jnp.log(total)
    return x


def scatter_sum(x, axis):
    n = lax.axis_size(axis)
    rows = x.shape[0] // n
    x = x.reshape((n, rows) + x.shape[1:])
    for shift, width in stages_of(n):
        size = 1 << width
        me = digit(axis, shift, width)
        x = x.reshape((-1, size) + x.shape[1:])
        own = lax.dynamic_index_in_dim(x, me, 1, keepdims=False)
        low = x.astype(jnp.bfloat16)
        got = [
            swap(lax.dynamic_index_in_dim(low, me ^ k, 1, keepdims=False), axis, k << shift)
            for k in range(1, size)
        ]
        x = tree(jnp.add, [own] + [part.astype(jnp.float32) for part in got])
    return x[0]


def per_device(spans, centroids, pattern):
    span_rows = gather_rows(spans, "col")
    all_centroids = gather_rows(centroids, "row")
    row_count = span_rows.shape[0]
    group_cols = all_centroids.shape[0]
    scores = (
        lax.dot_general(
            span_rows, all_centroids, (((1,), (1,)), ((), ())), preferred_element_type=jnp.float32
        )
        * logit_scale
    )
    row_blocks = row_count // 128
    col_blocks = group_cols // 128
    block_ids = lax.axis_index("col") * col_blocks + jnp.arange(col_blocks, dtype=jnp.int32)
    listed = jnp.any(pattern[:, :, None] == block_ids[None, None, :], axis=1)
    allowed_cells = jnp.broadcast_to(
        listed[:, None, :, None], (row_blocks, 128, col_blocks, 128)
    ).reshape(row_count, group_cols)
    scores = jnp.where(allowed_cells, scores, floor_value)
    mass_ratio = group_cols * lax.axis_size("col") / (row_count * lax.axis_size("row"))
    log_target = -math.log(mass_ratio)
    col_pot = jnp.zeros((group_cols,), jnp.float32)
    row_pot = jnp.zeros((row_count,), jnp.float32)
    for sweep in range(ITERS):
        shifted = scores + col_pot[None, :]
        row_high = jnp.max(shifted, axis=1)
        row_sum = jnp.sum(jnp.exp(shifted - row_high[:, None]), axis=1)
        row_pot = -log_sum_over(row_high + jnp.log(row_sum), "col")
        shifted = scores + row_pot[:, None]
        col_high = jnp.max(shifted, axis=0)
        col_sum = jnp.sum(jnp.exp(shifted - col_high[None, :]), axis=0)
        col_pot = log_target - log_sum_over(col_high + jnp.log(col_sum), "row")
    weights = jnp.exp(scores + row_pot[:, None] + col_pot[None, :]).astype(jnp.bfloat16)
    centroid_sum = scatter_sum(
        lax.dot_general(
            weights, span_rows, (((0,), (0,)), ((), ())), preferred_element_type=jnp.float32
        ),
        "row",
    )
    return ((centroid_sum * mass_ratio).astype(jnp.bfloat16), row_pot, col_pot)


def solution(mesh):
    placed = (P(("row", "col"), None), P(("col", "row"), None), P("row", None))
    return jax.shard_map(
        per_device,
        mesh=mesh,
        in_specs=placed,
        out_specs=(P(("col", "row"), None), P("row"), P("col")),
        check_vma=False,
    )
```

```python
import math

import jax
import jax.numpy as jnp
from jax import lax
from jax.sharding import PartitionSpec as P

ITERS = 3


logit_scale = 0.0625
floor_value = -1e30


def gather_rows(x, axis):
    n = lax.axis_size(axis)
    copies = jnp.broadcast_to(x[None], (n,) + x.shape)
    whole = lax.all_to_all(copies, axis, 0, 0, tiled=True)
    return whole.reshape((-1,) + x.shape[1:])


def log_sum_over(x, axis):
    parts = gather_rows(x[None], axis)
    high = jnp.max(parts, axis=0)
    return high + jnp.log(jnp.sum(jnp.exp(parts - high[None]), axis=0))


def scatter_sum(x, axis):
    n = lax.axis_size(axis)
    low = x.astype(jnp.bfloat16).reshape((n, -1) + x.shape[1:])
    got = lax.all_to_all(low, axis, 0, 0, tiled=True)
    return jnp.sum(got.astype(jnp.float32), axis=0)


def per_device(spans, centroids, pattern):
    span_rows = gather_rows(spans, "col")
    all_centroids = gather_rows(centroids, "row")
    row_count = span_rows.shape[0]
    group_cols = all_centroids.shape[0]
    scores = (
        lax.dot_general(
            span_rows, all_centroids, (((1,), (1,)), ((), ())), preferred_element_type=jnp.float32
        )
        * logit_scale
    )
    row_blocks = row_count // 128
    col_blocks = group_cols // 128
    block_ids = lax.axis_index("col") * col_blocks + jnp.arange(col_blocks, dtype=jnp.int32)
    listed = jnp.any(pattern[:, :, None] == block_ids[None, None, :], axis=1)
    allowed_cells = jnp.broadcast_to(
        listed[:, None, :, None], (row_blocks, 128, col_blocks, 128)
    ).reshape(row_count, group_cols)
    scores = jnp.where(allowed_cells, scores, floor_value)
    mass_ratio = group_cols * lax.axis_size("col") / (row_count * lax.axis_size("row"))
    log_target = -math.log(mass_ratio)
    col_pot = jnp.zeros((group_cols,), jnp.float32)
    row_pot = jnp.zeros((row_count,), jnp.float32)
    for sweep in range(ITERS):
        shifted = scores + col_pot[None, :]
        row_high = jnp.max(shifted, axis=1)
        row_sum = jnp.sum(jnp.exp(shifted - row_high[:, None]), axis=1)
        row_pot = -log_sum_over(row_high + jnp.log(row_sum), "col")
        shifted = scores + row_pot[:, None]
        col_high = jnp.max(shifted, axis=0)
        col_sum = jnp.sum(jnp.exp(shifted - col_high[None, :]), axis=0)
        col_pot = log_target - log_sum_over(col_high + jnp.log(col_sum), "row")
    weights = jnp.exp(scores + row_pot[:, None] + col_pot[None, :]).astype(jnp.bfloat16)
    centroid_sum = scatter_sum(
        lax.dot_general(
            weights, span_rows, (((0,), (0,)), ((), ())), preferred_element_type=jnp.float32
        ),
        "row",
    )
    return ((centroid_sum * mass_ratio).astype(jnp.bfloat16), row_pot, col_pot)


def solution(mesh):
    placed = (P(("row", "col"), None), P(("col", "row"), None), P("row", None))
    return jax.shard_map(
        per_device,
        mesh=mesh,
        in_specs=placed,
        out_specs=(P(("col", "row"), None), P("row"), P("col")),
        check_vma=False,
    )
```

```python
import math

import jax
import jax.numpy as jnp
from jax import lax
from jax.sharding import PartitionSpec as P

ITERS = 3


logit_scale = 0.0625
floor_value = -1e30


def bits_of(axis):
    return lax.axis_size(axis).bit_length() - 1


def swap(x, axis, k):
    return lax.ppermute(x, axis, [(i, i ^ k) for i in range(lax.axis_size(axis))])


def bulk_stages(axis):
    low = 1 if axis == "row" else 0
    out = []
    while low < bits_of(axis):
        width = min(2, bits_of(axis) - low)
        out.append([d << low for d in range(1 << width)])
        low += width
    return out + ([[0, 1]] if axis == "row" else [])


def gather_blocks(x, axis):
    held = {0: x}
    for steps in bulk_stages(axis):
        keys = list(held)
        block = jnp.concatenate([held[k] for k in keys]) if len(keys) > 1 else x
        for d in steps[1:]:
            got = swap(block, axis, d)
            for place, k in enumerate(keys):
                held[k ^ d] = got[place * x.shape[0] : (place + 1) * x.shape[0]]
    return jnp.concatenate([held[k] for k in range(lax.axis_size(axis))])


def scatter_sum(x, axis):
    n = lax.axis_size(axis)
    rows = x.shape[0] // n
    held = {k: x[k * rows : (k + 1) * rows] for k in range(n)}
    for steps in reversed(bulk_stages(axis)):
        keep = [k for k in held if not any(k & d for d in steps)]
        got = [
            swap(jnp.concatenate([held[k ^ d] for k in keep]).astype(jnp.bfloat16), axis, d)
            for d in steps[1:]
        ]
        new = {}
        for place, k in enumerate(keep):
            part = held[k]
            for g in got:
                part = part + g[place * rows : (place + 1) * rows].astype(jnp.float32)
            new[k] = part
        held = new
    return held[0]


def reorder(x, blocks, k):
    x = x.reshape(blocks, -1)
    return jnp.concatenate([x[p ^ k] for p in range(blocks)])


def log_sum_over(x, axis):
    n = lax.axis_size(axis)
    for bit in range(bits_of(axis)):
        got = reorder(swap(x, axis, 1 << bit), n, 1 << bit)
        high = jnp.maximum(x, got)
        x = high + jnp.log(jnp.exp(x - high) + jnp.exp(got - high))
    return x


def in_order(x, axis):
    n = lax.axis_size(axis)
    return x.reshape(n, -1)[lax.axis_index(axis) ^ jnp.arange(n)].reshape(-1)


def per_device(spans, centroids, pattern):
    rows, cols = lax.axis_size("row"), lax.axis_size("col")
    me_row, me_col = lax.axis_index("row"), lax.axis_index("col")
    all_centroids = gather_blocks(centroids, "row")
    span_rows = gather_blocks(spans, "col")
    row_count = span_rows.shape[0]
    group_cols = all_centroids.shape[0]
    scores = (
        lax.dot_general(
            span_rows, all_centroids, (((1,), (1,)), ((), ())), preferred_element_type=jnp.float32
        )
        * logit_scale
    )
    row_at = (me_col ^ jnp.arange(cols))[:, None] * spans.shape[0] + jnp.arange(spans.shape[0])
    col_at = (me_row ^ jnp.arange(rows))[:, None] * centroids.shape[0] + jnp.arange(centroids.shape[0])
    row_lists = pattern[row_at.reshape(-1) // 128]
    col_block = (me_col * group_cols + col_at.reshape(-1)) // 128
    allowed_cells = jnp.any(row_lists[:, :, None] == col_block[None, None, :], axis=1)
    scores = jnp.where(allowed_cells, scores, floor_value)
    mass_ratio = group_cols * cols / (row_count * rows)
    log_target = -math.log(mass_ratio)
    col_pot = jnp.zeros((group_cols,), jnp.float32)
    row_pot = jnp.zeros((row_count,), jnp.float32)
    for sweep in range(ITERS):
        shifted = scores + col_pot[None, :]
        row_high = jnp.max(shifted, axis=1)
        row_sum = jnp.sum(jnp.exp(shifted - row_high[:, None]), axis=1)
        row_pot = -log_sum_over(row_high + jnp.log(row_sum), "col")
        shifted = scores + row_pot[:, None]
        col_high = jnp.max(shifted, axis=0)
        col_sum = jnp.sum(jnp.exp(shifted - col_high[None, :]), axis=0)
        col_pot = log_target - log_sum_over(col_high + jnp.log(col_sum), "row")
    weights = jnp.exp(scores + row_pot[:, None] + col_pot[None, :]).astype(jnp.bfloat16)
    centroid_sum = scatter_sum(
        lax.dot_general(
            weights, span_rows, (((0,), (0,)), ((), ())), preferred_element_type=jnp.float32
        ),
        "row",
    )
    return (
        (centroid_sum * mass_ratio).astype(jnp.bfloat16),
        in_order(row_pot, "col"),
        in_order(col_pot, "row"),
    )


def solution(mesh):
    placed = (P(("row", "col"), None), P(("col", "row"), None), P("row", None))
    return jax.shard_map(
        per_device,
        mesh=mesh,
        in_specs=placed,
        out_specs=(P(("col", "row"), None), P("row"), P("col")),
        check_vma=False,
    )
```

```python
import math

import jax
import jax.numpy as jnp
from jax import lax
from jax.sharding import PartitionSpec as P

ITERS = 3


logit_scale = 0.0625
floor_value = -1e30


def swap(x, axis, k, one_core=False):
    if not one_core:
        return lax.ppermute(x, axis, [(i, i ^ k) for i in range(lax.axis_size(axis))])
    cols = lax.axis_size("col")
    k = k * cols if axis == "row" else k
    pairs = [(i, i ^ k) for i in range(lax.axis_size("row") * cols) if i // cols & 1]
    return lax.ppermute(x, ("row", "col"), pairs)


def stages(axis):
    low = 1 if axis == "row" else 0
    bits = (lax.axis_size(axis) - 1).bit_length()
    return [(at, 1 << min(2, bits - at)) for at in range(low, bits, 2)]


def digit(axis, at, size):
    return (lax.axis_index(axis) >> at) & (size - 1)


def place(parts, index):
    whole = jnp.zeros((len(parts),) + parts[0].shape, parts[0].dtype)
    for d, part in enumerate(parts):
        whole = lax.dynamic_update_index_in_dim(whole, part, index ^ d, 0)
    return whole.reshape((-1,) + parts[0].shape[1:])


def gather_blocks(x, axis):
    for at, size in stages(axis):
        parts = [x] + [swap(x, axis, d << at) for d in range(1, size)]
        x = place(parts, digit(axis, at, size))
    return x


def both_cores(x):
    return place([x, swap(x, "row", 1)], lax.axis_index("row") % 2)


def tree(op, parts):
    while len(parts) > 1:
        parts = [op(parts[i], parts[i + 1]) for i in range(0, len(parts), 2)]
    return parts[0]


def log_sum_over(x, axis):
    terms = []
    for at, size in stages(axis):
        parts = [x] + [swap(x, axis, d << at, one_core=True) for d in range(1, size)]
        high = tree(jnp.maximum, parts)
        x = high + jnp.log(tree(jnp.add, [jnp.exp(part - high) for part in parts]))
        terms.append(parts)
    return x, terms


def per_device(spans, centroids, pattern):
    rows, cols = lax.axis_size("row"), lax.axis_size("col")
    chips = rows // 2
    me_row, me_col = lax.axis_index("row"), lax.axis_index("col")
    core = me_row % 2
    per = centroids.shape[0]
    half_cols = per * chips
    group_cols = 2 * half_cols
    row_count = spans.shape[0] * cols

    chip_lists = both_cores(pattern)
    tile_centroids = both_cores(gather_blocks(centroids, "row"))
    tile_spans = both_cores(gather_blocks(spans, "col"))
    row_blocks = jnp.repeat(chip_lists, 128, axis=0)
    place_in_group = jnp.arange(group_cols)
    row_of = place_in_group % half_cols // per * 2 + place_in_group // half_cols
    col_block = (me_col * group_cols + row_of * per + place_in_group % per) // 128
    allowed_cells = jnp.any(row_blocks[:, :, None] == col_block[None, None, :], axis=1)
    scores = (
        lax.dot_general(
            tile_spans, tile_centroids, (((1,), (1,)), ((), ())), preferred_element_type=jnp.float32
        )
        * logit_scale
    )
    scores = jnp.where(allowed_cells, scores, floor_value)
    mass_ratio = group_cols * cols / (row_count * rows)
    log_target = -math.log(mass_ratio)
    col_pot = jnp.zeros((group_cols,), jnp.float32)
    for sweep in range(ITERS):
        shifted = scores + col_pot[None, :]
        row_high = jnp.max(shifted, axis=1)
        row_sum = jnp.sum(jnp.exp(shifted - row_high[:, None]), axis=1)
        row_log, unused = log_sum_over(row_high + jnp.log(row_sum), "col")
        row_pot = -row_log
        if sweep == ITERS - 1:
            row_pot = jnp.where(core == 1, row_pot, swap(row_pot, "row", 1))
        shifted = scores + row_pot[:, None]
        col_high = jnp.max(shifted, axis=0)
        weights = jnp.exp(shifted - col_high[None, :])
        col_sum = jnp.sum(weights, axis=0)
        col_log, terms = log_sum_over(col_high + jnp.log(col_sum), "row")
        col_pot = log_target - col_log

    own_weights = lax.dynamic_slice_in_dim(weights, core * half_cols, half_cols, 1)
    own_sum = lax.dynamic_slice_in_dim(col_sum, core * half_cols, half_cols, 0)
    averages = (
        lax.dot_general(
            own_weights.astype(jnp.bfloat16),
            tile_spans,
            (((0,), (0,)), ((), ())),
            preferred_element_type=jnp.float32,
        )
        / own_sum[:, None]
    )
    flat = [part for parts in terms for part in parts]
    got = swap(jnp.concatenate([col_pot] + [part[:half_cols] for part in flat]), "row", 1)
    mine = jnp.concatenate([col_pot] + [part[half_cols:] for part in flat])
    both = jnp.where(core == 1, mine, got)
    col_pot = both[:group_cols]
    logs = both[group_cols:].reshape(-1, half_cols)

    held = averages.reshape((chips, per) + averages.shape[1:])
    first = 0
    for number, (at, size) in enumerate(stages("row")):
        me = digit("row", at, size)
        held = held.reshape((-1, size) + held.shape[1:])
        own = lax.dynamic_index_in_dim(held, me, 1, keepdims=False)
        low = held.astype(jnp.bfloat16)
        parts = [own] + [
            swap(lax.dynamic_index_in_dim(low, me ^ d, 1, keepdims=False), "row", d << at).astype(jnp.float32)
            for d in range(1, size)
        ]
        share = logs[first : first + size].reshape(size, chips, per)
        for done_at, done_size in stages("row")[: number + 1]:
            share = share.reshape(size, -1, done_size, per)
            share = lax.dynamic_index_in_dim(share, digit("row", done_at, done_size), 2, keepdims=False)
        share = jnp.exp(share - jnp.max(share, axis=0))
        share = share / jnp.sum(share, axis=0)
        held = tree(jnp.add, [share[d][:, :, None] * parts[d] for d in range(size)])
        first += size
    centroid_sum = held.reshape(per, -1) * math.exp(log_target)
    return (
        (centroid_sum * mass_ratio).astype(jnp.bfloat16),
        lax.dynamic_slice_in_dim(row_pot, core * row_count, row_count, 0),
        col_pot.reshape(2, chips, per).swapaxes(0, 1).reshape(-1),
    )


def solution(mesh):
    placed = (P(("row", "col"), None), P(("col", "row"), None), P("row", None))
    return jax.shard_map(
        per_device,
        mesh=mesh,
        in_specs=placed,
        out_specs=(P(("col", "row"), None), P("row"), P("col")),
        check_vma=False,
    )
```

```python
import math

import jax
import jax.numpy as jnp
from jax import lax
from jax.sharding import PartitionSpec as P

ITERS = 3


logit_scale = 0.0625
floor_value = -1e30


def swap(x, axis, k, one_core=False):
    if not one_core:
        return lax.ppermute(x, axis, [(i, i ^ k) for i in range(lax.axis_size(axis))])
    cols = lax.axis_size("col")
    k = k * cols if axis == "row" else k
    pairs = [(i, i ^ k if i // cols & 1 else i) for i in range(lax.axis_size("row") * cols)]
    return lax.ppermute(x, ("row", "col"), pairs)


def stages(axis):
    low = 1 if axis == "row" else 0
    bits = (lax.axis_size(axis) - 1).bit_length()
    return [(at, 1 << min(2, bits - at)) for at in range(low, bits, 2)]


def digit(axis, at, size):
    return (lax.axis_index(axis) >> at) & (size - 1)


def place(parts, index):
    whole = jnp.zeros((len(parts),) + parts[0].shape, parts[0].dtype)
    for d, part in enumerate(parts):
        whole = lax.dynamic_update_index_in_dim(whole, part, index ^ d, 0)
    return whole.reshape((-1,) + parts[0].shape[1:])


def gather_blocks(x, axis):
    for at, size in stages(axis):
        parts = [x] + [swap(x, axis, d << at) for d in range(1, size)]
        x = place(parts, digit(axis, at, size))
    return x


def both_cores(x):
    return place([x, swap(x, "row", 1)], lax.axis_index("row") % 2)


def tree(op, parts):
    while len(parts) > 1:
        parts = [op(parts[i], parts[i + 1]) for i in range(0, len(parts), 2)]
    return parts[0]


def log_sum_over(x, axis):
    terms = []
    for at, size in stages(axis):
        parts = [x] + [swap(x, axis, d << at, one_core=True) for d in range(1, size)]
        high = tree(jnp.maximum, parts)
        x = high + jnp.log(tree(jnp.add, [jnp.exp(part - high) for part in parts]))
        terms.append(parts)
    return x, terms


def per_device(spans, centroids, pattern):
    rows, cols = lax.axis_size("row"), lax.axis_size("col")
    chips = rows // 2
    me_row, me_col = lax.axis_index("row"), lax.axis_index("col")
    core = me_row % 2
    per = centroids.shape[0]
    half_cols = per * chips
    group_cols = 2 * half_cols
    row_count = spans.shape[0] * cols

    chip_lists = both_cores(pattern)
    tile_centroids = both_cores(gather_blocks(centroids, "row"))
    tile_spans = both_cores(gather_blocks(spans, "col"))
    row_blocks = jnp.repeat(chip_lists, 128, axis=0)
    place_in_group = jnp.arange(group_cols)
    row_of = place_in_group % half_cols // per * 2 + place_in_group // half_cols
    col_block = (me_col * group_cols + row_of * per + place_in_group % per) // 128
    allowed_cells = jnp.any(row_blocks[:, :, None] == col_block[None, None, :], axis=1)
    scores = (
        lax.dot_general(
            tile_spans, tile_centroids, (((1,), (1,)), ((), ())), preferred_element_type=jnp.float32
        )
        * logit_scale
    )
    scores = jnp.where(allowed_cells, scores, floor_value)
    mass_ratio = group_cols * cols / (row_count * rows)
    log_target = -math.log(mass_ratio)
    col_pot = jnp.zeros((group_cols,), jnp.float32)
    for sweep in range(ITERS):
        shifted = scores + col_pot[None, :]
        row_high = jnp.max(shifted, axis=1)
        row_sum = jnp.sum(jnp.exp(shifted - row_high[:, None]), axis=1)
        row_log, unused = log_sum_over(row_high + jnp.log(row_sum), "col")
        row_pot = -row_log
        if sweep == ITERS - 1:
            row_pot = jnp.where(core == 1, row_pot, swap(row_pot, "row", 1))
        shifted = scores + row_pot[:, None]
        col_high = jnp.max(shifted, axis=0)
        weights = jnp.exp(shifted - col_high[None, :])
        col_sum = jnp.sum(weights, axis=0)
        col_log, terms = log_sum_over(col_high + jnp.log(col_sum), "row")
        col_pot = log_target - col_log

    own_weights = lax.dynamic_slice_in_dim(weights, core * half_cols, half_cols, 1)
    own_sum = lax.dynamic_slice_in_dim(col_sum, core * half_cols, half_cols, 0)
    averages = (
        lax.dot_general(
            own_weights.astype(jnp.bfloat16),
            tile_spans,
            (((0,), (0,)), ((), ())),
            preferred_element_type=jnp.float32,
        )
        / own_sum[:, None]
    )
    flat = [part for parts in terms for part in parts]
    got = swap(jnp.concatenate([col_pot] + [part[:half_cols] for part in flat]), "row", 1)
    mine = jnp.concatenate([col_pot] + [part[half_cols:] for part in flat])
    both = jnp.where(core == 1, mine, got)
    col_pot = both[:group_cols]
    logs = both[group_cols:].reshape(-1, half_cols)

    held = averages.reshape((chips, per) + averages.shape[1:])
    first = 0
    for number, (at, size) in enumerate(stages("row")):
        me = digit("row", at, size)
        held = held.reshape((-1, size) + held.shape[1:])
        own = lax.dynamic_index_in_dim(held, me, 1, keepdims=False)
        low = held.astype(jnp.bfloat16)
        parts = [own] + [
            swap(lax.dynamic_index_in_dim(low, me ^ d, 1, keepdims=False), "row", d << at).astype(jnp.float32)
            for d in range(1, size)
        ]
        share = logs[first : first + size].reshape(size, chips, per)
        for done_at, done_size in stages("row")[: number + 1]:
            share = share.reshape(size, -1, done_size, per)
            share = lax.dynamic_index_in_dim(share, digit("row", done_at, done_size), 2, keepdims=False)
        share = jnp.exp(share - jnp.max(share, axis=0))
        share = share / jnp.sum(share, axis=0)
        held = tree(jnp.add, [share[d][:, :, None] * parts[d] for d in range(size)])
        first += size
    centroid_sum = held.reshape(per, -1) * math.exp(log_target)
    return (
        (centroid_sum * mass_ratio).astype(jnp.bfloat16),
        lax.dynamic_slice_in_dim(row_pot, core * row_count, row_count, 0),
        col_pot.reshape(2, chips, per).swapaxes(0, 1).reshape(-1),
    )


def solution(mesh):
    placed = (P(("row", "col"), None), P(("col", "row"), None), P("row", None))
    return jax.shard_map(
        per_device,
        mesh=mesh,
        in_specs=placed,
        out_specs=(P(("col", "row"), None), P("row"), P("col")),
        check_vma=False,
    )
```

```python
import math

import jax
import jax.numpy as jnp
from jax import lax
from jax.sharding import PartitionSpec as P

ITERS = 3


logit_scale = 0.0625
floor_value = -1e30


def swap(x, axis, k):
    return lax.ppermute(x, axis, [(i, i ^ k) for i in range(lax.axis_size(axis))])


def stages(axis):
    low = 1 if axis == "row" else 0
    bits = (lax.axis_size(axis) - 1).bit_length()
    return [(at, 1 << min(2, bits - at)) for at in range(low, bits, 2)]


def digit(axis, at, size):
    return (lax.axis_index(axis) >> at) & (size - 1)


def place(parts, index):
    whole = jnp.zeros((len(parts),) + parts[0].shape, parts[0].dtype)
    for d, part in enumerate(parts):
        whole = lax.dynamic_update_index_in_dim(whole, part, index ^ d, 0)
    return whole.reshape((-1,) + parts[0].shape[1:])


def gather_blocks(x, axis):
    for at, size in stages(axis):
        parts = [x] + [swap(x, axis, d << at) for d in range(1, size)]
        x = place(parts, digit(axis, at, size))
    return x


def both_cores(x):
    return place([x, swap(x, "row", 1)], lax.axis_index("row") % 2)


def tree(op, parts):
    while len(parts) > 1:
        parts = [op(parts[i], parts[i + 1]) for i in range(0, len(parts), 2)]
    return parts[0]


def log_sum_over(x, axis):
    terms = []
    for at, size in stages(axis):
        parts = [x] + [swap(x, axis, d << at) for d in range(1, size)]
        high = tree(jnp.maximum, parts)
        x = high + jnp.log(tree(jnp.add, [jnp.exp(part - high) for part in parts]))
        terms.append(parts)
    return x, terms


def per_device(spans, centroids, pattern):
    rows, cols = lax.axis_size("row"), lax.axis_size("col")
    chips = rows // 2
    me_row, me_col = lax.axis_index("row"), lax.axis_index("col")
    core = me_row % 2
    per = centroids.shape[0]
    half_cols = per * chips
    group_cols = 2 * half_cols
    row_count = spans.shape[0] * cols

    chip_lists = both_cores(pattern)
    tile_centroids = both_cores(gather_blocks(centroids, "row"))
    tile_spans = both_cores(gather_blocks(spans, "col"))
    row_blocks = jnp.repeat(chip_lists, 128, axis=0)
    place_in_group = jnp.arange(group_cols)
    row_of = place_in_group % half_cols // per * 2 + place_in_group // half_cols
    col_block = (me_col * group_cols + row_of * per + place_in_group % per) // 128
    allowed_cells = jnp.any(row_blocks[:, :, None] == col_block[None, None, :], axis=1)
    scores = (
        lax.dot_general(
            tile_spans, tile_centroids, (((1,), (1,)), ((), ())), preferred_element_type=jnp.float32
        )
        * logit_scale
    )
    scores = jnp.where(allowed_cells, scores, floor_value)
    mass_ratio = group_cols * cols / (row_count * rows)
    log_target = -math.log(mass_ratio)

    def row_pass(col_pot):
        shifted = scores + col_pot[None, :]
        row_high = jnp.max(shifted, axis=1)
        row_sum = jnp.sum(jnp.exp(shifted - row_high[:, None]), axis=1)
        return -log_sum_over(row_high + jnp.log(row_sum), "col")[0]

    def col_pass(row_pot):
        shifted = scores + row_pot[:, None]
        col_high = jnp.max(shifted, axis=0)
        weights = jnp.exp(shifted - col_high[None, :])
        col_sum = jnp.sum(weights, axis=0)
        return weights, col_sum, col_high + jnp.log(col_sum)

    def rounds():
        col_pot = jnp.zeros((group_cols,), jnp.float32)
        for sweep in range(ITERS):
            row_pot = row_pass(col_pot)
            if sweep < ITERS - 1:
                col_pot = log_target - log_sum_over(col_pass(row_pot)[2], "row")[0]
        return row_pot

    def last_logs():
        col_log, terms = log_sum_over(part_log, "row")
        return log_target - col_log, [part for parts in terms for part in parts]

    row_pot = lax.cond(core == 1, rounds, lambda: jnp.zeros((2 * row_count,), jnp.float32))
    row_pot = jnp.where(core == 1, row_pot, swap(row_pot, "row", 1))
    weights, col_sum, part_log = col_pass(row_pot)
    col_pot, flat = lax.cond(
        core == 1,
        last_logs,
        lambda: (part_log, [part_log for at, size in stages("row") for d in range(size)]),
    )
    own_weights = lax.dynamic_slice_in_dim(weights, core * half_cols, half_cols, 1)
    own_sum = lax.dynamic_slice_in_dim(col_sum, core * half_cols, half_cols, 0)
    averages = (
        lax.dot_general(
            own_weights.astype(jnp.bfloat16),
            tile_spans,
            (((0,), (0,)), ((), ())),
            preferred_element_type=jnp.float32,
        )
        / own_sum[:, None]
    )
    got = swap(jnp.concatenate([col_pot] + [part[:half_cols] for part in flat]), "row", 1)
    mine = jnp.concatenate([col_pot] + [part[half_cols:] for part in flat])
    both = jnp.where(core == 1, mine, got)
    col_pot = both[:group_cols]
    logs = both[group_cols:].reshape(-1, half_cols)

    held = averages.reshape((chips, per) + averages.shape[1:])
    first = 0
    for number, (at, size) in enumerate(stages("row")):
        me = digit("row", at, size)
        held = held.reshape((-1, size) + held.shape[1:])
        own = lax.dynamic_index_in_dim(held, me, 1, keepdims=False)
        low = held.astype(jnp.bfloat16)
        parts = [own] + [
            swap(lax.dynamic_index_in_dim(low, me ^ d, 1, keepdims=False), "row", d << at).astype(jnp.float32)
            for d in range(1, size)
        ]
        share = logs[first : first + size].reshape(size, chips, per)
        for done_at, done_size in stages("row")[: number + 1]:
            share = share.reshape(size, -1, done_size, per)
            share = lax.dynamic_index_in_dim(share, digit("row", done_at, done_size), 2, keepdims=False)
        share = jnp.exp(share - jnp.max(share, axis=0))
        share = share / jnp.sum(share, axis=0)
        held = tree(jnp.add, [share[d][:, :, None] * parts[d] for d in range(size)])
        first += size
    centroid_sum = held.reshape(per, -1) * math.exp(log_target)
    return (
        (centroid_sum * mass_ratio).astype(jnp.bfloat16),
        lax.dynamic_slice_in_dim(row_pot, core * row_count, row_count, 0),
        col_pot.reshape(2, chips, per).swapaxes(0, 1).reshape(-1),
    )


def solution(mesh):
    placed = (P(("row", "col"), None), P(("col", "row"), None), P("row", None))
    return jax.shard_map(
        per_device,
        mesh=mesh,
        in_specs=placed,
        out_specs=(P(("col", "row"), None), P("row"), P("col")),
        check_vma=False,
    )
```

```python
import math

import jax
import jax.numpy as jnp
from jax import lax
from jax.sharding import PartitionSpec as P

ITERS = 3


logit_scale = 0.0625
floor_value = -1e30


def swap(x, axis, k):
    return lax.ppermute(x, axis, [(i, i ^ k) for i in range(lax.axis_size(axis))])


def stages(axis):
    low = 1 if axis == "row" else 0
    bits = (lax.axis_size(axis) - 1).bit_length()
    return [(at, 1 << min(2, bits - at)) for at in range(low, bits, 2)]


def digit(axis, at, size):
    return (lax.axis_index(axis) >> at) & (size - 1)


def gather_placed(x, axis):
    for at, size in stages(axis):
        parts = [x] + [swap(x, axis, d << at) for d in range(1, size)]
        whole = jnp.zeros((size,) + x.shape, x.dtype)
        for d, part in enumerate(parts):
            whole = lax.dynamic_update_index_in_dim(whole, part, digit(axis, at, size) ^ d, 0)
        x = whole.reshape((-1,) + x.shape[1:])
    return x


def gather_xor(x, axis):
    for at, size in stages(axis):
        x = jnp.concatenate([x] + [swap(x, axis, d << at) for d in range(1, size)])
    return x


def both_cores(x):
    return jnp.concatenate([x, swap(x, "row", 1)])


def reorder(x, blocks, k):
    x = x.reshape((blocks, -1) + x.shape[1:])
    return jnp.concatenate([x[p ^ k] for p in range(blocks)])


def unxor(x, index, blocks):
    shape = x.shape
    bit = 1
    while bit < blocks:
        pairs = x.reshape((blocks // (2 * bit), 2, -1) + shape[1:])
        x = jnp.where((index & bit) != 0, pairs[:, ::-1], pairs).reshape(shape)
        bit *= 2
    return x


def tree(op, parts):
    while len(parts) > 1:
        parts = [op(parts[i], parts[i + 1]) for i in range(0, len(parts), 2)]
    return parts[0]


def log_sum(parts):
    high = tree(jnp.maximum, parts)
    return high + jnp.log(tree(jnp.add, [jnp.exp(part - high) for part in parts]))


def log_sum_rows(x):
    for at, size in stages("row"):
        x = log_sum([x] + [swap(x, "row", d << at) for d in range(1, size)])
    return x


def log_sum_cols(x):
    cols = lax.axis_size("col")
    for at, size in stages("col"):
        parts = [x]
        for d in range(1, size):
            halves = swap(x, "col", d << at).reshape(2, -1)
            parts.append(jnp.concatenate([reorder(half, cols, d << at) for half in halves]))
        x = log_sum(parts)
    return x


def in_thirds(x, width):
    thirds = []
    for step in range(3):
        top = lax.reduce_precision(x, 8, 7)
        thirds.append(top.astype(jnp.bfloat16))
        x = x - top
    flat = jnp.concatenate(thirds)
    rows = -(-flat.shape[0] // (16 * width)) * 16
    return jnp.pad(flat, (0, rows * width - flat.shape[0])).reshape(rows, width)


def from_thirds(rows, count):
    thirds = rows.reshape(-1)[: 3 * count].astype(jnp.float32).reshape(3, count)
    return thirds[0] + thirds[1] + thirds[2]


def per_device(spans, centroids, pattern):
    rows, cols = lax.axis_size("row"), lax.axis_size("col")
    chips = rows // 2
    me_row, me_col = lax.axis_index("row"), lax.axis_index("col")
    core = me_row % 2
    per, width = centroids.shape
    half_cols = per * chips
    group_cols = 2 * half_cols
    row_count = spans.shape[0] * cols

    tile_spans = both_cores(gather_xor(spans, "col"))
    tile_centroids = both_cores(gather_placed(centroids, "row"))
    lists = both_cores(pattern)
    row_blocks = jnp.concatenate(
        [unxor(half, me_col, cols) for half in jnp.repeat(lists, 128, axis=0).reshape(2, row_count, -1)]
    )
    at = jnp.arange(group_cols)
    row_of = at % half_cols // per * 2 + (at // half_cols ^ core)
    col_block = (me_col * group_cols + row_of * per + at % per) // 128
    allowed_cells = jnp.any(row_blocks[:, :, None] == col_block[None, None, :], axis=1)
    scores = (
        lax.dot_general(
            tile_spans, tile_centroids, (((1,), (1,)), ((), ())), preferred_element_type=jnp.float32
        )
        * logit_scale
    )
    scores = jnp.where(allowed_cells, scores, floor_value)
    mass_ratio = group_cols * cols / (row_count * rows)
    log_target = -math.log(mass_ratio)

    def row_pass(col_pot):
        shifted = scores + col_pot[None, :]
        row_high = jnp.max(shifted, axis=1)
        row_sum = jnp.sum(jnp.exp(shifted - row_high[:, None]), axis=1)
        return -log_sum_cols(row_high + jnp.log(row_sum))

    def col_pass(scores, row_pot):
        shifted = scores + row_pot[:, None]
        col_high = jnp.max(shifted, axis=0)
        weights = jnp.exp(shifted - col_high[None, :])
        col_sum = jnp.sum(weights, axis=0)
        return weights, col_sum, col_high + jnp.log(col_sum)

    def rounds():
        col_pot = jnp.zeros((group_cols,), jnp.float32)
        for sweep in range(ITERS):
            row_pot = row_pass(col_pot)
            if sweep < ITERS - 1:
                col_pot = log_target - log_sum_rows(col_pass(scores, row_pot)[2])
        return row_pot

    row_pot = lax.cond(core == 1, rounds, lambda: jnp.zeros((2 * row_count,), jnp.float32))
    row_pot = jnp.where(core == 1, row_pot, reorder(swap(row_pot, "row", 1), 2, 1))

    weights, col_sum, part_log = col_pass(scores[:, :half_cols], row_pot)
    held = (
        lax.dot_general(
            weights.astype(jnp.bfloat16),
            tile_spans,
            (((0,), (0,)), ((), ())),
            preferred_element_type=jnp.float32,
        )
        / col_sum[:, None]
    ).reshape(chips, per, width)
    for at, size in stages("row"):
        me = digit("row", at, size)
        held = held.reshape((-1, size) + held.shape[1:])
        low = held.astype(jnp.bfloat16)
        extra = in_thirds(part_log, width)
        parts, logs = [lax.dynamic_index_in_dim(held, me, 1, keepdims=False)], [from_thirds(extra, half_cols)]
        for d in range(1, size):
            block = lax.dynamic_index_in_dim(low, me ^ d, 1, keepdims=False).reshape(-1, width)
            got = swap(jnp.concatenate([block, extra]), "row", d << at)
            parts.append(got[: block.shape[0]].astype(jnp.float32).reshape(parts[0].shape))
            logs.append(from_thirds(got[block.shape[0] :], half_cols))
        part_log = log_sum(logs)
        shares = []
        for log in logs:
            share = jnp.exp(log - part_log).reshape(chips, per)
            for done_at, done_size in stages("row"):
                if done_at <= at:
                    share = share.reshape(-1, done_size, per)
                    share = lax.dynamic_index_in_dim(share, digit("row", done_at, done_size), 1, keepdims=False)
            shares.append(share[:, :, None])
        held = tree(jnp.add, [share * part for share, part in zip(shares, parts)])
    col_pot = log_target - part_log
    col_pots = jnp.stack([col_pot, swap(col_pot, "row", 1)]).reshape(2, chips, per)
    col_pots = jnp.where(core == 1, col_pots[::-1], col_pots)
    return (
        (held.reshape(per, width) * (math.exp(log_target) * mass_ratio)).astype(jnp.bfloat16),
        unxor(row_pot[:row_count], me_col, cols),
        col_pots.swapaxes(0, 1).reshape(-1),
    )


def solution(mesh):
    placed = (P(("row", "col"), None), P(("col", "row"), None), P("row", None))
    return jax.shard_map(
        per_device,
        mesh=mesh,
        in_specs=placed,
        out_specs=(P(("col", "row"), None), P("row"), P("col")),
        check_vma=False,
    )
```

```python
import math

import jax
import jax.numpy as jnp
from jax import lax
from jax.sharding import PartitionSpec as P

ITERS = 3


logit_scale = 0.0625
floor_value = -1e30


def swap(x, axis, k):
    return lax.ppermute(x, axis, [(i, i ^ k) for i in range(lax.axis_size(axis))])


def stages(axis):
    low = 1 if axis == "row" else 0
    bits = (lax.axis_size(axis) - 1).bit_length()
    return [(at, 1 << min(2, bits - at)) for at in range(low, bits, 2)]


def digit(axis, at, size):
    return (lax.axis_index(axis) >> at) & (size - 1)


def after(x, other):
    return lax.optimization_barrier((x, other))[0]


def gather_tile(spans, centroids, pattern):
    span_parts, centroid_parts = [spans], [centroids]
    for d in range(1, stages("col")[0][1]):
        span_parts.append(swap(spans, "col", d))
    late = span_parts[1]
    for d in range(1, stages("row")[0][1]):
        block = after(centroids, late) if d == 1 else centroids
        centroid_parts.append(swap(block, "row", d << 1))
    for at, size in stages("col")[1:]:
        whole = jnp.concatenate(span_parts)
        span_parts = [whole] + [swap(whole, "col", d << at) for d in range(1, size)]
    for at, size in stages("row"):
        if at > 1:
            centroid_parts = [whole] + [swap(whole, "row", d << at) for d in range(1, size)]
        whole = jnp.zeros((size,) + centroid_parts[0].shape, centroids.dtype)
        for d, part in enumerate(centroid_parts):
            whole = lax.dynamic_update_index_in_dim(whole, part, digit("row", at, size) ^ d, 0)
        whole = whole.reshape((-1,) + centroids.shape[1:])
    return jnp.concatenate(span_parts), whole, after(pattern, late)


def both_cores(x):
    return jnp.concatenate([x, swap(x, "row", 1)])


def reorder(x, blocks, k):
    x = x.reshape((blocks, -1) + x.shape[1:])
    return jnp.concatenate([x[p ^ k] for p in range(blocks)])


def unxor(x, index, blocks):
    shape = x.shape
    bit = 1
    while bit < blocks:
        pairs = x.reshape((blocks // (2 * bit), 2, -1) + shape[1:])
        x = jnp.where((index & bit) != 0, pairs[:, ::-1], pairs).reshape(shape)
        bit *= 2
    return x


def tree(op, parts):
    while len(parts) > 1:
        parts = [op(parts[i], parts[i + 1]) for i in range(0, len(parts), 2)]
    return parts[0]


def log_sum(parts):
    high = tree(jnp.maximum, parts)
    return high + jnp.log(tree(jnp.add, [jnp.exp(part - high) for part in parts]))


def log_sum_rows(x):
    for at, size in stages("row"):
        x = log_sum([x] + [swap(x, "row", d << at) for d in range(1, size)])
    return x


def log_sum_cols(x):
    cols = lax.axis_size("col")
    for at, size in stages("col"):
        parts = [x]
        for d in range(1, size):
            halves = swap(x, "col", d << at).reshape(2, -1)
            parts.append(jnp.concatenate([reorder(half, cols, d << at) for half in halves]))
        x = log_sum(parts)
    return x


def per_device(spans, centroids, pattern):
    rows, cols = lax.axis_size("row"), lax.axis_size("col")
    chips = rows // 2
    me_row, me_col = lax.axis_index("row"), lax.axis_index("col")
    core = me_row % 2
    per, width = centroids.shape
    half_cols = per * chips
    group_cols = 2 * half_cols
    row_count = spans.shape[0] * cols

    own_spans, own_centroids, late_pattern = gather_tile(spans, centroids, pattern)
    tile_spans = both_cores(own_spans)
    tile_centroids = both_cores(own_centroids)
    lists = jnp.concatenate([pattern, swap(late_pattern, "row", 1)])
    row_blocks = jnp.concatenate(
        [unxor(half, me_col, cols) for half in jnp.repeat(lists, 128, axis=0).reshape(2, row_count, -1)]
    )
    at = jnp.arange(group_cols)
    row_of = at % half_cols // per * 2 + (at // half_cols ^ core)
    col_block = (me_col * group_cols + row_of * per + at % per) // 128
    allowed_cells = jnp.any(row_blocks[:, :, None] == col_block[None, None, :], axis=1)
    scores = (
        lax.dot_general(
            tile_spans, tile_centroids, (((1,), (1,)), ((), ())), preferred_element_type=jnp.float32
        )
        * logit_scale
    )
    scores = jnp.where(allowed_cells, scores, floor_value)
    mass_ratio = group_cols * cols / (row_count * rows)
    log_target = -math.log(mass_ratio)

    def row_pass(col_pot):
        shifted = scores + col_pot[None, :]
        row_high = jnp.max(shifted, axis=1)
        row_sum = jnp.sum(jnp.exp(shifted - row_high[:, None]), axis=1)
        return -log_sum_cols(row_high + jnp.log(row_sum))

    def col_pass(scores, row_pot):
        shifted = scores + row_pot[:, None]
        col_high = jnp.max(shifted, axis=0)
        weights = jnp.exp(shifted - col_high[None, :])
        col_sum = jnp.sum(weights, axis=0)
        return weights, col_sum, col_high + jnp.log(col_sum)

    def rounds():
        col_pot = jnp.zeros((group_cols,), jnp.float32)
        for sweep in range(ITERS):
            row_pot = row_pass(col_pot)
            if sweep < ITERS - 1:
                col_pot = log_target - log_sum_rows(col_pass(scores, row_pot)[2])
        return row_pot

    row_pot = lax.cond(core == 1, rounds, lambda: jnp.zeros((2 * row_count,), jnp.float32))
    row_pot = jnp.where(core == 1, row_pot, reorder(swap(row_pot, "row", 1), 2, 1))

    weights, col_sum, part_log = col_pass(scores[:, :half_cols], row_pot)
    held = (
        lax.dot_general(
            weights.astype(jnp.bfloat16),
            tile_spans,
            (((0,), (0,)), ((), ())),
            preferred_element_type=jnp.float32,
        )
        / col_sum[:, None]
    ).reshape(chips, per, width)
    for at, size in stages("row"):
        me = digit("row", at, size)
        held = held.reshape((-1, size) + held.shape[1:])
        low = held.astype(jnp.bfloat16)
        blocks = [low] + [lax.dynamic_index_in_dim(low, me ^ d, 1, keepdims=False) for d in range(1, size)]
        parts = [lax.dynamic_index_in_dim(held, me, 1, keepdims=False)]
        parts += [swap(block, "row", d << at) for d, block in enumerate(blocks) if d]
        logs = after(part_log[None], blocks)
        for step in range(size.bit_length() - 1):
            logs = jnp.concatenate([logs, swap(logs, "row", 1 << at + step)])
        part_log = log_sum(list(logs))
        shares = []
        for log in logs:
            share = jnp.exp(log - part_log).reshape(chips, per)
            for done_at, done_size in stages("row"):
                if done_at <= at:
                    share = share.reshape(-1, done_size, per)
                    share = lax.dynamic_index_in_dim(share, digit("row", done_at, done_size), 1, keepdims=False)
            shares.append(share[:, :, None])
        held = tree(jnp.add, [share * part.astype(jnp.float32) for share, part in zip(shares, parts)])
    col_pot = log_target - part_log
    col_pots = jnp.stack([col_pot, swap(col_pot, "row", 1)]).reshape(2, chips, per)
    col_pots = jnp.where(core == 1, col_pots[::-1], col_pots)
    return (
        (held.reshape(per, width) * (math.exp(log_target) * mass_ratio)).astype(jnp.bfloat16),
        unxor(row_pot[:row_count], me_col, cols),
        col_pots.swapaxes(0, 1).reshape(-1),
    )


def solution(mesh):
    placed = (P(("row", "col"), None), P(("col", "row"), None), P("row", None))
    return jax.shard_map(
        per_device,
        mesh=mesh,
        in_specs=placed,
        out_specs=(P(("col", "row"), None), P("row"), P("col")),
        check_vma=False,
    )
```

```python
import math

import jax
import jax.numpy as jnp
from jax import lax
from jax.sharding import PartitionSpec as P

ITERS = 3


logit_scale = 0.0625
floor_value = -1e30


def swap(x, axis, k):
    return lax.ppermute(x, axis, [(i, i ^ k) for i in range(lax.axis_size(axis))])


def swap_by_core(x, axis, for_core):
    cols = lax.axis_size("col")
    scale = cols if axis == "row" else 1
    pairs = [(i, i ^ (for_core[i // cols & 1] * scale)) for i in range(lax.axis_size("row") * cols)]
    return lax.ppermute(x, ("row", "col"), pairs)


def stages(axis):
    low = 1 if axis == "row" else 0
    bits = (lax.axis_size(axis) - 1).bit_length()
    return [(at, 1 << min(2, bits - at)) for at in range(low, bits, 2)]


def digit(axis, at, size):
    return (lax.axis_index(axis) >> at) & (size - 1)


def gather_spans(x, core):
    first = None
    for at, size in stages("col"):
        parts = [x] + [swap(x, "col", d << at) for d in range(1, min(size, 3))]
        first = parts[1] if first is None else first
        if size == 4:
            passed_on = jnp.where(core == 1, parts[2], parts[1])
            parts.append(swap_by_core(passed_on, "col", (2 << at, 1 << at)))
        x = jnp.concatenate(parts)
    return x, first


def after(x, other):
    return lax.optimization_barrier((x, other))[0]


def gather_centroids(x, first):
    for at, size in stages("row"):
        parts = [x] + [swap(after(x, first) if d << at == 2 else x, "row", d << at) for d in range(1, size)]
        whole = jnp.zeros((size,) + x.shape, x.dtype)
        for d, part in enumerate(parts):
            whole = lax.dynamic_update_index_in_dim(whole, part, digit("row", at, size) ^ d, 0)
        x = whole.reshape((-1,) + x.shape[1:])
    return x


def reorder(x, blocks, k):
    x = x.reshape((blocks, -1) + x.shape[1:])
    return jnp.concatenate([x[p ^ k] for p in range(blocks)])


def unxor(x, index, blocks):
    shape = x.shape
    bit = 1
    while bit < blocks:
        pairs = x.reshape((blocks // (2 * bit), 2, -1) + shape[1:])
        x = jnp.where((index & bit) != 0, pairs[:, ::-1], pairs).reshape(shape)
        bit *= 2
    return x


def tree(op, parts):
    while len(parts) > 1:
        parts = [op(parts[i], parts[i + 1]) for i in range(0, len(parts), 2)]
    return parts[0]


def add(parts):
    return tree(jnp.add, parts)


def log_sum(parts):
    high = tree(jnp.maximum, parts)
    return high + jnp.log(add([jnp.exp(part - high) for part in parts]))


def over_rows(merge, x):
    for at, size in stages("row"):
        x = merge([x] + [swap(x, "row", d << at) for d in range(1, size)])
    return x


def over_cols(merge, x):
    cols = lax.axis_size("col")
    for at, size in stages("col"):
        parts = [x]
        for d in range(1, size):
            halves = swap(x, "col", d << at).reshape(2, -1)
            parts.append(jnp.concatenate([reorder(half, cols, d << at) for half in halves]))
        x = merge(parts)
    return x


def per_device(spans, centroids, pattern):
    rows, cols = lax.axis_size("row"), lax.axis_size("col")
    chips = rows // 2
    me_row, me_col = lax.axis_index("row"), lax.axis_index("col")
    core = me_row % 2
    per, width = centroids.shape
    half_cols = per * chips
    group_cols = 2 * half_cols
    row_count = spans.shape[0] * cols
    mass_ratio = group_cols * cols / (row_count * rows)
    target = 1 / mass_ratio

    own_spans, first = gather_spans(spans, core)
    own_centroids = gather_centroids(centroids, first)
    span_halves = [own_spans, swap(own_spans, "row", 1)]
    tile_centroids = jnp.concatenate([own_centroids, swap(own_centroids, "row", 1)])
    lists = [pattern, swap(after(pattern, first), "row", 1)]
    at = jnp.arange(group_cols)
    row_of = at % half_cols // per * 2 + (at // half_cols ^ core)
    col_block = (me_col * group_cols + row_of * per + at % per) // 128

    def half_scores(half):
        row_lists = unxor(jnp.repeat(lists[half], 128, axis=0), me_col, cols)
        allowed_cells = jnp.any(row_lists[:, :, None] == col_block[None, None, :], axis=1)
        products = lax.dot_general(
            span_halves[half], tile_centroids, (((1,), (1,)), ((), ())), preferred_element_type=jnp.float32
        )
        return jnp.where(allowed_cells, products * logit_scale, floor_value)

    scores = [half_scores(0), half_scores(1)]

    def both(per_half):
        return jnp.concatenate([per_half(0), per_half(1)])

    def halves_of(x):
        return [x[:row_count, None], x[row_count:, None]]

    def rounds():
        def row_logs(half):
            high = jnp.max(scores[half], axis=1)
            return high + jnp.log(jnp.sum(jnp.exp(scores[half] - high[:, None]), axis=1))

        first_row_pot = -over_cols(log_sum, both(row_logs))
        pots = halves_of(first_row_pot)
        shifted = [scores[half] + pots[half] for half in range(2)]
        high = jnp.maximum(jnp.max(shifted[0], axis=0), jnp.max(shifted[1], axis=0))
        total = jnp.sum(jnp.exp(shifted[0] - high), axis=0) + jnp.sum(jnp.exp(shifted[1] - high), axis=0)
        first_col_pot = math.log(target) - over_rows(log_sum, high + jnp.log(total))
        plan = [jnp.exp(scores[half] + pots[half] + first_col_pot[None, :]) for half in range(2)]
        col_scale = jnp.ones((group_cols,), jnp.float32)
        for sweep in range(1, ITERS):
            row_sum = over_cols(add, both(lambda half: jnp.sum(plan[half] * col_scale[None, :], axis=1)))
            if sweep < ITERS - 1:
                row_scale = halves_of(1 / row_sum)
                part = [jnp.sum(plan[half] * row_scale[half], axis=0) for half in range(2)]
                col_scale = target / over_rows(add, part[0] + part[1])
        return jnp.concatenate([first_row_pot - jnp.log(row_sum), first_col_pot + jnp.log(col_scale)])

    count = 2 * row_count
    known = lax.cond(core == 1, rounds, lambda: jnp.zeros((count + group_cols,), jnp.float32))
    got = swap(known, "row", 1)
    row_pot = jnp.where(core == 1, known[:count], reorder(got[:count], 2, 1))
    col_pot = jnp.where(core == 1, known[count : count + half_cols], got[count + half_cols :])

    pots = halves_of(row_pot)
    weights = [jnp.exp(scores[half][:, :half_cols] + pots[half] + col_pot[None, :]) for half in range(2)]
    mass = over_rows(add, jnp.sum(weights[0], axis=0) + jnp.sum(weights[1], axis=0))
    held = add(
        [
            lax.dot_general(
                weights[half].astype(jnp.bfloat16),
                span_halves[half],
                (((0,), (0,)), ((), ())),
                preferred_element_type=jnp.float32,
            )
            for half in range(2)
        ]
    ).reshape(chips, per, width)
    for at, size in stages("row"):
        me = digit("row", at, size)
        held = held.reshape((-1, size) + held.shape[1:])
        low = held.astype(jnp.bfloat16)
        parts = [lax.dynamic_index_in_dim(held, me, 1, keepdims=False)]
        for d in range(1, size):
            block = lax.dynamic_index_in_dim(low, me ^ d, 1, keepdims=False)
            parts.append(swap(block, "row", d << at).astype(jnp.float32))
        held = add(parts)
    own_mass = lax.dynamic_slice_in_dim(mass, me_row // 2 * per, per, 0)
    col_pot = col_pot + math.log(target) - jnp.log(mass)
    col_pots = jnp.stack([col_pot, swap(col_pot, "row", 1)]).reshape(2, chips, per)
    col_pots = jnp.where(core == 1, col_pots[::-1], col_pots)
    return (
        (held.reshape(per, width) * (target * mass_ratio / own_mass)[:, None]).astype(jnp.bfloat16),
        unxor(row_pot[:row_count], me_col, cols),
        col_pots.swapaxes(0, 1).reshape(-1),
    )


def solution(mesh):
    placed = (P(("row", "col"), None), P(("col", "row"), None), P("row", None))
    return jax.shard_map(
        per_device,
        mesh=mesh,
        in_specs=placed,
        out_specs=(P(("col", "row"), None), P("row"), P("col")),
        check_vma=False,
    )
```

```python
import math

import jax
import jax.numpy as jnp
from jax import lax
from jax.sharding import PartitionSpec as P

ITERS = 3


logit_scale = 0.0625
floor_value = -1e30


def swap(x, axis, k):
    return lax.ppermute(x, axis, [(i, i ^ k) for i in range(lax.axis_size(axis))])


def swap_by_core(x, axis, for_core):
    cols = lax.axis_size("col")
    scale = cols if axis == "row" else 1
    pairs = [(i, i ^ (for_core[i // cols & 1] * scale)) for i in range(lax.axis_size("row") * cols)]
    return lax.ppermute(x, ("row", "col"), pairs)


def stages(axis):
    low = 1 if axis == "row" else 0
    bits = (lax.axis_size(axis) - 1).bit_length()
    return [(at, 1 << min(2, bits - at)) for at in range(low, bits, 2)]


def digit(axis, at, size):
    return (lax.axis_index(axis) >> at) & (size - 1)


def gather_spans(x, pattern, core):
    first = None
    for at, size in stages("col"):
        parts = [x] + [swap(x, "col", d << at) for d in range(1, min(size, 3))]
        first = parts[1] if first is None else first
        if size == 4:
            passed_on = jnp.where(core == 1, parts[2], parts[1])
            parts.append(swap_by_core(passed_on, "col", (2 << at, 1 << at)))
        x = jnp.concatenate(parts)
    lists, entries = pattern.shape
    rows = -(-lists // 16) * 16
    note = jnp.pad(pattern.astype(x.dtype), ((0, rows - lists), (0, x.shape[1] - entries)))
    got = swap(jnp.concatenate(parts[:3] + [note]), "row", 1)
    split = got.shape[0] - rows
    mate = [got[:split]] + [swap(part, "row", 1) for part in parts[3:]]
    return jnp.concatenate([x] + mate), got[split : split + lists, :entries].astype(jnp.int32), first


def after(x, other):
    return lax.optimization_barrier((x, other))[0]


def gather_centroids(x, first):
    for at, size in stages("row"):
        parts = [x] + [swap(after(x, first) if d << at == 2 else x, "row", d << at) for d in range(1, size)]
        whole = jnp.zeros((size,) + x.shape, x.dtype)
        for d, part in enumerate(parts):
            whole = lax.dynamic_update_index_in_dim(whole, part, digit("row", at, size) ^ d, 0)
        x = whole.reshape((-1,) + x.shape[1:])
    return x


def reorder(x, blocks, k):
    x = x.reshape((blocks, -1) + x.shape[1:])
    return jnp.concatenate([x[p ^ k] for p in range(blocks)])


def unxor(x, index, blocks):
    shape = x.shape
    bit = 1
    while bit < blocks:
        pairs = x.reshape((blocks // (2 * bit), 2, -1) + shape[1:])
        x = jnp.where((index & bit) != 0, pairs[:, ::-1], pairs).reshape(shape)
        bit *= 2
    return x


def tree(op, parts):
    while len(parts) > 1:
        parts = [op(parts[i], parts[i + 1]) for i in range(0, len(parts), 2)]
    return parts[0]


def add(parts):
    return tree(jnp.add, parts)


def log_sum(parts):
    high = tree(jnp.maximum, parts)
    return high + jnp.log(add([jnp.exp(part - high) for part in parts]))


def over_rows(merge, x):
    for at, size in stages("row"):
        x = merge([x] + [swap(x, "row", d << at) for d in range(1, size)])
    return x


def over_cols(merge, x):
    cols = lax.axis_size("col")
    for at, size in stages("col"):
        parts = [x]
        for d in range(1, size):
            halves = swap(x, "col", d << at).reshape(2, -1)
            parts.append(jnp.concatenate([reorder(half, cols, d << at) for half in halves]))
        x = merge(parts)
    return x


def in_thirds(x, width):
    thirds = []
    for step in range(3):
        top = lax.reduce_precision(x, 8, 7)
        thirds.append(top.astype(jnp.bfloat16))
        x = x - top
    return jnp.pad(jnp.stack(thirds), ((0, 5), (0, width - x.shape[0])))


def from_thirds(rows, count):
    thirds = rows[:3, :count].astype(jnp.float32)
    return thirds[0] + thirds[1] + thirds[2]


def per_device(spans, centroids, pattern):
    rows, cols = lax.axis_size("row"), lax.axis_size("col")
    chips = rows // 2
    me_row, me_col = lax.axis_index("row"), lax.axis_index("col")
    core = me_row % 2
    per, width = centroids.shape
    half_cols = per * chips
    group_cols = 2 * half_cols
    row_count = spans.shape[0] * cols
    mass_ratio = group_cols * cols / (row_count * rows)
    target = 1 / mass_ratio

    tile_spans, mate_pattern, first = gather_spans(spans, pattern, core)
    own_centroids = gather_centroids(centroids, first)
    tile_centroids = jnp.concatenate([own_centroids, swap(own_centroids, "row", 1)])
    row_lists = jnp.concatenate(
        [unxor(jnp.repeat(lists, 128, axis=0), me_col, cols) for lists in (pattern, mate_pattern)]
    )
    at = jnp.arange(group_cols)
    row_of = at % half_cols // per * 2 + (at // half_cols ^ core)
    col_block = (me_col * group_cols + row_of * per + at % per) // 128
    allowed_cells = jnp.any(row_lists[:, :, None] == col_block[None, None, :], axis=1)
    products = lax.dot_general(
        tile_spans, tile_centroids, (((1,), (1,)), ((), ())), preferred_element_type=jnp.float32
    )
    scores = jnp.where(allowed_cells, products * logit_scale, floor_value)

    def scaled(row_pot, col_pot):
        return jnp.exp(scores + row_pot[:, None] + col_pot[None, :])

    def rounds():
        high = jnp.max(scores, axis=1)
        total = jnp.sum(jnp.exp(scores - high[:, None]), axis=1)
        row_pot = -over_cols(log_sum, high + jnp.log(total))
        shifted = scores + row_pot[:, None]
        high = jnp.max(shifted, axis=0)
        total = jnp.sum(jnp.exp(shifted - high[None, :]), axis=0)
        col_pot = math.log(target) - over_rows(log_sum, high + jnp.log(total))
        for sweep in range(1, ITERS):
            row_pot = row_pot - jnp.log(over_cols(add, jnp.sum(scaled(row_pot, col_pot), axis=1)))
            if sweep < ITERS - 1:
                mass = over_rows(add, jnp.sum(scaled(row_pot, col_pot), axis=0))
                col_pot = col_pot + math.log(target) - jnp.log(mass)
        return row_pot, col_pot

    def nothing():
        return jnp.zeros((2 * row_count,), jnp.float32), jnp.zeros((group_cols,), jnp.float32)

    row_pot, col_pot = lax.cond(core == 1, rounds, nothing)
    row_pot = jnp.where(core == 1, row_pot, reorder(swap(row_pot, "row", 1), 2, 1))
    col_pot = jnp.where(core == 1, col_pot, reorder(swap(col_pot, "row", 1), 2, 1))

    weights = scaled(row_pot, col_pot)
    mass = add(list(jnp.sum(weights.reshape(2, row_count, group_cols), axis=1)))
    held = lax.dot_general(
        weights[:, :half_cols].astype(jnp.bfloat16),
        tile_spans,
        (((0,), (0,)), ((), ())),
        preferred_element_type=jnp.float32,
    ).reshape(chips, per, width)
    for at, size in stages("row"):
        me = digit("row", at, size)
        held = held.reshape((-1, size) + held.shape[1:])
        low = held.astype(jnp.bfloat16)
        note = in_thirds(mass, width)
        parts, masses = [lax.dynamic_index_in_dim(held, me, 1, keepdims=False)], [from_thirds(note, group_cols)]
        for d in range(1, size):
            block = lax.dynamic_index_in_dim(low, me ^ d, 1, keepdims=False).reshape(-1, width)
            got = swap(jnp.concatenate([block, note]), "row", d << at)
            parts.append(got[: block.shape[0]].astype(jnp.float32).reshape(parts[0].shape))
            masses.append(from_thirds(got[block.shape[0] :], group_cols))
        held, mass = add(parts), add(masses)
    own_mass = lax.dynamic_slice_in_dim(mass, me_row // 2 * per, per, 0)
    col_pots = (col_pot + math.log(target) - jnp.log(mass)).reshape(2, chips, per)
    col_pots = jnp.where(core == 1, col_pots[::-1], col_pots)
    return (
        (held.reshape(per, width) * (target * mass_ratio / own_mass)[:, None]).astype(jnp.bfloat16),
        unxor(row_pot[:row_count], me_col, cols),
        col_pots.swapaxes(0, 1).reshape(-1),
    )


def solution(mesh):
    placed = (P(("row", "col"), None), P(("col", "row"), None), P("row", None))
    return jax.shard_map(
        per_device,
        mesh=mesh,
        in_specs=placed,
        out_specs=(P(("col", "row"), None), P("row"), P("col")),
        check_vma=False,
    )
```

```python
import functools
import math

import jax
import jax.numpy as jnp
from jax import lax
from jax.experimental import pallas as pl
from jax.experimental.pallas import tpu as pltpu
from jax.sharding import PartitionSpec as P

ITERS = 3


logit_scale = 0.0625
floor_value = -1e30


def swap(x, axis, k):
    return lax.ppermute(x, axis, [(i, i ^ k) for i in range(lax.axis_size(axis))])


def swap_by_core(x, axis, for_core):
    cols = lax.axis_size("col")
    scale = cols if axis == "row" else 1
    pairs = [(i, i ^ (for_core[i // cols & 1] * scale)) for i in range(lax.axis_size("row") * cols)]
    return lax.ppermute(x, ("row", "col"), pairs)


def stages(axis):
    low = 1 if axis == "row" else 0
    bits = (lax.axis_size(axis) - 1).bit_length()
    return [(at, 1 << min(2, bits - at)) for at in range(low, bits, 2)]


def digit(axis, at, size):
    return (lax.axis_index(axis) >> at) & (size - 1)


def gather_spans(x, core):
    first = None
    parts = [x]
    for at, size in stages("col"):
        x = jnp.concatenate(parts)
        parts = [x] + [swap(x, "col", d << at) for d in range(1, min(size, 3))]
        first = parts[1] if first is None else first
        near = parts
        if size == 4:
            passed_on = jnp.where(core == 1, parts[2], parts[1])
            near = lax.optimization_barrier((parts, passed_on))[0]
            parts = parts + [swap_by_core(passed_on, "col", (2 << at, 1 << at))]
    mate = [swap(part, "row", 1) for part in near + parts[3:]]
    return parts, mate, first


def after(x, other):
    return lax.optimization_barrier((x, other))[0]


def gather_centroids(x, first):
    for at, size in stages("row"):
        if at > 1:
            whole = jnp.zeros((len(parts),) + x.shape, x.dtype)
            for d, part in enumerate(parts):
                whole = lax.dynamic_update_index_in_dim(whole, part, digit("row", *last) ^ d, 0)
            x = whole.reshape((-1,) + x.shape[1:])
        parts = [x] + [swap(after(x, first) if d << at == 2 else x, "row", d << at) for d in range(1, size)]
        last = at, size
    return parts


def tile_kernel(rows, own_count, centroid_count, *refs):
    info, own_lists, mate_lists, col_block = refs[:4]
    spans = refs[4 : 4 + 2 * own_count]
    own_centroids = refs[4 + 2 * own_count : 4 + 2 * own_count + centroid_count]
    mate_centroids, scores, stacked, table = refs[4 + 2 * own_count + centroid_count :]
    block = own_centroids[0].shape[0]
    half = centroid_count * block
    for d, part in enumerate(own_centroids):
        start = pl.multiple_of((info[1] ^ d) * block, block)
        table[pl.ds(start, block), :] = part[...]
        table[pl.ds(half + start, block), :] = mate_centroids[d * block : (d + 1) * block, :]
    count = spans[0].shape[0]
    for number, part in enumerate(spans):
        lists = own_lists if number < own_count else mate_lists
        top = number * count
        stacked[top : top + count, :] = part[...]
        products = lax.dot_general(
            part[...], table[...], (((1,), (1,)), ((), ())), preferred_element_type=jnp.float32
        )
        for piece in range(count // rows):
            device = info[0] ^ (number % own_count * (count // rows) + piece)
            row_block = lax.div(device * rows, 128)
            keep = jnp.zeros(col_block.shape, jnp.float32)
            for entry in range(lists.shape[1]):
                keep = jnp.where(col_block[...] == lists[row_block, entry], 1.0, keep)
            keep = jnp.broadcast_to(keep, (rows, keep.shape[1]))
            scores[top + piece * rows : top + (piece + 1) * rows, :] = jnp.where(
                keep > 0.5, products[piece * rows : (piece + 1) * rows] * logit_scale, floor_value
            )


def tile(info, own_lists, mate_lists, col_block, own, mate, centroid_parts, mate_centroids, rows):
    count, width = own[0].shape
    total, group_cols = 2 * len(own) * count, 2 * mate_centroids.shape[0]
    in_smem, in_vmem = pl.BlockSpec(memory_space=pltpu.SMEM), pl.BlockSpec(memory_space=pltpu.VMEM)
    return pl.pallas_call(
        functools.partial(tile_kernel, rows, len(own), len(centroid_parts)),
        out_shape=(
            jax.ShapeDtypeStruct((total, group_cols), jnp.float32),
            jax.ShapeDtypeStruct((total, width), own[0].dtype),
        ),
        in_specs=[in_smem] * 3 + [in_vmem] * (2 * len(own) + len(centroid_parts) + 2),
        out_specs=(in_vmem, in_vmem),
        scratch_shapes=[pltpu.VMEM((group_cols, width), own[0].dtype)],
        compiler_params=pltpu.CompilerParams(vmem_limit_bytes=16 << 20),
        cost_estimate=pl.CostEstimate(
            flops=2 * total * group_cols * width, bytes_accessed=8 << 20, transcendentals=0
        ),
    )(info, own_lists, mate_lists, col_block, *own, *mate, *centroid_parts, mate_centroids)


def reorder(x, blocks, k):
    x = x.reshape((blocks, -1) + x.shape[1:])
    return jnp.concatenate([x[p ^ k] for p in range(blocks)])


def unxor(x, index, blocks):
    shape = x.shape
    bit = 1
    while bit < blocks:
        pairs = x.reshape((blocks // (2 * bit), 2, -1) + shape[1:])
        x = jnp.where((index & bit) != 0, pairs[:, ::-1], pairs).reshape(shape)
        bit *= 2
    return x


def tree(op, parts):
    while len(parts) > 1:
        parts = [op(parts[i], parts[i + 1]) for i in range(0, len(parts), 2)]
    return parts[0]


def add(parts):
    return tree(jnp.add, parts)


def log_sum(parts):
    high = tree(jnp.maximum, parts)
    return high + jnp.log(add([jnp.exp(part - high) for part in parts]))


def over_rows(merge, x):
    for at, size in stages("row"):
        x = merge([x] + [swap(x, "row", d << at) for d in range(1, size)])
    return x


def over_cols(merge, x):
    cols = lax.axis_size("col")
    for at, size in stages("col"):
        parts = [x]
        for d in range(1, size):
            halves = swap(x, "col", d << at).reshape(2, -1)
            parts.append(jnp.concatenate([reorder(half, cols, d << at) for half in halves]))
        x = merge(parts)
    return x


def in_thirds(x, width):
    thirds = []
    for step in range(3):
        top = lax.reduce_precision(x, 8, 7)
        thirds.append(top.astype(jnp.bfloat16))
        x = x - top
    return jnp.pad(jnp.stack(thirds), ((0, 5), (0, width - x.shape[0])))


def from_thirds(rows, count):
    thirds = rows[:3, :count].astype(jnp.float32)
    return thirds[0] + thirds[1] + thirds[2]


def per_device(spans, centroids, pattern):
    rows, cols = lax.axis_size("row"), lax.axis_size("col")
    chips = rows // 2
    me_row, me_col = lax.axis_index("row"), lax.axis_index("col")
    core = me_row % 2
    per, width = centroids.shape
    half_cols = per * chips
    group_cols = 2 * half_cols
    row_count = spans.shape[0] * cols
    mass_ratio = group_cols * cols / (row_count * rows)
    target = 1 / mass_ratio

    mate_pattern = swap(pattern, "row", 1)
    own_parts, mate_parts, first = gather_spans(spans, core)
    centroid_parts = gather_centroids(centroids, first)
    mate_centroids = swap(jnp.concatenate(centroid_parts), "row", 1)
    at = jnp.arange(group_cols)
    row_of = at % half_cols // per * 2 + (at // half_cols ^ core)
    col_block = (me_col * group_cols + row_of * per + at % per) // 128
    info = jnp.stack([me_col, digit("row", *stages("row")[-1])])
    scores, tile_spans = tile(
        info,
        pattern,
        mate_pattern,
        col_block[None, :],
        own_parts,
        mate_parts,
        centroid_parts,
        mate_centroids,
        spans.shape[0],
    )

    def scaled(row_pot, col_pot):
        return jnp.exp(scores + row_pot[:, None] + col_pot[None, :])

    def rounds():
        high = jnp.max(scores, axis=1)
        total = jnp.sum(jnp.exp(scores - high[:, None]), axis=1)
        row_pot = -over_cols(log_sum, high + jnp.log(total))
        shifted = scores + row_pot[:, None]
        high = jnp.max(shifted, axis=0)
        total = jnp.sum(jnp.exp(shifted - high[None, :]), axis=0)
        col_pot = math.log(target) - over_rows(log_sum, high + jnp.log(total))
        for sweep in range(1, ITERS):
            row_pot = row_pot - jnp.log(over_cols(add, jnp.sum(scaled(row_pot, col_pot), axis=1)))
            if sweep < ITERS - 1:
                mass = over_rows(add, jnp.sum(scaled(row_pot, col_pot), axis=0))
                col_pot = col_pot + math.log(target) - jnp.log(mass)
        return jnp.concatenate([row_pot.reshape(-1, group_cols), col_pot[None]])

    def nothing():
        return jnp.zeros((2 * row_count // group_cols + 1, group_cols), jnp.float32)

    known = lax.cond(core == 1, rounds, nothing)
    got = swap(known, "row", 1)
    row_pot = jnp.where(core == 1, known[:-1].reshape(-1), reorder(got[:-1].reshape(-1), 2, 1))
    col_pot = jnp.where(core == 1, known[-1], reorder(got[-1], 2, 1))

    weights = scaled(row_pot, col_pot)
    mass = add(list(jnp.sum(weights.reshape(2, row_count, group_cols), axis=1)))
    held = lax.dot_general(
        weights[:, :half_cols].astype(jnp.bfloat16),
        tile_spans,
        (((0,), (0,)), ((), ())),
        preferred_element_type=jnp.float32,
    ).reshape(chips, per, width)
    for at, size in stages("row"):
        me = digit("row", at, size)
        held = held.reshape((-1, size) + held.shape[1:])
        low = held.astype(jnp.bfloat16)
        note = in_thirds(mass, width)
        parts, masses = [lax.dynamic_index_in_dim(held, me, 1, keepdims=False)], [from_thirds(note, group_cols)]
        for d in range(1, size):
            block = lax.dynamic_index_in_dim(low, me ^ d, 1, keepdims=False).reshape(-1, width)
            got = swap(jnp.concatenate([block, note]), "row", d << at)
            parts.append(got[: block.shape[0]].astype(jnp.float32).reshape(parts[0].shape))
            masses.append(from_thirds(got[block.shape[0] :], group_cols))
        held, mass = add(parts), add(masses)
    own_mass = lax.dynamic_slice_in_dim(mass, me_row // 2 * per, per, 0)
    col_pots = (col_pot + math.log(target) - jnp.log(mass)).reshape(2, chips, per)
    col_pots = jnp.where(core == 1, col_pots[::-1], col_pots)
    return (
        (held.reshape(per, width) * (target * mass_ratio / own_mass)[:, None]).astype(jnp.bfloat16),
        unxor(row_pot[:row_count], me_col, cols),
        col_pots.swapaxes(0, 1).reshape(-1),
    )


def solution(mesh):
    placed = (P(("row", "col"), None), P(("col", "row"), None), P("row", None))
    return jax.shard_map(
        per_device,
        mesh=mesh,
        in_specs=placed,
        out_specs=(P(("col", "row"), None), P("row"), P("col")),
        check_vma=False,
    )
```

```python
import math

import jax
import jax.numpy as jnp
from jax import lax
from jax.sharding import PartitionSpec as P

ITERS = 3


logit_scale = 0.0625
floor_value = -1e30


def swap(x, axis, k):
    return lax.ppermute(x, axis, [(i, i ^ k) for i in range(lax.axis_size(axis))])


def swap_by_core(x, axis, for_core):
    cols = lax.axis_size("col")
    scale = cols if axis == "row" else 1
    pairs = [(i, i ^ (for_core[i // cols & 1] * scale)) for i in range(lax.axis_size("row") * cols)]
    return lax.ppermute(x, ("row", "col"), pairs)


def stages(axis):
    low = 1 if axis == "row" else 0
    bits = (lax.axis_size(axis) - 1).bit_length()
    return [(at, 1 << min(2, bits - at)) for at in range(low, bits, 2)]


def digit(axis, at, size):
    return (lax.axis_index(axis) >> at) & (size - 1)


def gather_spans(x, core):
    first = None
    parts = [x]
    ready = x
    for at, size in stages("col"):
        x = jnp.concatenate(parts)
        parts = [x] + [swap(x, "col", d << at) for d in range(1, min(size, 3))]
        first = parts[1] if first is None else first
        near = parts
        if size == 4:
            passed_on = jnp.where(core == 1, parts[2], parts[1])
            near = lax.optimization_barrier((parts, passed_on))[0]
            ready = passed_on
            parts = parts + [swap_by_core(passed_on, "col", (2 << at, 1 << at))]
    mate = [swap(part, "row", 1) for part in near + parts[3:]]
    return parts, mate, first, ready


def after(x, other):
    return lax.optimization_barrier((x, other))[0]


def placed(parts, index):
    whole = jnp.zeros((len(parts),) + parts[0].shape, parts[0].dtype)
    for d, part in enumerate(parts):
        whole = lax.dynamic_update_index_in_dim(whole, part, index ^ d, 0)
    return whole.reshape((-1,) + parts[0].shape[1:])


def gather_centroids(x, first, ready):
    for at, size in stages("row"):
        parts = [x] + [swap(after(x, first) if d << at == 2 else x, "row", d << at) for d in range(1, size)]
        mate = [swap(after(part, ready), "row", 1) for part in parts]
        position = digit("row", at, size)
        x = placed(parts, position)
    return jnp.concatenate([x, placed(mate, position)])


def reorder(x, blocks, k):
    x = x.reshape((blocks, -1) + x.shape[1:])
    return jnp.concatenate([x[p ^ k] for p in range(blocks)])


def unxor(x, index, blocks):
    shape = x.shape
    bit = 1
    while bit < blocks:
        pairs = x.reshape((blocks // (2 * bit), 2, -1) + shape[1:])
        x = jnp.where((index & bit) != 0, pairs[:, ::-1], pairs).reshape(shape)
        bit *= 2
    return x


def tree(op, parts):
    while len(parts) > 1:
        parts = [op(parts[i], parts[i + 1]) for i in range(0, len(parts), 2)]
    return parts[0]


def add(parts):
    return tree(jnp.add, parts)


def log_sum(parts):
    high = tree(jnp.maximum, parts)
    return high + jnp.log(add([jnp.exp(part - high) for part in parts]))


def over_rows(merge, x):
    for at, size in stages("row"):
        x = merge([x] + [swap(x, "row", d << at) for d in range(1, size)])
    return x


def over_cols(merge, x):
    cols = lax.axis_size("col")
    for at, size in stages("col"):
        parts = [x]
        for d in range(1, size):
            halves = swap(x, "col", d << at).reshape(2, -1)
            parts.append(jnp.concatenate([reorder(half, cols, d << at) for half in halves]))
        x = merge(parts)
    return x


def in_thirds(x, width):
    thirds = []
    for step in range(3):
        top = lax.reduce_precision(x, 8, 7)
        thirds.append(top.astype(jnp.bfloat16))
        x = x - top
    return jnp.pad(jnp.stack(thirds), ((0, 5), (0, width - x.shape[0])))


def from_thirds(rows, count):
    thirds = rows[:3, :count].astype(jnp.float32)
    return thirds[0] + thirds[1] + thirds[2]


def per_device(spans, centroids, pattern):
    rows, cols = lax.axis_size("row"), lax.axis_size("col")
    chips = rows // 2
    me_row, me_col = lax.axis_index("row"), lax.axis_index("col")
    core = me_row % 2
    per, width = centroids.shape
    half_cols = per * chips
    group_cols = 2 * half_cols
    row_count = spans.shape[0] * cols
    mass_ratio = group_cols * cols / (row_count * rows)
    target = 1 / mass_ratio

    mate_pattern = swap(pattern, "row", 1)
    own_parts, mate_parts, first, ready = gather_spans(spans, core)
    tile_centroids = gather_centroids(centroids, first, ready)
    span_halves = [jnp.concatenate(own_parts), jnp.concatenate(mate_parts)]
    at = jnp.arange(group_cols)
    row_of = at % half_cols // per * 2 + (at // half_cols ^ core)
    col_block = (me_col * group_cols + row_of * per + at % per) // 128

    def half_scores(lists, span_half):
        row_lists = unxor(jnp.repeat(lists, 128, axis=0), me_col, cols)
        allowed_cells = jnp.any(row_lists[:, :, None] == col_block[None, None, :], axis=1)
        products = lax.dot_general(
            span_half, tile_centroids, (((1,), (1,)), ((), ())), preferred_element_type=jnp.float32
        )
        return jnp.where(allowed_cells, products * logit_scale, floor_value)

    scores = [half_scores(pattern, span_halves[0]), half_scores(mate_pattern, span_halves[1])]

    def with_rows(row_pot):
        return [half + row_pot[n * row_count : (n + 1) * row_count, None] for n, half in enumerate(scores)]

    def row_sums(row_pot, col_pot):
        return jnp.concatenate([jnp.sum(jnp.exp(x + col_pot[None, :]), axis=1) for x in with_rows(row_pot)])

    def col_sums(row_pot, col_pot):
        return add([jnp.sum(jnp.exp(x + col_pot[None, :]), axis=0) for x in with_rows(row_pot)])

    def rounds():
        highs = [jnp.max(half, axis=1) for half in scores]
        totals = [jnp.sum(jnp.exp(half - high[:, None]), axis=1) for half, high in zip(scores, highs)]
        row_pot = -over_cols(log_sum, jnp.concatenate([high + jnp.log(total) for high, total in zip(highs, totals)]))
        high = tree(jnp.maximum, [jnp.max(x, axis=0) for x in with_rows(row_pot)])
        total = col_sums(row_pot, -high)
        col_pot = math.log(target) - over_rows(log_sum, high + jnp.log(total))
        for sweep in range(1, ITERS):
            row_pot = row_pot - jnp.log(over_cols(add, row_sums(row_pot, col_pot)))
            if sweep < ITERS - 1:
                mass = over_rows(add, col_sums(row_pot, col_pot))
                col_pot = col_pot + math.log(target) - jnp.log(mass)
        return jnp.concatenate([row_pot.reshape(-1, group_cols), col_pot[None]])

    def nothing():
        return jnp.zeros((2 * row_count // group_cols + 1, group_cols), jnp.float32)

    known = lax.cond(core == 1, rounds, nothing)
    got = swap(known, "row", 1)
    row_pot = jnp.where(core == 1, known[:-1].reshape(-1), reorder(got[:-1].reshape(-1), 2, 1))
    col_pot = jnp.where(core == 1, known[-1], reorder(got[-1], 2, 1))

    mass = col_sums(row_pot, col_pot)
    held = add(
        [
            lax.dot_general(
                jnp.exp(x[:, :half_cols] + col_pot[None, :half_cols]).astype(jnp.bfloat16),
                span_half,
                (((0,), (0,)), ((), ())),
                preferred_element_type=jnp.float32,
            )
            for x, span_half in zip(with_rows(row_pot), span_halves)
        ]
    ).reshape(chips, per, width)
    for at, size in stages("row"):
        me = digit("row", at, size)
        held = held.reshape((-1, size) + held.shape[1:])
        low = held.astype(jnp.bfloat16)
        note = in_thirds(mass, width)
        parts, masses = [lax.dynamic_index_in_dim(held, me, 1, keepdims=False)], [from_thirds(note, group_cols)]
        for d in range(1, size):
            block = lax.dynamic_index_in_dim(low, me ^ d, 1, keepdims=False).reshape(-1, width)
            got = swap(jnp.concatenate([block, note]), "row", d << at)
            parts.append(got[: block.shape[0]].astype(jnp.float32).reshape(parts[0].shape))
            masses.append(from_thirds(got[block.shape[0] :], group_cols))
        held, mass = add(parts), add(masses)
    own_mass = lax.dynamic_slice_in_dim(mass, me_row // 2 * per, per, 0)
    col_pots = (col_pot + math.log(target) - jnp.log(mass)).reshape(2, chips, per)
    col_pots = jnp.where(core == 1, col_pots[::-1], col_pots)
    return (
        (held.reshape(per, width) * (target * mass_ratio / own_mass)[:, None]).astype(jnp.bfloat16),
        unxor(row_pot[:row_count], me_col, cols),
        col_pots.swapaxes(0, 1).reshape(-1),
    )


def solution(mesh):
    placed = (P(("row", "col"), None), P(("col", "row"), None), P("row", None))
    return jax.shard_map(
        per_device,
        mesh=mesh,
        in_specs=placed,
        out_specs=(P(("col", "row"), None), P("row"), P("col")),
        check_vma=False,
    )
```

```python
import math

import jax
import jax.numpy as jnp
from jax import lax
from jax.sharding import PartitionSpec as P

ITERS = 3


logit_scale = 0.0625
floor_value = -1e30


def swap(x, axis, k):
    return lax.ppermute(x, axis, [(i, i ^ k) for i in range(lax.axis_size(axis))])


def swap_by_core(x, axis, for_core):
    cols = lax.axis_size("col")
    scale = cols if axis == "row" else 1
    pairs = [(i, i ^ (for_core[i // cols & 1] * scale)) for i in range(lax.axis_size("row") * cols)]
    return lax.ppermute(x, ("row", "col"), pairs)


def stages(axis):
    low = 1 if axis == "row" else 0
    bits = (lax.axis_size(axis) - 1).bit_length()
    return [(at, 1 << min(2, bits - at)) for at in range(low, bits, 2)]


def digit(axis, at, size):
    return (lax.axis_index(axis) >> at) & (size - 1)


def after(x, other):
    return lax.optimization_barrier((x, other))[0]


def gather_spans(x, core):
    parts = [x]
    for at, size in stages("col"):
        x = jnp.concatenate(parts)
        parts = [x] + [swap(x, "col", d << at) for d in range(1, min(size, 3))]
        if size == 4:
            passed_on = jnp.where(core == 1, parts[2], parts[1])
            parts.append(swap_by_core(passed_on, "col", (2 << at, 1 << at)))
    return parts, parts[-1]


def placed(parts, index):
    whole = jnp.zeros((len(parts),) + parts[0].shape, parts[0].dtype)
    for d, part in enumerate(parts):
        whole = lax.dynamic_update_index_in_dim(whole, part, index ^ d, 0)
    return whole.reshape((-1,) + parts[0].shape[1:])


def gather_centroids(x):
    parts = [x]
    for at, size in stages("row"):
        x = placed(parts, digit("row", *last)) if at > 1 else x
        parts = [x] + [swap(x, "row", d << at) for d in range(1, size)]
        last = at, size
    return parts


def with_mate(parts, ready):
    parts = [after(part, ready) for part in parts]
    return parts, [swap(part, "row", 1) for part in parts]


def reorder(x, blocks, k):
    x = x.reshape((blocks, -1) + x.shape[1:])
    return jnp.concatenate([x[p ^ k] for p in range(blocks)])


def unxor(x, index, blocks):
    shape = x.shape
    bit = 1
    while bit < blocks:
        pairs = x.reshape((blocks // (2 * bit), 2, -1) + shape[1:])
        x = jnp.where((index & bit) != 0, pairs[:, ::-1], pairs).reshape(shape)
        bit *= 2
    return x


def tree(op, parts):
    while len(parts) > 1:
        parts = [op(parts[i], parts[i + 1]) for i in range(0, len(parts), 2)]
    return parts[0]


def add(parts):
    return tree(jnp.add, parts)


def log_sum(parts):
    high = tree(jnp.maximum, parts)
    return high + jnp.log(add([jnp.exp(part - high) for part in parts]))


def over_rows(merge, x):
    for at, size in stages("row"):
        x = merge([x] + [swap(x, "row", d << at) for d in range(1, size)])
    return x


def over_cols(merge, x):
    cols = lax.axis_size("col")
    for at, size in stages("col"):
        parts = [x]
        for d in range(1, size):
            halves = swap(x, "col", d << at).reshape(2, -1)
            parts.append(jnp.concatenate([reorder(half, cols, d << at) for half in halves]))
        x = merge(parts)
    return x


def in_thirds(x, width):
    thirds = []
    for step in range(3):
        top = lax.reduce_precision(x, 8, 7)
        thirds.append(top.astype(jnp.bfloat16))
        x = x - top
    return jnp.pad(jnp.stack(thirds), ((0, 5), (0, width - x.shape[0])))


def from_thirds(rows, count):
    thirds = rows[:3, :count].astype(jnp.float32)
    return thirds[0] + thirds[1] + thirds[2]


def per_device(spans, centroids, pattern):
    rows, cols = lax.axis_size("row"), lax.axis_size("col")
    chips = rows // 2
    me_row, me_col = lax.axis_index("row"), lax.axis_index("col")
    core = me_row % 2
    per, width = centroids.shape
    half_cols = per * chips
    group_cols = 2 * half_cols
    row_count = spans.shape[0] * cols
    mass_ratio = group_cols * cols / (row_count * rows)
    target = 1 / mass_ratio

    own_parts, ready = gather_spans(spans, core)
    span_halves = [jnp.concatenate(parts) for parts in with_mate(own_parts, ready)]
    position = digit("row", *stages("row")[-1])
    centroid_halves = with_mate(gather_centroids(centroids), ready)
    tile_centroids = jnp.concatenate([placed(parts, position) for parts in centroid_halves])
    at = jnp.arange(group_cols)
    row_of = at % half_cols // per * 2 + (at // half_cols ^ core)
    blocks = jnp.arange(group_cols // 128)
    in_block = ((row_of * per + at % per) // 128 == blocks[:, None]).astype(jnp.bfloat16)

    def half_scores(lists, span_half):
        listed = jnp.any(lists[:, :, None] == me_col * blocks.shape[0] + blocks, axis=1)
        listed = unxor(jnp.repeat(listed, 128 // spans.shape[0], axis=0).astype(jnp.bfloat16), me_col, cols)
        allowed_cells = jnp.dot(
            jnp.repeat(listed, spans.shape[0], axis=0), in_block, preferred_element_type=jnp.float32
        )
        products = lax.dot_general(
            span_half, tile_centroids, (((1,), (1,)), ((), ())), preferred_element_type=jnp.float32
        )
        return jnp.where(allowed_cells > 0.5, products * logit_scale, floor_value)

    all_lists = with_mate([pattern], ready)
    scores = [half_scores(lists[0], span_half) for lists, span_half in zip(all_lists, span_halves)]

    def with_rows(row_pot):
        return [half + row_pot[n * row_count : (n + 1) * row_count, None] for n, half in enumerate(scores)]

    def row_sums(row_pot, col_pot):
        return jnp.concatenate([jnp.sum(jnp.exp(x + col_pot[None, :]), axis=1) for x in with_rows(row_pot)])

    def col_sums(row_pot, col_pot):
        return add([jnp.sum(jnp.exp(x + col_pot[None, :]), axis=0) for x in with_rows(row_pot)])

    def rounds():
        highs = [jnp.max(half, axis=1) for half in scores]
        totals = [jnp.sum(jnp.exp(half - high[:, None]), axis=1) for half, high in zip(scores, highs)]
        row_pot = -over_cols(log_sum, jnp.concatenate([high + jnp.log(total) for high, total in zip(highs, totals)]))
        high = tree(jnp.maximum, [jnp.max(x, axis=0) for x in with_rows(row_pot)])
        total = col_sums(row_pot, -high)
        col_pot = math.log(target) - over_rows(log_sum, high + jnp.log(total))
        for sweep in range(1, ITERS):
            row_pot = row_pot - jnp.log(over_cols(add, row_sums(row_pot, col_pot)))
            if sweep < ITERS - 1:
                mass = over_rows(add, col_sums(row_pot, col_pot))
                col_pot = col_pot + math.log(target) - jnp.log(mass)
        return jnp.concatenate([row_pot.reshape(-1, group_cols), col_pot[None]])

    def nothing():
        return jnp.zeros((2 * row_count // group_cols + 1, group_cols), jnp.float32)

    known = lax.cond(core == 1, rounds, nothing)
    got = swap(known, "row", 1)
    row_pot = jnp.where(core == 1, known[:-1].reshape(-1), reorder(got[:-1].reshape(-1), 2, 1))
    col_pot = jnp.where(core == 1, known[-1], reorder(got[-1], 2, 1))

    mass = col_sums(row_pot, col_pot)
    held = add(
        [
            lax.dot_general(
                jnp.exp(x[:, :half_cols] + col_pot[None, :half_cols]).astype(jnp.bfloat16),
                span_half,
                (((0,), (0,)), ((), ())),
                preferred_element_type=jnp.float32,
            )
            for x, span_half in zip(with_rows(row_pot), span_halves)
        ]
    ).reshape(chips, per, width)
    for at, size in stages("row"):
        me = digit("row", at, size)
        held = held.reshape((-1, size) + held.shape[1:])
        low = held.astype(jnp.bfloat16)
        note = in_thirds(mass, width)
        parts, masses = [lax.dynamic_index_in_dim(held, me, 1, keepdims=False)], [from_thirds(note, group_cols)]
        for d in range(1, size):
            block = lax.dynamic_index_in_dim(low, me ^ d, 1, keepdims=False).reshape(-1, width)
            got = swap(jnp.concatenate([block, note]), "row", d << at)
            if d << at == 2:
                row_pot = after(row_pot, got)
            parts.append(got[: block.shape[0]].astype(jnp.float32).reshape(parts[0].shape))
            masses.append(from_thirds(got[block.shape[0] :], group_cols))
        held, mass = add(parts), add(masses)
    own_mass = lax.dynamic_slice_in_dim(mass, me_row // 2 * per, per, 0)
    col_pots = (col_pot + math.log(target) - jnp.log(mass)).reshape(2, chips, per)
    col_pots = jnp.where(core == 1, col_pots[::-1], col_pots)
    return (
        (held.reshape(per, width) * (target * mass_ratio / own_mass)[:, None]).astype(jnp.bfloat16),
        unxor(row_pot[:row_count], me_col, cols),
        col_pots.swapaxes(0, 1).reshape(-1),
    )


def solution(mesh):
    placed = (P(("row", "col"), None), P(("col", "row"), None), P("row", None))
    return jax.shard_map(
        per_device,
        mesh=mesh,
        in_specs=placed,
        out_specs=(P(("col", "row"), None), P("row"), P("col")),
        check_vma=False,
    )
```

```python
import math

import jax
import jax.numpy as jnp
from jax import lax
from jax.sharding import PartitionSpec as P

ITERS = 3


logit_scale = 0.0625
floor_value = -1e30


def swap(x, axis, k):
    return lax.ppermute(x, axis, [(i, i ^ k) for i in range(lax.axis_size(axis))])


def swap_by_core(x, axis, for_core):
    cols = lax.axis_size("col")
    scale = cols if axis == "row" else 1
    pairs = [(i, i ^ (for_core[i // cols & 1] * scale)) for i in range(lax.axis_size("row") * cols)]
    return lax.ppermute(x, ("row", "col"), pairs)


def stages(axis):
    low = 1 if axis == "row" else 0
    bits = (lax.axis_size(axis) - 1).bit_length()
    return [(at, 1 << min(2, bits - at)) for at in range(low, bits, 2)]


def digit(axis, at, size):
    return (lax.axis_index(axis) >> at) & (size - 1)


def after(x, other):
    return lax.optimization_barrier((x, other))[0]


def gather_spans(x, core):
    parts = [x]
    for at, size in stages("col"):
        x = jnp.concatenate(parts)
        parts = [x] + [swap(x, "col", d << at) for d in range(1, min(size, 3))]
        if size == 4:
            passed_on = jnp.where(core == 1, parts[2], parts[1])
            parts.append(swap_by_core(passed_on, "col", (2 << at, 1 << at)))
    return parts, parts[-1]


def placed(parts, index):
    whole = jnp.zeros((len(parts),) + parts[0].shape, parts[0].dtype)
    for d, part in enumerate(parts):
        whole = lax.dynamic_update_index_in_dim(whole, part, index ^ d, 0)
    return whole.reshape((-1,) + parts[0].shape[1:])


def gather_centroids(x):
    parts = [x]
    for at, size in stages("row"):
        x = placed(parts, digit("row", *last)) if at > 1 else x
        parts = [x] + [swap(x, "row", d << at) for d in range(1, size)]
        last = at, size
    return parts


def with_mate(parts, ready):
    parts = [after(part, ready) for part in parts]
    mate = [swap(parts[0], "row", 1)]
    if len(parts) > 1:
        got = swap(jnp.concatenate(parts[1:]), "row", 1)
        mate += jnp.split(got, len(parts) - 1)
    return parts, mate


def reorder(x, blocks, k):
    x = x.reshape((blocks, -1) + x.shape[1:])
    return jnp.concatenate([x[p ^ k] for p in range(blocks)])


def unxor(x, index, blocks):
    shape = x.shape
    bit = 1
    while bit < blocks:
        pairs = x.reshape((blocks // (2 * bit), 2, -1) + shape[1:])
        x = jnp.where((index & bit) != 0, pairs[:, ::-1], pairs).reshape(shape)
        bit *= 2
    return x


def tree(op, parts):
    while len(parts) > 1:
        parts = [op(parts[i], parts[i + 1]) for i in range(0, len(parts), 2)]
    return parts[0]


def add(parts):
    return tree(jnp.add, parts)


def log_sum(parts):
    high = tree(jnp.maximum, parts)
    return high + jnp.log(add([jnp.exp(part - high) for part in parts]))


def over_rows(merge, x):
    for at, size in stages("row"):
        x = merge([x] + [swap(x, "row", d << at) for d in range(1, size)])
    return x


def over_cols(merge, x):
    cols = lax.axis_size("col")
    for at, size in stages("col"):
        parts = [x]
        for d in range(1, size):
            halves = swap(x, "col", d << at).reshape(2, -1)
            parts.append(jnp.concatenate([reorder(half, cols, d << at) for half in halves]))
        x = merge(parts)
    return x


def in_thirds(x, width):
    thirds = []
    for step in range(3):
        top = lax.reduce_precision(x, 8, 7)
        thirds.append(top.astype(jnp.bfloat16))
        x = x - top
    return jnp.pad(jnp.stack(thirds), ((0, 5), (0, width - x.shape[0])))


def from_thirds(rows, count):
    thirds = rows[:3, :count].astype(jnp.float32)
    return thirds[0] + thirds[1] + thirds[2]


def per_device(spans, centroids, pattern):
    rows, cols = lax.axis_size("row"), lax.axis_size("col")
    chips = rows // 2
    me_row, me_col = lax.axis_index("row"), lax.axis_index("col")
    core = me_row % 2
    per, width = centroids.shape
    half_cols = per * chips
    group_cols = 2 * half_cols
    row_count = spans.shape[0] * cols
    mass_ratio = group_cols * cols / (row_count * rows)
    target = 1 / mass_ratio

    own_parts, ready = gather_spans(spans, core)
    span_halves = [jnp.concatenate(parts) for parts in with_mate(own_parts, ready)]
    position = digit("row", *stages("row")[-1])
    centroid_halves = with_mate(gather_centroids(centroids), ready)
    tile_centroids = jnp.concatenate([placed(parts, position) for parts in centroid_halves])
    at = jnp.arange(group_cols)
    row_of = at % half_cols // per * 2 + (at // half_cols ^ core)
    blocks = jnp.arange(group_cols // 128)
    in_block = ((row_of * per + at % per) // 128 == blocks[:, None]).astype(jnp.bfloat16)

    def half_scores(lists, span_half):
        listed = jnp.any(lists[:, :, None] == me_col * blocks.shape[0] + blocks, axis=1)
        listed = unxor(jnp.repeat(listed, 128 // spans.shape[0], axis=0).astype(jnp.bfloat16), me_col, cols)
        allowed_cells = jnp.dot(
            jnp.repeat(listed, spans.shape[0], axis=0), in_block, preferred_element_type=jnp.float32
        )
        products = lax.dot_general(
            span_half, tile_centroids, (((1,), (1,)), ((), ())), preferred_element_type=jnp.float32
        )
        return jnp.where(allowed_cells > 0.5, products * logit_scale, floor_value)

    all_lists = with_mate([pattern], ready)
    scores = [half_scores(lists[0], span_half) for lists, span_half in zip(all_lists, span_halves)]

    def with_rows(row_pot):
        return [half + row_pot[n * row_count : (n + 1) * row_count, None] for n, half in enumerate(scores)]

    def row_sums(row_pot, col_pot):
        return jnp.concatenate([jnp.sum(jnp.exp(x + col_pot[None, :]), axis=1) for x in with_rows(row_pot)])

    def col_sums(row_pot, col_pot):
        return add([jnp.sum(jnp.exp(x + col_pot[None, :]), axis=0) for x in with_rows(row_pot)])

    def rounds():
        highs = [jnp.max(half, axis=1) for half in scores]
        totals = [jnp.sum(jnp.exp(half - high[:, None]), axis=1) for half, high in zip(scores, highs)]
        row_pot = -over_cols(log_sum, jnp.concatenate([high + jnp.log(total) for high, total in zip(highs, totals)]))
        high = tree(jnp.maximum, [jnp.max(x, axis=0) for x in with_rows(row_pot)])
        total = col_sums(row_pot, -high)
        col_pot = math.log(target) - over_rows(log_sum, high + jnp.log(total))
        for sweep in range(1, ITERS):
            row_pot = row_pot - jnp.log(over_cols(add, row_sums(row_pot, col_pot)))
            if sweep < ITERS - 1:
                mass = over_rows(add, col_sums(row_pot, col_pot))
                col_pot = col_pot + math.log(target) - jnp.log(mass)
        return jnp.concatenate([row_pot.reshape(-1, group_cols), col_pot[None]])

    def nothing():
        return jnp.zeros((2 * row_count // group_cols + 1, group_cols), jnp.float32)

    known = lax.cond(core == 1, rounds, nothing)
    got = swap(known, "row", 1)
    row_pot = jnp.where(core == 1, known[:-1].reshape(-1), reorder(got[:-1].reshape(-1), 2, 1))
    col_pot = jnp.where(core == 1, known[-1], reorder(got[-1], 2, 1))

    mass = col_sums(row_pot, col_pot)
    held = add(
        [
            lax.dot_general(
                jnp.exp(x[:, :half_cols] + col_pot[None, :half_cols]).astype(jnp.bfloat16),
                span_half,
                (((0,), (0,)), ((), ())),
                preferred_element_type=jnp.float32,
            )
            for x, span_half in zip(with_rows(row_pot), span_halves)
        ]
    ).reshape(chips, per, width)
    for at, size in stages("row"):
        me = digit("row", at, size)
        held = held.reshape((-1, size) + held.shape[1:])
        low = held.astype(jnp.bfloat16)
        note = in_thirds(mass, width)
        parts, masses = [lax.dynamic_index_in_dim(held, me, 1, keepdims=False)], [from_thirds(note, group_cols)]
        for d in range(1, size):
            block = lax.dynamic_index_in_dim(low, me ^ d, 1, keepdims=False).reshape(-1, width)
            got = swap(jnp.concatenate([block, note]), "row", d << at)
            if d << at == 2:
                row_pot = after(row_pot, got)
            parts.append(got[: block.shape[0]].astype(jnp.float32).reshape(parts[0].shape))
            masses.append(from_thirds(got[block.shape[0] :], group_cols))
        held, mass = add(parts), add(masses)
    own_mass = lax.dynamic_slice_in_dim(mass, me_row // 2 * per, per, 0)
    col_pots = (col_pot + math.log(target) - jnp.log(mass)).reshape(2, chips, per)
    col_pots = jnp.where(core == 1, col_pots[::-1], col_pots)
    return (
        (held.reshape(per, width) * (target * mass_ratio / own_mass)[:, None]).astype(jnp.bfloat16),
        unxor(row_pot[:row_count], me_col, cols),
        col_pots.swapaxes(0, 1).reshape(-1),
    )


def solution(mesh):
    placed = (P(("row", "col"), None), P(("col", "row"), None), P("row", None))
    return jax.shard_map(
        per_device,
        mesh=mesh,
        in_specs=placed,
        out_specs=(P(("col", "row"), None), P("row"), P("col")),
        check_vma=False,
    )
```

```python
import math

import jax
import jax.numpy as jnp
from jax import lax
from jax.sharding import PartitionSpec as P

ITERS = 3


logit_scale = 0.0625
floor_value = -1e30


def swap(x, axis, k):
    return lax.ppermute(x, axis, [(i, i ^ k) for i in range(lax.axis_size(axis))])


def swap_by_core(x, axis, for_core):
    cols = lax.axis_size("col")
    scale = cols if axis == "row" else 1
    pairs = [(i, i ^ (for_core[i // cols & 1] * scale)) for i in range(lax.axis_size("row") * cols)]
    return lax.ppermute(x, ("row", "col"), pairs)


def stages(axis):
    low = 1 if axis == "row" else 0
    bits = (lax.axis_size(axis) - 1).bit_length()
    return [(at, 1 << min(2, bits - at)) for at in range(low, bits, 2)]


def digit(axis, at, size):
    return (lax.axis_index(axis) >> at) & (size - 1)


def after(x, other):
    return lax.optimization_barrier((x, other))[0]


def gather_spans(x, core):
    first = None
    parts = [x]
    ready = x
    for at, size in stages("col"):
        x = jnp.concatenate(parts)
        parts = [x] + [swap(x, "col", d << at) for d in range(1, min(size, 3))]
        first = parts[1] if first is None else first
        near = parts
        if size == 4:
            passed_on = jnp.where(core == 1, parts[2], parts[1])
            near = lax.optimization_barrier((parts, passed_on))[0]
            ready = passed_on
            parts = parts + [swap_by_core(passed_on, "col", (2 << at, 1 << at))]
    mate = [swap(part, "row", 1) for part in near + parts[3:]]
    return [after(parts[0], parts[-1])] + parts[1:], mate, first, ready


def placed(parts, index):
    whole = jnp.zeros((len(parts),) + parts[0].shape, parts[0].dtype)
    for d, part in enumerate(parts):
        whole = lax.dynamic_update_index_in_dim(whole, part, index ^ d, 0)
    return whole.reshape((-1,) + parts[0].shape[1:])


def gather_centroids(x, first, ready, last):
    for at, size in stages("row"):
        parts = [x] + [swap(after(x, first) if d << at == 2 else x, "row", d << at) for d in range(1, size)]
        mate = [swap(after(part, last if part is x else ready), "row", 1) for part in parts]
        position = digit("row", at, size)
        x = placed([after(parts[0], last)] + parts[1:], position)
    return jnp.concatenate([x, placed(mate, position)])


def reorder(x, blocks, k):
    x = x.reshape((blocks, -1) + x.shape[1:])
    return jnp.concatenate([x[p ^ k] for p in range(blocks)])


def unxor(x, index, blocks):
    shape = x.shape
    bit = 1
    while bit < blocks:
        pairs = x.reshape((blocks // (2 * bit), 2, -1) + shape[1:])
        x = jnp.where((index & bit) != 0, pairs[:, ::-1], pairs).reshape(shape)
        bit *= 2
    return x


def tree(op, parts):
    while len(parts) > 1:
        parts = [op(parts[i], parts[i + 1]) for i in range(0, len(parts), 2)]
    return parts[0]


def add(parts):
    return tree(jnp.add, parts)


def log_sum(parts):
    high = tree(jnp.maximum, parts)
    return high + jnp.log(add([jnp.exp(part - high) for part in parts]))


def over_rows(merge, x):
    for at, size in stages("row"):
        x = merge([x] + [swap(x, "row", d << at) for d in range(1, size)])
    return x


def over_cols(merge, x):
    cols = lax.axis_size("col")
    for at, size in stages("col"):
        parts = [x]
        for d in range(1, size):
            halves = swap(x, "col", d << at).reshape(2, -1)
            parts.append(jnp.concatenate([reorder(half, cols, d << at) for half in halves]))
        x = merge(parts)
    return x


def in_thirds(x, width):
    thirds = []
    for step in range(3):
        top = lax.reduce_precision(x, 8, 7)
        thirds.append(top.astype(jnp.bfloat16))
        x = x - top
    return jnp.pad(jnp.stack(thirds), ((0, 5), (0, width - x.shape[0])))


def from_thirds(rows, count):
    thirds = rows[:3, :count].astype(jnp.float32)
    return thirds[0] + thirds[1] + thirds[2]


def per_device(spans, centroids, pattern):
    rows, cols = lax.axis_size("row"), lax.axis_size("col")
    chips = rows // 2
    me_row, me_col = lax.axis_index("row"), lax.axis_index("col")
    core = me_row % 2
    per, width = centroids.shape
    half_cols = per * chips
    group_cols = 2 * half_cols
    row_count = spans.shape[0] * cols
    mass_ratio = group_cols * cols / (row_count * rows)
    target = 1 / mass_ratio

    own_parts, mate_parts, first, ready = gather_spans(spans, core)
    pattern = after(pattern, own_parts[-1])
    mate_pattern = swap(pattern, "row", 1)
    tile_centroids = gather_centroids(centroids, first, ready, own_parts[-1])
    span_halves = [jnp.concatenate(own_parts), jnp.concatenate(mate_parts)]
    at = jnp.arange(group_cols)
    row_of = at % half_cols // per * 2 + (at // half_cols ^ core)
    blocks = jnp.arange(group_cols // 128)
    in_block = ((row_of * per + at % per) // 128 == blocks[:, None]).astype(jnp.bfloat16)

    def half_scores(lists, span_half):
        listed = jnp.any(lists[:, :, None] == me_col * blocks.shape[0] + blocks, axis=1)
        listed = unxor(jnp.repeat(listed, 128 // spans.shape[0], axis=0).astype(jnp.bfloat16), me_col, cols)
        allowed_cells = jnp.dot(
            jnp.repeat(listed, spans.shape[0], axis=0), in_block, preferred_element_type=jnp.float32
        )
        products = lax.dot_general(
            span_half, tile_centroids, (((1,), (1,)), ((), ())), preferred_element_type=jnp.float32
        )
        return jnp.where(allowed_cells > 0.5, products * logit_scale, floor_value)

    scores = [half_scores(pattern, span_halves[0]), half_scores(mate_pattern, span_halves[1])]

    def with_rows(row_pot):
        return [half + row_pot[n * row_count : (n + 1) * row_count, None] for n, half in enumerate(scores)]

    def row_sums(row_pot, col_pot):
        return jnp.concatenate([jnp.sum(jnp.exp(x + col_pot[None, :]), axis=1) for x in with_rows(row_pot)])

    def col_sums(row_pot, col_pot):
        return add([jnp.sum(jnp.exp(x + col_pot[None, :]), axis=0) for x in with_rows(row_pot)])

    def rounds():
        highs = [jnp.max(half, axis=1) for half in scores]
        totals = [jnp.sum(jnp.exp(half - high[:, None]), axis=1) for half, high in zip(scores, highs)]
        row_pot = -over_cols(log_sum, jnp.concatenate([high + jnp.log(total) for high, total in zip(highs, totals)]))
        high = tree(jnp.maximum, [jnp.max(x, axis=0) for x in with_rows(row_pot)])
        total = col_sums(row_pot, -high)
        col_pot = math.log(target) - over_rows(log_sum, high + jnp.log(total))
        for sweep in range(1, ITERS):
            row_pot = row_pot - jnp.log(over_cols(add, row_sums(row_pot, col_pot)))
            if sweep < ITERS - 1:
                mass = over_rows(add, col_sums(row_pot, col_pot))
                col_pot = col_pot + math.log(target) - jnp.log(mass)
        return jnp.concatenate([row_pot.reshape(-1, group_cols), col_pot[None]])

    def nothing():
        return jnp.zeros((2 * row_count // group_cols + 1, group_cols), jnp.float32)

    known = lax.cond(core == 1, rounds, nothing)
    got = swap(known, "row", 1)
    row_pot = jnp.where(core == 1, known[:-1].reshape(-1), reorder(got[:-1].reshape(-1), 2, 1))
    col_pot = jnp.where(core == 1, known[-1], reorder(got[-1], 2, 1))

    mass = col_sums(row_pot, col_pot)
    held = add(
        [
            lax.dot_general(
                jnp.exp(x[:, :half_cols] + col_pot[None, :half_cols]).astype(jnp.bfloat16),
                span_half,
                (((0,), (0,)), ((), ())),
                preferred_element_type=jnp.float32,
            )
            for x, span_half in zip(with_rows(row_pot), span_halves)
        ]
    ).reshape(chips, per, width)
    for at, size in stages("row"):
        me = digit("row", at, size)
        held = held.reshape((-1, size) + held.shape[1:])
        low = held.astype(jnp.bfloat16)
        note = in_thirds(mass, width)
        parts = [lax.dynamic_index_in_dim(held, me, 1, keepdims=False)] + [None] * (size - 1)
        masses = [from_thirds(note, group_cols)] + [None] * (size - 1)
        for d in reversed(range(1, size)):
            block = lax.dynamic_index_in_dim(low, me ^ d, 1, keepdims=False).reshape(-1, width)
            message = jnp.concatenate([block, note])
            got = swap(message, "row", d << at)
            if d << at == 2:
                row_out = unxor(after(row_pot[:row_count], got), me_col, cols)
            parts[d] = got[: block.shape[0]].astype(jnp.float32).reshape(parts[0].shape)
            masses[d] = from_thirds(got[block.shape[0] :], group_cols)
        held, mass = add(parts), add(masses)
    own_mass = lax.dynamic_slice_in_dim(mass, me_row // 2 * per, per, 0)
    col_pots = (col_pot + math.log(target) - jnp.log(mass)).reshape(2, chips, per)
    col_pots = jnp.where(core == 1, col_pots[::-1], col_pots)
    return (
        (held.reshape(per, width) * (target * mass_ratio / own_mass)[:, None]).astype(jnp.bfloat16),
        row_out,
        col_pots.swapaxes(0, 1).reshape(-1),
    )


def solution(mesh):
    placed = (P(("row", "col"), None), P(("col", "row"), None), P("row", None))
    return jax.shard_map(
        per_device,
        mesh=mesh,
        in_specs=placed,
        out_specs=(P(("col", "row"), None), P("row"), P("col")),
        check_vma=False,
    )
```

```python
import math

import jax
import jax.numpy as jnp
from jax import lax
from jax.sharding import PartitionSpec as P

ITERS = 3


logit_scale = 0.0625
floor_value = -1e30


def swap(x, axis, k):
    return lax.ppermute(x, axis, [(i, i ^ k) for i in range(lax.axis_size(axis))])


def swap_by_core(x, axis, for_core):
    cols = lax.axis_size("col")
    scale = cols if axis == "row" else 1
    pairs = [(i, i ^ (for_core[i // cols & 1] * scale)) for i in range(lax.axis_size("row") * cols)]
    return lax.ppermute(x, ("row", "col"), pairs)


def stages(axis):
    low = 1 if axis == "row" else 0
    bits = (lax.axis_size(axis) - 1).bit_length()
    return [(at, 1 << min(2, bits - at)) for at in range(low, bits, 2)]


def digit(axis, at, size):
    return (lax.axis_index(axis) >> at) & (size - 1)


def gather_spans(x, core):
    first = None
    parts = [x]
    ready = x
    for at, size in stages("col"):
        x = jnp.concatenate(parts)
        parts = [x] + [swap(x, "col", d << at) for d in range(1, min(size, 3))]
        first = parts[1] if first is None else first
        near = parts
        if size == 4:
            passed_on = jnp.where(core == 1, parts[2], parts[1])
            near = lax.optimization_barrier((parts, passed_on))[0]
            ready = passed_on
            parts = parts + [swap_by_core(passed_on, "col", (2 << at, 1 << at))]
    mate = [swap(part, "row", 1) for part in near + parts[3:]]
    return parts, mate, first, ready


def after(x, other):
    return lax.optimization_barrier((x, other))[0]


def placed(parts, index):
    whole = jnp.zeros((len(parts),) + parts[0].shape, parts[0].dtype)
    for d, part in enumerate(parts):
        whole = lax.dynamic_update_index_in_dim(whole, part, index ^ d, 0)
    return whole.reshape((-1,) + parts[0].shape[1:])


def gather_centroids(x, first, ready):
    for at, size in stages("row"):
        parts = [x] + [swap(after(x, first) if d << at == 2 else x, "row", d << at) for d in range(1, size)]
        mate = [swap(after(part, ready), "row", 1) for part in parts]
        position = digit("row", at, size)
        x = placed(parts, position)
    return jnp.concatenate([x, placed(mate, position)])


def reorder(x, blocks, k):
    x = x.reshape((blocks, -1) + x.shape[1:])
    return jnp.concatenate([x[p ^ k] for p in range(blocks)])


def unxor(x, index, blocks):
    shape = x.shape
    bit = 1
    while bit < blocks:
        pairs = x.reshape((blocks // (2 * bit), 2, -1) + shape[1:])
        x = jnp.where((index & bit) != 0, pairs[:, ::-1], pairs).reshape(shape)
        bit *= 2
    return x


def tree(op, parts):
    while len(parts) > 1:
        parts = [op(parts[i], parts[i + 1]) for i in range(0, len(parts), 2)]
    return parts[0]


def add(parts):
    return tree(jnp.add, parts)


def log_sum(parts):
    high = tree(jnp.maximum, parts)
    return high + jnp.log(add([jnp.exp(part - high) for part in parts]))


def over_rows(merge, x):
    for at, size in stages("row"):
        x = merge([x] + [swap(x, "row", d << at) for d in range(1, size)])
    return x


def over_cols(merge, x):
    cols = lax.axis_size("col")
    for at, size in stages("col"):
        parts = [x]
        for d in range(1, size):
            halves = swap(x, "col", d << at).reshape(2, -1)
            parts.append(jnp.concatenate([reorder(half, cols, d << at) for half in halves]))
        x = merge(parts)
    return x


def in_thirds(x, width):
    thirds = []
    for step in range(3):
        top = lax.reduce_precision(x, 8, 7)
        thirds.append(top.astype(jnp.bfloat16))
        x = x - top
    return jnp.pad(jnp.stack(thirds), ((0, 5), (0, width - x.shape[0])))


def from_thirds(rows, count):
    thirds = rows[:3, :count].astype(jnp.float32)
    return thirds[0] + thirds[1] + thirds[2]


def per_device(spans, centroids, pattern):
    rows, cols = lax.axis_size("row"), lax.axis_size("col")
    chips = rows // 2
    me_row, me_col = lax.axis_index("row"), lax.axis_index("col")
    core = me_row % 2
    per, width = centroids.shape
    half_cols = per * chips
    group_cols = 2 * half_cols
    row_count = spans.shape[0] * cols
    mass_ratio = group_cols * cols / (row_count * rows)
    target = 1 / mass_ratio

    mate_pattern = swap(pattern, "row", 1)
    own_parts, mate_parts, first, ready = gather_spans(spans, core)
    tile_centroids = gather_centroids(centroids, first, ready)
    span_halves = [jnp.concatenate(own_parts), jnp.concatenate(mate_parts)]
    at = jnp.arange(group_cols)
    row_of = at % half_cols // per * 2 + (at // half_cols ^ core)
    blocks = jnp.arange(group_cols // 128)
    in_block = ((row_of * per + at % per) // 128 == blocks[:, None]).astype(jnp.bfloat16)

    def half_scores(lists, span_half):
        listed = jnp.any(lists[:, :, None] == me_col * blocks.shape[0] + blocks, axis=1)
        listed = unxor(jnp.repeat(listed, 128 // spans.shape[0], axis=0).astype(jnp.bfloat16), me_col, cols)
        allowed_cells = jnp.dot(
            jnp.repeat(listed, spans.shape[0], axis=0), in_block, preferred_element_type=jnp.float32
        )
        products = lax.dot_general(
            span_half, tile_centroids, (((1,), (1,)), ((), ())), preferred_element_type=jnp.float32
        )
        return jnp.where(allowed_cells > 0.5, products * logit_scale, floor_value)

    scores = [half_scores(pattern, span_halves[0]), half_scores(mate_pattern, span_halves[1])]

    def with_rows(row_pot):
        return [half + row_pot[n * row_count : (n + 1) * row_count, None] for n, half in enumerate(scores)]

    def row_sums(row_pot, col_pot):
        return jnp.concatenate([jnp.sum(jnp.exp(x + col_pot[None, :]), axis=1) for x in with_rows(row_pot)])

    def col_sums(row_pot, col_pot):
        return add([jnp.sum(jnp.exp(x + col_pot[None, :]), axis=0) for x in with_rows(row_pot)])

    def rounds():
        highs = [jnp.max(half, axis=1) for half in scores]
        totals = [jnp.sum(jnp.exp(half - high[:, None]), axis=1) for half, high in zip(scores, highs)]
        row_pot = -over_cols(log_sum, jnp.concatenate([high + jnp.log(total) for high, total in zip(highs, totals)]))
        high = tree(jnp.maximum, [jnp.max(x, axis=0) for x in with_rows(row_pot)])
        total = col_sums(row_pot, -high)
        col_pot = math.log(target) - over_rows(log_sum, high + jnp.log(total))
        for sweep in range(1, ITERS):
            row_pot = row_pot - jnp.log(over_cols(add, row_sums(row_pot, col_pot)))
            if sweep < ITERS - 1:
                mass = over_rows(add, col_sums(row_pot, col_pot))
                col_pot = col_pot + math.log(target) - jnp.log(mass)
        return jnp.concatenate([row_pot.reshape(-1, group_cols), col_pot[None]])

    def nothing():
        return jnp.zeros((2 * row_count // group_cols + 1, group_cols), jnp.float32)

    known = lax.cond(core == 1, rounds, nothing)
    got = swap(known, "row", 1)
    row_pot = jnp.where(core == 1, known[:-1].reshape(-1), reorder(got[:-1].reshape(-1), 2, 1))
    col_pot = jnp.where(core == 1, known[-1], reorder(got[-1], 2, 1))

    mass = col_sums(row_pot, col_pot)
    held = add(
        [
            lax.dot_general(
                jnp.exp(x[:, :half_cols] + col_pot[None, :half_cols]).astype(jnp.bfloat16),
                span_half,
                (((0,), (0,)), ((), ())),
                preferred_element_type=jnp.float32,
            )
            for x, span_half in zip(with_rows(row_pot), span_halves)
        ]
    ).reshape(chips, per, width)
    for at, size in stages("row"):
        me = digit("row", at, size)
        held = held.reshape((-1, size) + held.shape[1:])
        low = held.astype(jnp.bfloat16)
        note = in_thirds(mass, width)
        parts, masses = [lax.dynamic_index_in_dim(held, me, 1, keepdims=False)], [from_thirds(note, group_cols)]
        for d in range(1, size):
            block = lax.dynamic_index_in_dim(low, me ^ d, 1, keepdims=False).reshape(-1, width)
            got = swap(jnp.concatenate([block, note]), "row", d << at)
            if d << at == 2:
                row_out = unxor(after(row_pot[:row_count], got), me_col, cols)
            parts.append(got[: block.shape[0]].astype(jnp.float32).reshape(parts[0].shape))
            masses.append(from_thirds(got[block.shape[0] :], group_cols))
        held, mass = add(parts), add(masses)
    own_mass = lax.dynamic_slice_in_dim(mass, me_row // 2 * per, per, 0)
    col_pots = (col_pot + math.log(target) - jnp.log(mass)).reshape(2, chips, per)
    col_pots = jnp.where(core == 1, col_pots[::-1], col_pots)
    return (
        (held.reshape(per, width) * (target * mass_ratio / own_mass)[:, None]).astype(jnp.bfloat16),
        row_out,
        col_pots.swapaxes(0, 1).reshape(-1),
    )


def solution(mesh):
    placed = (P(("row", "col"), None), P(("col", "row"), None), P("row", None))
    return jax.shard_map(
        per_device,
        mesh=mesh,
        in_specs=placed,
        out_specs=(P(("col", "row"), None), P("row"), P("col")),
        check_vma=False,
    )
```

```python
import math

import jax
import jax.numpy as jnp
from jax import lax
from jax.sharding import PartitionSpec as P

ITERS = 3


logit_scale = 0.0625
floor_value = -1e30


def swap(x, axis, k):
    return lax.ppermute(x, axis, [(i, i ^ k) for i in range(lax.axis_size(axis))])


def swap_by_core(x, axis, for_core):
    cols = lax.axis_size("col")
    scale = cols if axis == "row" else 1
    pairs = [(i, i ^ (for_core[i // cols & 1] * scale)) for i in range(lax.axis_size("row") * cols)]
    return lax.ppermute(x, ("row", "col"), pairs)


def stages(axis):
    low = 1 if axis == "row" else 0
    bits = (lax.axis_size(axis) - 1).bit_length()
    return [(at, 1 << min(2, bits - at)) for at in range(low, bits, 2)]


def digit(axis, at, size):
    return (lax.axis_index(axis) >> at) & (size - 1)


def gather_spans(x, core):
    first = None
    parts = [x]
    ready = x
    for at, size in stages("col"):
        x = jnp.concatenate(parts)
        parts = [x] + [swap(x, "col", d << at) for d in range(1, min(size, 3))]
        first = parts[1] if first is None else first
        near = parts
        if size == 4:
            passed_on = jnp.where(core == 1, parts[2], parts[1])
            near = lax.optimization_barrier((parts, passed_on))[0]
            ready = passed_on
            parts = parts + [swap_by_core(passed_on, "col", (2 << at, 1 << at))]
    mate = [swap(part, "row", 1) for part in near + parts[3:]]
    return parts, mate, first, ready


def after(x, other):
    return lax.optimization_barrier((x, other))[0]


def placed(parts, index):
    whole = jnp.zeros((len(parts),) + parts[0].shape, parts[0].dtype)
    for d, part in enumerate(parts):
        whole = lax.dynamic_update_index_in_dim(whole, part, index ^ d, 0)
    return whole.reshape((-1,) + parts[0].shape[1:])


def gather_centroids(x, ready):
    for at, size in stages("row"):
        parts = [x] + [after(swap(x, "row", d << at), ready) for d in range(1, size)]
        mate = [swap(after(part, ready) if part is x else part, "row", 1) for part in parts]
        position = digit("row", at, size)
        x = placed(parts, position)
    return jnp.concatenate([x, placed(mate, position)])


def reorder(x, blocks, k):
    x = x.reshape((blocks, -1) + x.shape[1:])
    return jnp.concatenate([x[p ^ k] for p in range(blocks)])


def unxor(x, index, blocks):
    shape = x.shape
    bit = 1
    while bit < blocks:
        pairs = x.reshape((blocks // (2 * bit), 2, -1) + shape[1:])
        x = jnp.where((index & bit) != 0, pairs[:, ::-1], pairs).reshape(shape)
        bit *= 2
    return x


def unxor_list(parts, index):
    bit = 1
    while bit < len(parts):
        parts = [jnp.where((index & bit) != 0, parts[p ^ bit], part) for p, part in enumerate(parts)]
        bit *= 2
    return parts


def tree(op, parts):
    while len(parts) > 1:
        parts = [op(parts[i], parts[i + 1]) for i in range(0, len(parts), 2)]
    return parts[0]


def add(parts):
    return tree(jnp.add, parts)


def log_sum(parts):
    high = tree(jnp.maximum, parts)
    return high + jnp.log(add([jnp.exp(part - high) for part in parts]))


def over_rows(merge, x):
    for at, size in stages("row"):
        x = merge([x] + [swap(x, "row", d << at) for d in range(1, size)])
    return x


def over_cols(merge, x):
    cols = lax.axis_size("col")
    for at, size in stages("col"):
        parts = [x]
        for d in range(1, size):
            halves = swap(x, "col", d << at).reshape(2, -1)
            parts.append(jnp.concatenate([reorder(half, cols, d << at) for half in halves]))
        x = merge(parts)
    return x


def in_thirds(x, width):
    thirds = []
    for step in range(3):
        top = lax.reduce_precision(x, 8, 7)
        thirds.append(top.astype(jnp.bfloat16))
        x = x - top
    return jnp.pad(jnp.stack(thirds), ((0, 5), (0, width - x.shape[0])))


def from_thirds(rows, count):
    thirds = rows[:3, :count].astype(jnp.float32)
    return thirds[0] + thirds[1] + thirds[2]


def per_device(spans, centroids, pattern):
    rows, cols = lax.axis_size("row"), lax.axis_size("col")
    chips = rows // 2
    me_row, me_col = lax.axis_index("row"), lax.axis_index("col")
    core = me_row % 2
    per, width = centroids.shape
    half_cols = per * chips
    group_cols = 2 * half_cols
    row_count = spans.shape[0] * cols
    mass_ratio = group_cols * cols / (row_count * rows)
    target = 1 / mass_ratio

    own_parts, mate_parts, first, ready = gather_spans(spans, core)
    mate_pattern = swap(after(pattern, first), "row", 1)
    tile_centroids = gather_centroids(centroids, ready)
    span_halves = [jnp.concatenate(own_parts), jnp.concatenate(mate_parts)]
    at = jnp.arange(group_cols)
    row_of = at % half_cols // per * 2 + (at // half_cols ^ core)
    blocks = jnp.arange(group_cols // 128)
    in_block = ((row_of * per + at % per) // 128 == blocks[:, None]).astype(jnp.bfloat16)

    def half_scores(lists, span_half):
        listed = jnp.any(lists[:, :, None] == me_col * blocks.shape[0] + blocks, axis=1)
        listed = unxor(jnp.repeat(listed, 128 // spans.shape[0], axis=0).astype(jnp.bfloat16), me_col, cols)
        allowed_cells = jnp.dot(
            jnp.repeat(listed, spans.shape[0], axis=0), in_block, preferred_element_type=jnp.float32
        )
        products = lax.dot_general(
            span_half, tile_centroids, (((1,), (1,)), ((), ())), preferred_element_type=jnp.float32
        )
        return jnp.where(allowed_cells > 0.5, products * logit_scale, floor_value)

    scores = [half_scores(pattern, span_halves[0]), half_scores(mate_pattern, span_halves[1])]

    def with_rows(row_pot):
        return [half + row_pot[n * row_count : (n + 1) * row_count, None] for n, half in enumerate(scores)]

    def row_sums(row_pot, col_pot):
        return jnp.concatenate([jnp.sum(jnp.exp(x + col_pot[None, :]), axis=1) for x in with_rows(row_pot)])

    def col_sums(row_pot, col_pot):
        return add([jnp.sum(jnp.exp(x + col_pot[None, :]), axis=0) for x in with_rows(row_pot)])

    def rounds():
        highs = [jnp.max(half, axis=1) for half in scores]
        totals = [jnp.sum(jnp.exp(half - high[:, None]), axis=1) for half, high in zip(scores, highs)]
        row_pot = -over_cols(log_sum, jnp.concatenate([high + jnp.log(total) for high, total in zip(highs, totals)]))
        high = tree(jnp.maximum, [jnp.max(x, axis=0) for x in with_rows(row_pot)])
        total = col_sums(row_pot, -high)
        col_pot = math.log(target) - over_rows(log_sum, high + jnp.log(total))
        for sweep in range(1, ITERS):
            row_pot = row_pot - jnp.log(over_cols(add, row_sums(row_pot, col_pot)))
            if sweep < ITERS - 1:
                mass = over_rows(add, col_sums(row_pot, col_pot))
                col_pot = col_pot + math.log(target) - jnp.log(mass)
        return jnp.concatenate([row_pot.reshape(-1, group_cols), col_pot[None]])

    def nothing():
        return jnp.zeros((2 * row_count // group_cols + 1, group_cols), jnp.float32)

    known = lax.cond(core == 1, rounds, nothing)
    got = swap(known, "row", 1)
    row_pot = jnp.where(core == 1, known[:-1].reshape(-1), reorder(got[:-1].reshape(-1), 2, 1))
    col_pot = jnp.where(core == 1, known[-1], reorder(got[-1], 2, 1))

    mass = col_sums(row_pot, col_pot)
    held = add(
        [
            lax.dot_general(
                jnp.exp(x[:, :half_cols] + col_pot[None, :half_cols]).astype(jnp.bfloat16),
                span_half,
                (((0,), (0,)), ((), ())),
                preferred_element_type=jnp.float32,
            )
            for x, span_half in zip(with_rows(row_pot), span_halves)
        ]
    ).reshape(chips, per, width)
    for at, size in stages("row"):
        me = digit("row", at, size)
        held = held.reshape((-1, size) + held.shape[1:])
        low = held.astype(jnp.bfloat16)
        note = in_thirds(mass, width)
        parts, masses = [lax.dynamic_index_in_dim(held, me, 1, keepdims=False)], [from_thirds(note, group_cols)]
        for d in range(1, size):
            block = lax.dynamic_index_in_dim(low, me ^ d, 1, keepdims=False).reshape(-1, width)
            got = swap(jnp.concatenate([block, note]), "row", d << at)
            if d << at == 2:
                row_out = after(row_pot[:row_count], got)
                row_out = jnp.concatenate(unxor_list(jnp.split(row_out, cols), me_col))
            parts.append(got[: block.shape[0]].astype(jnp.float32).reshape(parts[0].shape))
            masses.append(from_thirds(got[block.shape[0] :], group_cols))
        held, mass = add(parts), add(masses)
    own_mass = lax.dynamic_slice_in_dim(mass, me_row // 2 * per, per, 0)
    col_pots = (col_pot + math.log(target) - jnp.log(mass)).reshape(2, chips, per)
    col_pots = jnp.where(core == 1, col_pots[::-1], col_pots)
    return (
        (held.reshape(per, width) * (target * mass_ratio / own_mass)[:, None]).astype(jnp.bfloat16),
        row_out,
        col_pots.swapaxes(0, 1).reshape(-1),
    )


def solution(mesh):
    placed = (P(("row", "col"), None), P(("col", "row"), None), P("row", None))
    return jax.shard_map(
        per_device,
        mesh=mesh,
        in_specs=placed,
        out_specs=(P(("col", "row"), None), P("row"), P("col")),
        check_vma=False,
    )
```

```python
import math

import jax
import jax.numpy as jnp
from jax import lax
from jax.sharding import PartitionSpec as P

ITERS = 3


logit_scale = 0.0625
floor_value = -1e30


def swap(x, axis, k):
    return lax.ppermute(x, axis, [(i, i ^ k) for i in range(lax.axis_size(axis))])


def swap_by_core(x, axis, for_core):
    cols = lax.axis_size("col")
    scale = cols if axis == "row" else 1
    pairs = [(i, i ^ (for_core[i // cols & 1] * scale)) for i in range(lax.axis_size("row") * cols)]
    return lax.ppermute(x, ("row", "col"), pairs)


def stages(axis):
    low = 1 if axis == "row" else 0
    bits = (lax.axis_size(axis) - 1).bit_length()
    return [(at, 1 << min(2, bits - at)) for at in range(low, bits, 2)]


def digit(axis, at, size):
    return (lax.axis_index(axis) >> at) & (size - 1)


def gather_spans(x, core):
    parts = [x]
    ready = x
    for at, size in stages("col"):
        x = jnp.concatenate(parts)
        parts = [x] + [swap(x, "col", d << at) for d in range(1, min(size, 3))]
        near = parts
        if size == 4:
            passed_on = jnp.where(core == 1, parts[2], parts[1])
            near = lax.optimization_barrier((parts, passed_on))[0]
            ready = passed_on
            parts = parts + [swap_by_core(passed_on, "col", (2 << at, 1 << at))]
    mate = [swap(part, "row", 1) for part in near + parts[3:]]
    return parts, mate, ready


def after(x, other):
    return lax.optimization_barrier((x, other))[0]


def placed(parts, index):
    whole = jnp.zeros((len(parts),) + parts[0].shape, parts[0].dtype)
    for d, part in enumerate(parts):
        whole = lax.dynamic_update_index_in_dim(whole, part, index ^ d, 0)
    return whole.reshape((-1,) + parts[0].shape[1:])


def gather_centroids(x, first, ready):
    for at, size in stages("row"):
        sent = after(x, first)
        parts = [sent] + [after(swap(sent, "row", d << at), ready) for d in range(1, size)]
        mate = [swap(after(part, ready) if part is sent else part, "row", 1) for part in parts]
        position = digit("row", at, size)
        x = placed(parts, position)
    return jnp.concatenate([x, placed(mate, position)])


def reorder(x, blocks, k):
    x = x.reshape((blocks, -1) + x.shape[1:])
    return jnp.concatenate([x[p ^ k] for p in range(blocks)])


def unxor(x, index, blocks):
    shape = x.shape
    bit = 1
    while bit < blocks:
        pairs = x.reshape((blocks // (2 * bit), 2, -1) + shape[1:])
        x = jnp.where((index & bit) != 0, pairs[:, ::-1], pairs).reshape(shape)
        bit *= 2
    return x


def unxor_list(parts, index):
    bit = 1
    while bit < len(parts):
        parts = [jnp.where((index & bit) != 0, parts[p ^ bit], part) for p, part in enumerate(parts)]
        bit *= 2
    return parts


def tree(op, parts):
    while len(parts) > 1:
        parts = [op(parts[i], parts[i + 1]) for i in range(0, len(parts), 2)]
    return parts[0]


def add(parts):
    return tree(jnp.add, parts)


def log_sum(parts):
    high = tree(jnp.maximum, parts)
    return high + jnp.log(add([jnp.exp(part - high) for part in parts]))


def over_rows(merge, x):
    for at, size in stages("row"):
        x = merge([x] + [swap(x, "row", d << at) for d in range(1, size)])
    return x


def over_cols(merge, x):
    cols = lax.axis_size("col")
    for at, size in stages("col"):
        parts = [x]
        for d in range(1, size):
            halves = swap(x, "col", d << at).reshape(2, -1)
            parts.append(jnp.concatenate([reorder(half, cols, d << at) for half in halves]))
        x = merge(parts)
    return x


def in_thirds(x, width):
    thirds = []
    for step in range(3):
        top = lax.reduce_precision(x, 8, 7)
        thirds.append(top.astype(jnp.bfloat16))
        x = x - top
    return jnp.pad(jnp.stack(thirds), ((0, 5), (0, width - x.shape[0])))


def from_thirds(rows, count):
    thirds = rows[:3, :count].astype(jnp.float32)
    return thirds[0] + thirds[1] + thirds[2]


def per_device(spans, centroids, pattern):
    rows, cols = lax.axis_size("row"), lax.axis_size("col")
    chips = rows // 2
    me_row, me_col = lax.axis_index("row"), lax.axis_index("col")
    core = me_row % 2
    per, width = centroids.shape
    half_cols = per * chips
    group_cols = 2 * half_cols
    row_count = spans.shape[0] * cols
    mass_ratio = group_cols * cols / (row_count * rows)
    target = 1 / mass_ratio

    mate_pattern = swap(pattern, "row", 1)
    own_parts, mate_parts, ready = gather_spans(spans, core)
    tile_centroids = gather_centroids(centroids, mate_pattern, ready)
    own_parts = [after(own_parts[0], mate_pattern)] + own_parts[1:]
    span_halves = [jnp.concatenate(own_parts), jnp.concatenate(mate_parts)]
    at = jnp.arange(group_cols)
    row_of = at % half_cols // per * 2 + (at // half_cols ^ core)
    blocks = jnp.arange(group_cols // 128)
    in_block = ((row_of * per + at % per) // 128 == blocks[:, None]).astype(jnp.bfloat16)

    def half_scores(lists, span_half):
        listed = jnp.any(lists[:, :, None] == me_col * blocks.shape[0] + blocks, axis=1)
        listed = unxor(jnp.repeat(listed, 128 // spans.shape[0], axis=0).astype(jnp.bfloat16), me_col, cols)
        allowed_cells = jnp.dot(
            jnp.repeat(listed, spans.shape[0], axis=0), in_block, preferred_element_type=jnp.float32
        )
        products = lax.dot_general(
            span_half, tile_centroids, (((1,), (1,)), ((), ())), preferred_element_type=jnp.float32
        )
        return jnp.where(allowed_cells > 0.5, products * logit_scale, floor_value)

    scores = [half_scores(pattern, span_halves[0]), half_scores(mate_pattern, span_halves[1])]

    def with_rows(row_pot):
        return [half + row_pot[n * row_count : (n + 1) * row_count, None] for n, half in enumerate(scores)]

    def row_sums(row_pot, col_pot):
        return jnp.concatenate([jnp.sum(jnp.exp(x + col_pot[None, :]), axis=1) for x in with_rows(row_pot)])

    def col_sums(row_pot, col_pot):
        return add([jnp.sum(jnp.exp(x + col_pot[None, :]), axis=0) for x in with_rows(row_pot)])

    def rounds():
        highs = [jnp.max(half, axis=1) for half in scores]
        totals = [jnp.sum(jnp.exp(half - high[:, None]), axis=1) for half, high in zip(scores, highs)]
        row_pot = -over_cols(log_sum, jnp.concatenate([high + jnp.log(total) for high, total in zip(highs, totals)]))
        high = tree(jnp.maximum, [jnp.max(x, axis=0) for x in with_rows(row_pot)])
        total = col_sums(row_pot, -high)
        col_pot = math.log(target) - over_rows(log_sum, high + jnp.log(total))
        for sweep in range(1, ITERS):
            row_pot = row_pot - jnp.log(over_cols(add, row_sums(row_pot, col_pot)))
            if sweep < ITERS - 1:
                mass = over_rows(add, col_sums(row_pot, col_pot))
                col_pot = col_pot + math.log(target) - jnp.log(mass)
        return jnp.concatenate([row_pot.reshape(-1, group_cols), col_pot[None]])

    def nothing():
        return jnp.zeros((2 * row_count // group_cols + 1, group_cols), jnp.float32)

    known = lax.cond(core == 1, rounds, nothing)
    got = swap(known, "row", 1)
    row_pot = jnp.where(core == 1, known[:-1].reshape(-1), reorder(got[:-1].reshape(-1), 2, 1))
    col_pot = jnp.where(core == 1, known[-1], reorder(got[-1], 2, 1))

    mass = col_sums(row_pot, col_pot)
    held = add(
        [
            lax.dot_general(
                jnp.exp(x[:, :half_cols] + col_pot[None, :half_cols]).astype(jnp.bfloat16),
                span_half,
                (((0,), (0,)), ((), ())),
                preferred_element_type=jnp.float32,
            )
            for x, span_half in zip(with_rows(row_pot), span_halves)
        ]
    ).reshape(chips, per, width)
    for at, size in stages("row"):
        me = digit("row", at, size)
        held = held.reshape((-1, size) + held.shape[1:])
        low = held.astype(jnp.bfloat16)
        note = in_thirds(mass, width)
        parts, masses = [lax.dynamic_index_in_dim(held, me, 1, keepdims=False)], [from_thirds(note, group_cols)]
        for d in range(1, size):
            block = lax.dynamic_index_in_dim(low, me ^ d, 1, keepdims=False).reshape(-1, width)
            got = swap(jnp.concatenate([block, note]), "row", d << at)
            if d << at == 2:
                row_out = after(row_pot[:row_count], got)
                row_out = jnp.concatenate(unxor_list(jnp.split(row_out, cols), me_col))
            parts.append(got[: block.shape[0]].astype(jnp.float32).reshape(parts[0].shape))
            masses.append(from_thirds(got[block.shape[0] :], group_cols))
        held, mass = add(parts), add(masses)
    own_mass = lax.dynamic_slice_in_dim(mass, me_row // 2 * per, per, 0)
    col_pots = (col_pot + math.log(target) - jnp.log(mass)).reshape(2, chips, per)
    col_pots = jnp.where(core == 1, col_pots[::-1], col_pots)
    return (
        (held.reshape(per, width) * (target * mass_ratio / own_mass)[:, None]).astype(jnp.bfloat16),
        row_out,
        col_pots.swapaxes(0, 1).reshape(-1),
    )


def solution(mesh):
    placed = (P(("row", "col"), None), P(("col", "row"), None), P("row", None))
    return jax.shard_map(
        per_device,
        mesh=mesh,
        in_specs=placed,
        out_specs=(P(("col", "row"), None), P("row"), P("col")),
        check_vma=False,
    )
```

```python
import math

import jax
import jax.numpy as jnp
from jax import lax
from jax.sharding import PartitionSpec as P

ITERS = 3


logit_scale = 0.0625
floor_value = -1e30


def swap(x, axis, k):
    return lax.ppermute(x, axis, [(i, i ^ k) for i in range(lax.axis_size(axis))])


def swap_by_core(x, axis, for_core):
    cols = lax.axis_size("col")
    scale = cols if axis == "row" else 1
    pairs = [(i, i ^ (for_core[i // cols & 1] * scale)) for i in range(lax.axis_size("row") * cols)]
    return lax.ppermute(x, ("row", "col"), pairs)


def stages(axis):
    low = 1 if axis == "row" else 0
    bits = (lax.axis_size(axis) - 1).bit_length()
    return [(at, 1 << min(2, bits - at)) for at in range(low, bits, 2)]


def digit(axis, at, size):
    return (lax.axis_index(axis) >> at) & (size - 1)


def gather_spans(x, core):
    first = None
    parts = [x]
    ready = x
    for at, size in stages("col"):
        x = jnp.concatenate(parts)
        parts = [x] + [swap(x, "col", d << at) for d in range(1, min(size, 3))]
        first = parts[1] if first is None else first
        near = parts
        if size == 4:
            passed_on = jnp.where(core == 1, parts[2], parts[1])
            near = lax.optimization_barrier((parts, passed_on))[0]
            ready = passed_on
            parts = parts + [swap_by_core(passed_on, "col", (2 << at, 1 << at))]
    mate = [swap(part, "row", 1) for part in near + parts[3:]]
    return near[:1] + parts[1:], mate, first, ready


def after(x, other):
    return lax.optimization_barrier((x, other))[0]


def placed(parts, index):
    whole = jnp.zeros((len(parts),) + parts[0].shape, parts[0].dtype)
    for d, part in enumerate(parts):
        whole = lax.dynamic_update_index_in_dim(whole, part, index ^ d, 0)
    return whole.reshape((-1,) + parts[0].shape[1:])


def gather_centroids(x, ready):
    for at, size in stages("row"):
        sent = after(x, ready)
        parts = [sent] + [after(swap(x, "row", d << at), ready) for d in range(1, size)]
        mate = [swap(part, "row", 1) for part in parts]
        position = digit("row", at, size)
        x = placed(parts, position)
    return jnp.concatenate([x, placed(mate, position)])


def reorder(x, blocks, k):
    x = x.reshape((blocks, -1) + x.shape[1:])
    return jnp.concatenate([x[p ^ k] for p in range(blocks)])


def unxor(x, index, blocks):
    shape = x.shape
    bit = 1
    while bit < blocks:
        pairs = x.reshape((blocks // (2 * bit), 2, -1) + shape[1:])
        x = jnp.where((index & bit) != 0, pairs[:, ::-1], pairs).reshape(shape)
        bit *= 2
    return x


def unxor_list(parts, index):
    bit = 1
    while bit < len(parts):
        parts = [jnp.where((index & bit) != 0, parts[p ^ bit], part) for p, part in enumerate(parts)]
        bit *= 2
    return parts


def tree(op, parts):
    while len(parts) > 1:
        parts = [op(parts[i], parts[i + 1]) for i in range(0, len(parts), 2)]
    return parts[0]


def add(parts):
    return tree(jnp.add, parts)


def log_sum(parts):
    high = tree(jnp.maximum, parts)
    return high + jnp.log(add([jnp.exp(part - high) for part in parts]))


def over_rows(merge, x):
    for at, size in stages("row"):
        x = merge([x] + [swap(x, "row", d << at) for d in range(1, size)])
    return x


def over_cols(merge, x):
    cols = lax.axis_size("col")
    for at, size in stages("col"):
        parts = [x]
        for d in range(1, size):
            halves = swap(x, "col", d << at).reshape(2, -1)
            parts.append(jnp.concatenate([reorder(half, cols, d << at) for half in halves]))
        x = merge(parts)
    return x


def in_thirds(x, width):
    thirds = []
    for step in range(3):
        top = lax.reduce_precision(x, 8, 7)
        thirds.append(top.astype(jnp.bfloat16))
        x = x - top
    return jnp.pad(jnp.stack(thirds), ((0, 5), (0, width - x.shape[0])))


def from_thirds(rows, count):
    thirds = rows[:3, :count].astype(jnp.float32)
    return thirds[0] + thirds[1] + thirds[2]


def per_device(spans, centroids, pattern):
    rows, cols = lax.axis_size("row"), lax.axis_size("col")
    chips = rows // 2
    me_row, me_col = lax.axis_index("row"), lax.axis_index("col")
    core = me_row % 2
    per, width = centroids.shape
    half_cols = per * chips
    group_cols = 2 * half_cols
    row_count = spans.shape[0] * cols
    mass_ratio = group_cols * cols / (row_count * rows)
    target = 1 / mass_ratio

    own_parts, mate_parts, first, ready = gather_spans(spans, core)
    mate_pattern = swap(after(pattern, first), "row", 1)
    tile_centroids = gather_centroids(centroids, ready)
    span_halves = [jnp.concatenate(own_parts), jnp.concatenate(mate_parts)]
    at = jnp.arange(group_cols)
    row_of = at % half_cols // per * 2 + (at // half_cols ^ core)
    blocks = jnp.arange(group_cols // 128)
    in_block = ((row_of * per + at % per) // 128 == blocks[:, None]).astype(jnp.bfloat16)

    def half_scores(lists, span_half):
        listed = jnp.any(lists[:, :, None] == me_col * blocks.shape[0] + blocks, axis=1)
        listed = unxor(jnp.repeat(listed, 128 // spans.shape[0], axis=0).astype(jnp.bfloat16), me_col, cols)
        allowed_cells = jnp.dot(
            jnp.repeat(listed, spans.shape[0], axis=0), in_block, preferred_element_type=jnp.float32
        )
        products = lax.dot_general(
            span_half, tile_centroids, (((1,), (1,)), ((), ())), preferred_element_type=jnp.float32
        )
        return jnp.where(allowed_cells > 0.5, products * logit_scale, floor_value)

    scores = [half_scores(pattern, span_halves[0]), half_scores(mate_pattern, span_halves[1])]

    def with_rows(row_pot):
        return [half + row_pot[n * row_count : (n + 1) * row_count, None] for n, half in enumerate(scores)]

    def row_sums(row_pot, col_pot):
        return jnp.concatenate([jnp.sum(jnp.exp(x + col_pot[None, :]), axis=1) for x in with_rows(row_pot)])

    def col_sums(row_pot, col_pot):
        return add([jnp.sum(jnp.exp(x + col_pot[None, :]), axis=0) for x in with_rows(row_pot)])

    def rounds():
        highs = [jnp.max(half, axis=1) for half in scores]
        totals = [jnp.sum(jnp.exp(half - high[:, None]), axis=1) for half, high in zip(scores, highs)]
        row_pot = -over_cols(log_sum, jnp.concatenate([high + jnp.log(total) for high, total in zip(highs, totals)]))
        high = tree(jnp.maximum, [jnp.max(x, axis=0) for x in with_rows(row_pot)])
        total = col_sums(row_pot, -high)
        col_pot = math.log(target) - over_rows(log_sum, high + jnp.log(total))
        for sweep in range(1, ITERS):
            row_pot = row_pot - jnp.log(over_cols(add, row_sums(row_pot, col_pot)))
            if sweep < ITERS - 1:
                mass = over_rows(add, col_sums(row_pot, col_pot))
                col_pot = col_pot + math.log(target) - jnp.log(mass)
        return jnp.concatenate([row_pot.reshape(-1, group_cols), col_pot[None]])

    def nothing():
        return jnp.zeros((2 * row_count // group_cols + 1, group_cols), jnp.float32)

    known = lax.cond(core == 1, rounds, nothing)
    got = swap(known, "row", 1)
    row_pot = jnp.where(core == 1, known[:-1].reshape(-1), reorder(got[:-1].reshape(-1), 2, 1))
    col_pot = jnp.where(core == 1, known[-1], reorder(got[-1], 2, 1))

    halves = [
        lax.dot_general(
            jnp.exp(x[:, :half_cols] + col_pot[None, :half_cols]).astype(jnp.bfloat16),
            span_half,
            (((0,), (0,)), ((), ())),
            preferred_element_type=jnp.float32,
        )
        for x, span_half in zip(with_rows(row_pot), span_halves)
    ]
    mass = col_sums(after(row_pot, halves[1]), col_pot)
    held = add(halves).reshape(chips, per, width)
    for at, size in stages("row"):
        me = digit("row", at, size)
        held = held.reshape((-1, size) + held.shape[1:])
        low = held.astype(jnp.bfloat16)
        note = in_thirds(mass, width)
        parts, masses = [lax.dynamic_index_in_dim(held, me, 1, keepdims=False)], [from_thirds(note, group_cols)]
        for d in range(1, size):
            block = lax.dynamic_index_in_dim(low, me ^ d, 1, keepdims=False).reshape(-1, width)
            got = swap(jnp.concatenate([block, note]), "row", d << at)
            if d << at == 2:
                row_out = after(row_pot[:row_count], got)
                row_out = jnp.concatenate(unxor_list(jnp.split(row_out, cols), me_col))
            parts.append(got[: block.shape[0]].astype(jnp.float32).reshape(parts[0].shape))
            masses.append(from_thirds(got[block.shape[0] :], group_cols))
        held, mass = add(parts), add(masses)
    own_mass = lax.dynamic_slice_in_dim(mass, me_row // 2 * per, per, 0)
    col_pots = (col_pot + math.log(target) - jnp.log(mass)).reshape(2, chips, per)
    col_pots = jnp.where(core == 1, col_pots[::-1], col_pots)
    return (
        (held.reshape(per, width) * (target * mass_ratio / own_mass)[:, None]).astype(jnp.bfloat16),
        row_out,
        col_pots.swapaxes(0, 1).reshape(-1),
    )


def solution(mesh):
    placed = (P(("row", "col"), None), P(("col", "row"), None), P("row", None))
    return jax.shard_map(
        per_device,
        mesh=mesh,
        in_specs=placed,
        out_specs=(P(("col", "row"), None), P("row"), P("col")),
        check_vma=False,
    )
```

```python
import math

import jax
import jax.numpy as jnp
from jax import lax
from jax.sharding import PartitionSpec as P

ITERS = 3


logit_scale = 0.0625
floor_value = -1e30


def swap(x, axis, k):
    return lax.ppermute(x, axis, [(i, i ^ k) for i in range(lax.axis_size(axis))])


def swap_by_core(x, axis, for_core):
    cols = lax.axis_size("col")
    scale = cols if axis == "row" else 1
    pairs = [(i, i ^ (for_core[i // cols & 1] * scale)) for i in range(lax.axis_size("row") * cols)]
    return lax.ppermute(x, ("row", "col"), pairs)


def stages(axis):
    low = 1 if axis == "row" else 0
    bits = (lax.axis_size(axis) - 1).bit_length()
    return [(at, 1 << min(2, bits - at)) for at in range(low, bits, 2)]


def digit(axis, at, size):
    return (lax.axis_index(axis) >> at) & (size - 1)


def gather_spans(x, core):
    parts = [x]
    ready = x
    for at, size in stages("col"):
        x = jnp.concatenate(parts)
        parts = [x] + [swap(x, "col", d << at) for d in range(1, min(size, 3))]
        near = parts
        if size == 4:
            passed_on = jnp.where(core == 1, parts[2], parts[1])
            near = lax.optimization_barrier((parts, passed_on))[0]
            ready = passed_on
            parts = parts + [swap_by_core(passed_on, "col", (2 << at, 1 << at))]
    mate = [swap(part, "row", 1) for part in [jnp.concatenate(near)] + parts[3:]]
    return parts, mate, ready


def after(x, other):
    return lax.optimization_barrier((x, other))[0]


def placed(parts, index):
    whole = jnp.zeros((len(parts),) + parts[0].shape, parts[0].dtype)
    for d, part in enumerate(parts):
        whole = lax.dynamic_update_index_in_dim(whole, part, index ^ d, 0)
    return whole.reshape((-1,) + parts[0].shape[1:])


def gather_centroids(x, first, ready, arrived):
    for at, size in stages("row"):
        sent = after(x, first)
        parts = [sent] + [after(swap(sent, "row", d << at), ready) for d in range(1, size)]
        mate = [swap(after(part, ready if part is sent else arrived), "row", 1) for part in parts]
        position = digit("row", at, size)
        x = placed(parts, position)
    return jnp.concatenate([x, placed(mate, position)])


def reorder(x, blocks, k):
    x = x.reshape((blocks, -1) + x.shape[1:])
    return jnp.concatenate([x[p ^ k] for p in range(blocks)])


def unxor(x, index, blocks):
    shape = x.shape
    bit = 1
    while bit < blocks:
        pairs = x.reshape((blocks // (2 * bit), 2, -1) + shape[1:])
        x = jnp.where((index & bit) != 0, pairs[:, ::-1], pairs).reshape(shape)
        bit *= 2
    return x


def unxor_list(parts, index):
    bit = 1
    while bit < len(parts):
        parts = [jnp.where((index & bit) != 0, parts[p ^ bit], part) for p, part in enumerate(parts)]
        bit *= 2
    return parts


def tree(op, parts):
    while len(parts) > 1:
        parts = [op(parts[i], parts[i + 1]) for i in range(0, len(parts), 2)]
    return parts[0]


def add(parts):
    return tree(jnp.add, parts)


def log_sum(parts):
    high = tree(jnp.maximum, parts)
    return high + jnp.log(add([jnp.exp(part - high) for part in parts]))


def over_rows(merge, x):
    for at, size in stages("row"):
        x = merge([x] + [swap(x, "row", d << at) for d in range(1, size)])
    return x


def over_cols(merge, x):
    cols = lax.axis_size("col")
    for at, size in stages("col"):
        parts = [x]
        for d in range(1, size):
            halves = swap(x, "col", d << at).reshape(2, -1)
            parts.append(jnp.concatenate([reorder(half, cols, d << at) for half in halves]))
        x = merge(parts)
    return x


def in_thirds(x, width):
    thirds = []
    for step in range(3):
        top = lax.reduce_precision(x, 8, 7)
        thirds.append(top.astype(jnp.bfloat16))
        x = x - top
    return jnp.pad(jnp.stack(thirds), ((0, 5), (0, width - x.shape[0])))


def from_thirds(rows, count):
    thirds = rows[:3, :count].astype(jnp.float32)
    return thirds[0] + thirds[1] + thirds[2]


def per_device(spans, centroids, pattern):
    rows, cols = lax.axis_size("row"), lax.axis_size("col")
    chips = rows // 2
    me_row, me_col = lax.axis_index("row"), lax.axis_index("col")
    core = me_row % 2
    per, width = centroids.shape
    half_cols = per * chips
    group_cols = 2 * half_cols
    row_count = spans.shape[0] * cols
    mass_ratio = group_cols * cols / (row_count * rows)
    target = 1 / mass_ratio

    mate_pattern = swap(pattern, "row", 1)
    own_parts, mate_parts, ready = gather_spans(spans, core)
    tile_centroids = gather_centroids(centroids, mate_pattern, ready, mate_parts[0])
    own_parts = [after(own_parts[0], mate_pattern)] + own_parts[1:]
    span_halves = [jnp.concatenate(own_parts), jnp.concatenate(mate_parts)]
    at = jnp.arange(group_cols)
    row_of = at % half_cols // per * 2 + (at // half_cols ^ core)
    blocks = jnp.arange(group_cols // 128)
    in_block = ((row_of * per + at % per) // 128 == blocks[:, None]).astype(jnp.bfloat16)

    def half_scores(lists, span_half):
        listed = jnp.any(lists[:, :, None] == me_col * blocks.shape[0] + blocks, axis=1)
        listed = unxor(jnp.repeat(listed, 128 // spans.shape[0], axis=0).astype(jnp.bfloat16), me_col, cols)
        allowed_cells = jnp.dot(
            jnp.repeat(listed, spans.shape[0], axis=0), in_block, preferred_element_type=jnp.float32
        )
        products = lax.dot_general(
            span_half, tile_centroids, (((1,), (1,)), ((), ())), preferred_element_type=jnp.float32
        )
        return jnp.where(allowed_cells > 0.5, products * logit_scale, floor_value)

    scores = [half_scores(pattern, span_halves[0]), half_scores(mate_pattern, span_halves[1])]

    def with_rows(row_pot):
        return [half + row_pot[n * row_count : (n + 1) * row_count, None] for n, half in enumerate(scores)]

    def row_sums(row_pot, col_pot):
        return jnp.concatenate([jnp.sum(jnp.exp(x + col_pot[None, :]), axis=1) for x in with_rows(row_pot)])

    def col_sums(row_pot, col_pot):
        return add([jnp.sum(jnp.exp(x + col_pot[None, :]), axis=0) for x in with_rows(row_pot)])

    def rounds():
        highs = [jnp.max(half, axis=1) for half in scores]
        totals = [jnp.sum(jnp.exp(half - high[:, None]), axis=1) for half, high in zip(scores, highs)]
        row_pot = -over_cols(log_sum, jnp.concatenate([high + jnp.log(total) for high, total in zip(highs, totals)]))
        high = tree(jnp.maximum, [jnp.max(x, axis=0) for x in with_rows(row_pot)])
        total = col_sums(row_pot, -high)
        col_pot = math.log(target) - over_rows(log_sum, high + jnp.log(total))
        for sweep in range(1, ITERS):
            row_pot = row_pot - jnp.log(over_cols(add, row_sums(row_pot, col_pot)))
            if sweep < ITERS - 1:
                mass = over_rows(add, col_sums(row_pot, col_pot))
                col_pot = col_pot + math.log(target) - jnp.log(mass)
        return jnp.concatenate([row_pot.reshape(-1, group_cols), col_pot[None]])

    def nothing():
        return jnp.zeros((2 * row_count // group_cols + 1, group_cols), jnp.float32)

    known = lax.cond(core == 1, rounds, nothing)
    got = swap(known, "row", 1)
    row_pot = jnp.where(core == 1, known[:-1].reshape(-1), reorder(got[:-1].reshape(-1), 2, 1))
    col_pot = jnp.where(core == 1, known[-1], reorder(got[-1], 2, 1))

    mass = col_sums(row_pot, col_pot)
    held = add(
        [
            lax.dot_general(
                jnp.exp(x[:, :half_cols] + col_pot[None, :half_cols]).astype(jnp.bfloat16),
                span_half,
                (((0,), (0,)), ((), ())),
                preferred_element_type=jnp.float32,
            )
            for x, span_half in zip(with_rows(row_pot), span_halves)
        ]
    ).reshape(chips, per, width)
    for at, size in stages("row"):
        me = digit("row", at, size)
        held = held.reshape((-1, size) + held.shape[1:])
        low = held.astype(jnp.bfloat16)
        note = in_thirds(mass, width)
        parts, masses = [lax.dynamic_index_in_dim(held, me, 1, keepdims=False)], [from_thirds(note, group_cols)]
        for d in range(1, size):
            block = lax.dynamic_index_in_dim(low, me ^ d, 1, keepdims=False).reshape(-1, width)
            got = swap(jnp.concatenate([block, note]), "row", d << at)
            if d << at == 2:
                row_out = after(row_pot[:row_count], got)
                row_out = jnp.concatenate(unxor_list(jnp.split(row_out, cols), me_col))
            parts.append(got[: block.shape[0]].astype(jnp.float32).reshape(parts[0].shape))
            masses.append(from_thirds(got[block.shape[0] :], group_cols))
        held, mass = add(parts), add(masses)
    own_mass = lax.dynamic_slice_in_dim(mass, me_row // 2 * per, per, 0)
    col_pots = (col_pot + math.log(target) - jnp.log(mass)).reshape(2, chips, per)
    col_pots = jnp.where(core == 1, col_pots[::-1], col_pots)
    return (
        (held.reshape(per, width) * (target * mass_ratio / own_mass)[:, None]).astype(jnp.bfloat16),
        row_out,
        col_pots.swapaxes(0, 1).reshape(-1),
    )


def solution(mesh):
    placed = (P(("row", "col"), None), P(("col", "row"), None), P("row", None))
    return jax.shard_map(
        per_device,
        mesh=mesh,
        in_specs=placed,
        out_specs=(P(("col", "row"), None), P("row"), P("col")),
        check_vma=False,
    )
```

```python
import math

import jax
import jax.numpy as jnp
from jax import lax
from jax.sharding import PartitionSpec as P

ITERS = 3


logit_scale = 0.0625
floor_value = -1e30


def swap(x, axis, k):
    return lax.ppermute(x, axis, [(i, i ^ k) for i in range(lax.axis_size(axis))])


def swap_by_core(x, axis, for_core):
    cols = lax.axis_size("col")
    scale = cols if axis == "row" else 1
    pairs = [(i, i ^ (for_core[i // cols & 1] * scale)) for i in range(lax.axis_size("row") * cols)]
    return lax.ppermute(x, ("row", "col"), pairs)


def stages(axis):
    low = 1 if axis == "row" else 0
    bits = (lax.axis_size(axis) - 1).bit_length()
    return [(at, 1 << min(2, bits - at)) for at in range(low, bits, 2)]


def digit(axis, at, size):
    return (lax.axis_index(axis) >> at) & (size - 1)


def gather_spans(x, core):
    parts = [x]
    ready = x
    for at, size in stages("col"):
        x = jnp.concatenate(parts)
        parts = [x] + [swap(x, "col", d << at) for d in range(1, min(size, 3))]
        near = parts
        if size == 4:
            passed_on = jnp.where(core == 1, parts[2], parts[1])
            near = lax.optimization_barrier((parts, passed_on))[0]
            ready = passed_on
            parts = parts + [swap_by_core(passed_on, "col", (2 << at, 1 << at))]
    mate = [swap(part, "row", 1) for part in [jnp.concatenate(near)] + parts[3:]]
    return parts, mate, ready


def after(x, other):
    return lax.optimization_barrier((x, other))[0]


def placed(parts, index):
    whole = jnp.zeros((len(parts),) + parts[0].shape, parts[0].dtype)
    for d, part in enumerate(parts):
        whole = lax.dynamic_update_index_in_dim(whole, part, index ^ d, 0)
    return whole.reshape((-1,) + parts[0].shape[1:])


def gather_centroids(x, first, arrived):
    for at, size in stages("row"):
        sent = after(x, first)
        parts = [sent] + [swap(sent, "row", d << at) for d in range(1, size)]
        parts = [after(part, arrived) for part in parts]
        mate = [swap(part, "row", 1) for part in parts]
        position = digit("row", at, size)
        x = placed(parts, position)
    return jnp.concatenate([x, placed(mate, position)])


def reorder(x, blocks, k):
    x = x.reshape((blocks, -1) + x.shape[1:])
    return jnp.concatenate([x[p ^ k] for p in range(blocks)])


def unxor(x, index, blocks):
    shape = x.shape
    bit = 1
    while bit < blocks:
        pairs = x.reshape((blocks // (2 * bit), 2, -1) + shape[1:])
        x = jnp.where((index & bit) != 0, pairs[:, ::-1], pairs).reshape(shape)
        bit *= 2
    return x


def unxor_list(parts, index):
    bit = 1
    while bit < len(parts):
        parts = [jnp.where((index & bit) != 0, parts[p ^ bit], part) for p, part in enumerate(parts)]
        bit *= 2
    return parts


def tree(op, parts):
    while len(parts) > 1:
        parts = [op(parts[i], parts[i + 1]) for i in range(0, len(parts), 2)]
    return parts[0]


def add(parts):
    return tree(jnp.add, parts)


def log_sum(parts):
    high = tree(jnp.maximum, parts)
    return high + jnp.log(add([jnp.exp(part - high) for part in parts]))


def over_rows(merge, x):
    for at, size in stages("row"):
        x = merge([x] + [swap(x, "row", d << at) for d in range(1, size)])
    return x


def over_cols(merge, x):
    cols = lax.axis_size("col")
    for at, size in stages("col"):
        parts = [x]
        for d in range(1, size):
            halves = swap(x, "col", d << at).reshape(2, -1)
            parts.append(jnp.concatenate([reorder(half, cols, d << at) for half in halves]))
        x = merge(parts)
    return x


def in_thirds(x, width):
    thirds = []
    for step in range(3):
        top = lax.reduce_precision(x, 8, 7)
        thirds.append(top.astype(jnp.bfloat16))
        x = x - top
    return jnp.pad(jnp.stack(thirds), ((0, 5), (0, width - x.shape[0])))


def from_thirds(rows, count):
    thirds = rows[:3, :count].astype(jnp.float32)
    return thirds[0] + thirds[1] + thirds[2]


def per_device(spans, centroids, pattern):
    rows, cols = lax.axis_size("row"), lax.axis_size("col")
    chips = rows // 2
    me_row, me_col = lax.axis_index("row"), lax.axis_index("col")
    core = me_row % 2
    per, width = centroids.shape
    half_cols = per * chips
    group_cols = 2 * half_cols
    row_count = spans.shape[0] * cols
    mass_ratio = group_cols * cols / (row_count * rows)
    target = 1 / mass_ratio

    mate_pattern = swap(pattern, "row", 1)
    own_parts, mate_parts, ready = gather_spans(spans, core)
    tile_centroids = gather_centroids(centroids, mate_pattern, mate_parts[0])
    own_parts = [after(own_parts[0], mate_pattern)] + own_parts[1:]
    span_halves = [jnp.concatenate(own_parts), jnp.concatenate(mate_parts)]
    at = jnp.arange(group_cols)
    row_of = at % half_cols // per * 2 + (at // half_cols ^ core)
    blocks = jnp.arange(group_cols // 128)
    in_block = ((row_of * per + at % per) // 128 == blocks[:, None]).astype(jnp.bfloat16)

    def half_scores(lists, span_half):
        listed = jnp.any(lists[:, :, None] == me_col * blocks.shape[0] + blocks, axis=1)
        listed = unxor(jnp.repeat(listed, 128 // spans.shape[0], axis=0).astype(jnp.bfloat16), me_col, cols)
        allowed_cells = jnp.dot(
            jnp.repeat(listed, spans.shape[0], axis=0), in_block, preferred_element_type=jnp.float32
        )
        products = lax.dot_general(
            span_half, tile_centroids, (((1,), (1,)), ((), ())), preferred_element_type=jnp.float32
        )
        return jnp.where(allowed_cells > 0.5, products * logit_scale, floor_value)

    scores = [half_scores(pattern, span_halves[0]), half_scores(mate_pattern, span_halves[1])]

    def with_rows(row_pot):
        return [half + row_pot[n * row_count : (n + 1) * row_count, None] for n, half in enumerate(scores)]

    def row_sums(row_pot, col_pot):
        return jnp.concatenate([jnp.sum(jnp.exp(x + col_pot[None, :]), axis=1) for x in with_rows(row_pot)])

    def col_sums(row_pot, col_pot):
        return add([jnp.sum(jnp.exp(x + col_pot[None, :]), axis=0) for x in with_rows(row_pot)])

    def rounds():
        highs = [jnp.max(half, axis=1) for half in scores]
        totals = [jnp.sum(jnp.exp(half - high[:, None]), axis=1) for half, high in zip(scores, highs)]
        row_pot = -over_cols(log_sum, jnp.concatenate([high + jnp.log(total) for high, total in zip(highs, totals)]))
        high = tree(jnp.maximum, [jnp.max(x, axis=0) for x in with_rows(row_pot)])
        total = col_sums(row_pot, -high)
        col_pot = math.log(target) - over_rows(log_sum, high + jnp.log(total))
        for sweep in range(1, ITERS):
            row_pot = row_pot - jnp.log(over_cols(add, row_sums(row_pot, col_pot)))
            if sweep < ITERS - 1:
                mass = over_rows(add, col_sums(row_pot, col_pot))
                col_pot = col_pot + math.log(target) - jnp.log(mass)
        return jnp.concatenate([row_pot.reshape(-1, group_cols), col_pot[None]])

    def nothing():
        return jnp.zeros((2 * row_count // group_cols + 1, group_cols), jnp.float32)

    known = lax.cond(core == 1, rounds, nothing)
    got = swap(known, "row", 1)
    row_pot = jnp.where(core == 1, known[:-1].reshape(-1), reorder(got[:-1].reshape(-1), 2, 1))
    col_pot = jnp.where(core == 1, known[-1], reorder(got[-1], 2, 1))

    mass = col_sums(row_pot, col_pot)
    held = add(
        [
            lax.dot_general(
                jnp.exp(x[:, :half_cols] + col_pot[None, :half_cols]).astype(jnp.bfloat16),
                span_half,
                (((0,), (0,)), ((), ())),
                preferred_element_type=jnp.float32,
            )
            for x, span_half in zip(with_rows(row_pot), span_halves)
        ]
    ).reshape(chips, per, width)
    for at, size in stages("row"):
        me = digit("row", at, size)
        held = held.reshape((-1, size) + held.shape[1:])
        low = held.astype(jnp.bfloat16)
        note = in_thirds(mass, width)
        parts, masses = [lax.dynamic_index_in_dim(held, me, 1, keepdims=False)], [from_thirds(note, group_cols)]
        for d in range(1, size):
            block = lax.dynamic_index_in_dim(low, me ^ d, 1, keepdims=False).reshape(-1, width)
            got = swap(jnp.concatenate([block, note]), "row", d << at)
            if d << at == 2:
                row_out = after(row_pot[:row_count], got)
                row_out = jnp.concatenate(unxor_list(jnp.split(row_out, cols), me_col))
            parts.append(got[: block.shape[0]].astype(jnp.float32).reshape(parts[0].shape))
            masses.append(from_thirds(got[block.shape[0] :], group_cols))
        held, mass = add(parts), add(masses)
    own_mass = lax.dynamic_slice_in_dim(mass, me_row // 2 * per, per, 0)
    col_pots = (col_pot + math.log(target) - jnp.log(mass)).reshape(2, chips, per)
    col_pots = jnp.where(core == 1, col_pots[::-1], col_pots)
    return (
        (held.reshape(per, width) * (target * mass_ratio / own_mass)[:, None]).astype(jnp.bfloat16),
        row_out,
        col_pots.swapaxes(0, 1).reshape(-1),
    )


def solution(mesh):
    placed = (P(("row", "col"), None), P(("col", "row"), None), P("row", None))
    return jax.shard_map(
        per_device,
        mesh=mesh,
        in_specs=placed,
        out_specs=(P(("col", "row"), None), P("row"), P("col")),
        check_vma=False,
    )
```

```python
import math

import jax
import jax.numpy as jnp
from jax import lax
from jax.sharding import PartitionSpec as P

ITERS = 3


logit_scale = 0.0625
floor_value = -1e30


def swap(x, axis, k):
    return lax.ppermute(x, axis, [(i, i ^ k) for i in range(lax.axis_size(axis))])


def swap_by_core(x, axis, for_core):
    cols = lax.axis_size("col")
    scale = cols if axis == "row" else 1
    pairs = [(i, i ^ (for_core[i // cols & 1] * scale)) for i in range(lax.axis_size("row") * cols)]
    return lax.ppermute(x, ("row", "col"), pairs)


def stages(axis):
    low = 1 if axis == "row" else 0
    bits = (lax.axis_size(axis) - 1).bit_length()
    return [(at, 1 << min(2, bits - at)) for at in range(low, bits, 2)]


def digit(axis, at, size):
    return (lax.axis_index(axis) >> at) & (size - 1)


def gather_spans(x, core):
    parts = [x]
    ready = x
    for at, size in stages("col"):
        x = jnp.concatenate(parts)
        parts = [x] + [swap(x, "col", d << at) for d in range(1, min(size, 3))]
        near = parts
        if size == 4:
            passed_on = jnp.where(core == 1, parts[2], parts[1])
            near = lax.optimization_barrier((parts, passed_on))[0]
            ready = passed_on
            parts = parts + [swap_by_core(passed_on, "col", (2 << at, 1 << at))]
    mate = [swap(part, "row", 1) for part in [jnp.concatenate(near)] + parts[3:]]
    return parts, mate, ready


def after(x, other):
    return lax.optimization_barrier((x, other))[0]


def placed(parts, index):
    whole = jnp.zeros((len(parts),) + parts[0].shape, parts[0].dtype)
    for d, part in enumerate(parts):
        whole = lax.dynamic_update_index_in_dim(whole, part, index ^ d, 0)
    return whole.reshape((-1,) + parts[0].shape[1:])


def gather_centroids(x, first, arrived):
    for at, size in stages("row"):
        sent = after(x, first)
        parts = [sent] + [swap(sent, "row", d << at) for d in range(1, size)]
        parts = [after(part, arrived) for part in parts]
        mate = [swap(part, "row", 1) for part in parts]
        position = digit("row", at, size)
        x = placed(parts, position)
    return jnp.concatenate([x, placed(mate, position)])


def reorder(x, blocks, k):
    x = x.reshape((blocks, -1) + x.shape[1:])
    return jnp.concatenate([x[p ^ k] for p in range(blocks)])


def unxor(x, index, blocks):
    shape = x.shape
    bit = 1
    while bit < blocks:
        pairs = x.reshape((blocks // (2 * bit), 2, -1) + shape[1:])
        x = jnp.where((index & bit) != 0, pairs[:, ::-1], pairs).reshape(shape)
        bit *= 2
    return x


def unxor_list(parts, index):
    bit = 1
    while bit < len(parts):
        parts = [jnp.where((index & bit) != 0, parts[p ^ bit], part) for p, part in enumerate(parts)]
        bit *= 2
    return parts


def tree(op, parts):
    while len(parts) > 1:
        parts = [op(parts[i], parts[i + 1]) for i in range(0, len(parts), 2)]
    return parts[0]


def add(parts):
    return tree(jnp.add, parts)


def log_sum(parts):
    high = tree(jnp.maximum, parts)
    return high + jnp.log(add([jnp.exp(part - high) for part in parts]))


def over_rows(merge, x):
    for at, size in stages("row"):
        x = merge([x] + [swap(x, "row", d << at) for d in range(1, size)])
    return x


def over_cols(merge, x):
    cols = lax.axis_size("col")
    for at, size in stages("col"):
        parts = [x]
        for d in range(1, size):
            halves = swap(x, "col", d << at).reshape(2, -1)
            parts.append(jnp.concatenate([reorder(half, cols, d << at) for half in halves]))
        x = merge(parts)
    return x


def in_thirds(x, width):
    thirds = []
    for step in range(3):
        top = lax.reduce_precision(x, 8, 7)
        thirds.append(top.astype(jnp.bfloat16))
        x = x - top
    return jnp.pad(jnp.stack(thirds), ((0, 5), (0, width - x.shape[0])))


def from_thirds(rows, count):
    thirds = rows[:3, :count].astype(jnp.float32)
    return thirds[0] + thirds[1] + thirds[2]


def per_device(spans, centroids, pattern):
    rows, cols = lax.axis_size("row"), lax.axis_size("col")
    chips = rows // 2
    me_row, me_col = lax.axis_index("row"), lax.axis_index("col")
    core = me_row % 2
    per, width = centroids.shape
    half_cols = per * chips
    group_cols = 2 * half_cols
    row_count = spans.shape[0] * cols
    mass_ratio = group_cols * cols / (row_count * rows)
    target = 1 / mass_ratio

    mate_pattern = swap(pattern, "row", 1)
    own_parts, mate_parts, ready = gather_spans(spans, core)
    tile_centroids = gather_centroids(centroids, mate_pattern, mate_parts[0])
    own_parts = [after(own_parts[0], mate_parts[0])] + own_parts[1:]
    span_halves = [jnp.concatenate(own_parts), jnp.concatenate(mate_parts)]
    at = jnp.arange(group_cols)
    row_of = at % half_cols // per * 2 + (at // half_cols ^ core)
    blocks = jnp.arange(group_cols // 128)
    in_block = ((row_of * per + at % per) // 128 == blocks[:, None]).astype(jnp.bfloat16)

    def half_scores(lists, span_half):
        listed = jnp.any(lists[:, :, None] == me_col * blocks.shape[0] + blocks, axis=1)
        listed = unxor(jnp.repeat(listed, 128 // spans.shape[0], axis=0).astype(jnp.bfloat16), me_col, cols)
        allowed_cells = jnp.dot(
            jnp.repeat(listed, spans.shape[0], axis=0), in_block, preferred_element_type=jnp.float32
        )
        products = lax.dot_general(
            span_half, tile_centroids, (((1,), (1,)), ((), ())), preferred_element_type=jnp.float32
        )
        return jnp.where(allowed_cells > 0.5, products * logit_scale, floor_value)

    lists = [after(part, mate_parts[0]) for part in (pattern, mate_pattern)]
    scores = [half_scores(*pair) for pair in zip(lists, span_halves)]

    def with_rows(row_pot):
        return [half + row_pot[n * row_count : (n + 1) * row_count, None] for n, half in enumerate(scores)]

    def row_sums(row_pot, col_pot):
        return jnp.concatenate([jnp.sum(jnp.exp(x + col_pot[None, :]), axis=1) for x in with_rows(row_pot)])

    def col_sums(row_pot, col_pot):
        return add([jnp.sum(jnp.exp(x + col_pot[None, :]), axis=0) for x in with_rows(row_pot)])

    def rounds():
        highs = [jnp.max(half, axis=1) for half in scores]
        totals = [jnp.sum(jnp.exp(half - high[:, None]), axis=1) for half, high in zip(scores, highs)]
        row_pot = -over_cols(log_sum, jnp.concatenate([high + jnp.log(total) for high, total in zip(highs, totals)]))
        high = tree(jnp.maximum, [jnp.max(x, axis=0) for x in with_rows(row_pot)])
        total = col_sums(row_pot, -high)
        col_pot = math.log(target) - over_rows(log_sum, high + jnp.log(total))
        for sweep in range(1, ITERS):
            row_pot = row_pot - jnp.log(over_cols(add, row_sums(row_pot, col_pot)))
            if sweep < ITERS - 1:
                mass = over_rows(add, col_sums(row_pot, col_pot))
                col_pot = col_pot + math.log(target) - jnp.log(mass)
        return jnp.concatenate([row_pot.reshape(-1, group_cols), col_pot[None]])

    def nothing():
        return jnp.zeros((2 * row_count // group_cols + 1, group_cols), jnp.float32)

    known = lax.cond(core == 1, rounds, nothing)
    got = swap(known, "row", 1)
    row_pot = jnp.where(core == 1, known[:-1].reshape(-1), reorder(got[:-1].reshape(-1), 2, 1))
    col_pot = jnp.where(core == 1, known[-1], reorder(got[-1], 2, 1))

    mass = col_sums(row_pot, col_pot)
    held = add(
        [
            lax.dot_general(
                jnp.exp(x[:, :half_cols] + col_pot[None, :half_cols]).astype(jnp.bfloat16),
                span_half,
                (((0,), (0,)), ((), ())),
                preferred_element_type=jnp.float32,
            )
            for x, span_half in zip(with_rows(row_pot), span_halves)
        ]
    ).reshape(chips, per, width)
    for at, size in stages("row"):
        me = digit("row", at, size)
        held = held.reshape((-1, size) + held.shape[1:])
        low = held.astype(jnp.bfloat16)
        note = in_thirds(mass, width)
        parts, masses = [lax.dynamic_index_in_dim(held, me, 1, keepdims=False)], [from_thirds(note, group_cols)]
        for d in range(1, size):
            block = lax.dynamic_index_in_dim(low, me ^ d, 1, keepdims=False).reshape(-1, width)
            got = swap(jnp.concatenate([block, note]), "row", d << at)
            if d << at == 2:
                row_out = after(row_pot[:row_count], got)
                row_out = jnp.concatenate(unxor_list(jnp.split(row_out, cols), me_col))
            parts.append(got[: block.shape[0]].astype(jnp.float32).reshape(parts[0].shape))
            masses.append(from_thirds(got[block.shape[0] :], group_cols))
        held, mass = add(parts), add(masses)
    own_mass = lax.dynamic_slice_in_dim(mass, me_row // 2 * per, per, 0)
    col_pots = (col_pot + math.log(target) - jnp.log(mass)).reshape(2, chips, per)
    col_pots = jnp.where(core == 1, col_pots[::-1], col_pots)
    return (
        (held.reshape(per, width) * (target * mass_ratio / own_mass)[:, None]).astype(jnp.bfloat16),
        row_out,
        col_pots.swapaxes(0, 1).reshape(-1),
    )


def solution(mesh):
    placed = (P(("row", "col"), None), P(("col", "row"), None), P("row", None))
    return jax.shard_map(
        per_device,
        mesh=mesh,
        in_specs=placed,
        out_specs=(P(("col", "row"), None), P("row"), P("col")),
        check_vma=False,
    )
```

```python
import math

import jax
import jax.numpy as jnp
from jax import lax
from jax.sharding import PartitionSpec as P

ITERS = 3


logit_scale = 0.0625
floor_value = -1e30


def swap(x, axis, k):
    return lax.ppermute(x, axis, [(i, i ^ k) for i in range(lax.axis_size(axis))])


def swap_by_core(x, axis, for_core):
    cols = lax.axis_size("col")
    scale = cols if axis == "row" else 1
    pairs = [(i, i ^ (for_core[i // cols & 1] * scale)) for i in range(lax.axis_size("row") * cols)]
    return lax.ppermute(x, ("row", "col"), pairs)


def stages(axis):
    low = 1 if axis == "row" else 0
    bits = (lax.axis_size(axis) - 1).bit_length()
    return [(at, 1 << min(2, bits - at)) for at in range(low, bits, 2)]


def digit(axis, at, size):
    return (lax.axis_index(axis) >> at) & (size - 1)


def gather_spans(x, core):
    parts = [x]
    ready = x
    for at, size in stages("col"):
        x = jnp.concatenate(parts)
        parts = [x] + [swap(x, "col", d << at) for d in range(1, min(size, 3))]
        near = parts
        if size == 4:
            passed_on = jnp.where(core == 1, parts[2], parts[1])
            near = lax.optimization_barrier((parts, passed_on))[0]
            ready = passed_on
            parts = parts + [swap_by_core(passed_on, "col", (2 << at, 1 << at))]
    mate = [swap(part, "row", 1) for part in [jnp.concatenate(near)] + parts[3:]]
    return parts, mate, ready


def after(x, other):
    return lax.optimization_barrier((x, other))[0]


def placed(parts, index):
    whole = jnp.zeros((len(parts),) + parts[0].shape, parts[0].dtype)
    for d, part in enumerate(parts):
        whole = lax.dynamic_update_index_in_dim(whole, part, index ^ d, 0)
    return whole.reshape((-1,) + parts[0].shape[1:])


def gather_centroids(x, first, arrived):
    for at, size in stages("row"):
        sent = after(x, first)
        parts = [sent] + [swap(sent, "row", d << at) for d in range(1, size)]
        parts = [after(part, arrived) for part in parts]
        mate = [swap(part, "row", 1) for part in parts]
        position = digit("row", at, size)
        x = placed(parts, position)
    return jnp.concatenate([x, placed(mate, position)])


def reorder(x, blocks, k):
    x = x.reshape((blocks, -1) + x.shape[1:])
    return jnp.concatenate([x[p ^ k] for p in range(blocks)])


def unxor(x, index, blocks):
    shape = x.shape
    bit = 1
    while bit < blocks:
        pairs = x.reshape((blocks // (2 * bit), 2, -1) + shape[1:])
        x = jnp.where((index & bit) != 0, pairs[:, ::-1], pairs).reshape(shape)
        bit *= 2
    return x


def unxor_list(parts, index):
    bit = 1
    while bit < len(parts):
        parts = [jnp.where((index & bit) != 0, parts[p ^ bit], part) for p, part in enumerate(parts)]
        bit *= 2
    return parts


def tree(op, parts):
    while len(parts) > 1:
        parts = [op(parts[i], parts[i + 1]) for i in range(0, len(parts), 2)]
    return parts[0]


def add(parts):
    return tree(jnp.add, parts)


def log_sum(parts):
    high = tree(jnp.maximum, parts)
    return high + jnp.log(add([jnp.exp(part - high) for part in parts]))


def over_rows(merge, x):
    for at, size in stages("row"):
        x = merge([x] + [swap(x, "row", d << at) for d in range(1, size)])
    return x


def over_cols(merge, x):
    cols = lax.axis_size("col")
    for at, size in stages("col"):
        parts = [x]
        for d in range(1, size):
            halves = swap(x, "col", d << at).reshape(2, -1)
            parts.append(jnp.concatenate([reorder(half, cols, d << at) for half in halves]))
        x = merge(parts)
    return x


def in_thirds(x, width):
    thirds = []
    for step in range(3):
        top = lax.reduce_precision(x, 8, 7)
        thirds.append(top.astype(jnp.bfloat16))
        x = x - top
    return jnp.pad(jnp.stack(thirds), ((0, 5), (0, width - x.shape[0])))


def from_thirds(rows, count):
    thirds = rows[:3, :count].astype(jnp.float32)
    return thirds[0] + thirds[1] + thirds[2]


def per_device(spans, centroids, pattern):
    rows, cols = lax.axis_size("row"), lax.axis_size("col")
    chips = rows // 2
    me_row, me_col = lax.axis_index("row"), lax.axis_index("col")
    core = me_row % 2
    per, width = centroids.shape
    half_cols = per * chips
    group_cols = 2 * half_cols
    row_count = spans.shape[0] * cols
    mass_ratio = group_cols * cols / (row_count * rows)
    target = 1 / mass_ratio

    mate_pattern = swap(pattern, "row", 1)
    own_parts, mate_parts, ready = gather_spans(spans, core)
    tile_centroids = gather_centroids(centroids, mate_pattern, mate_parts[0])
    own_parts = [after(own_parts[0], mate_parts[0])] + own_parts[1:]
    span_halves = [jnp.concatenate(own_parts), jnp.concatenate(mate_parts)]
    at = jnp.arange(group_cols)
    row_of = at % half_cols // per * 2 + (at // half_cols ^ core)
    blocks = jnp.arange(group_cols // 128)
    in_block = ((row_of * per + at % per) // 128 == blocks[:, None]).astype(jnp.bfloat16)

    def half_scores(lists, span_half):
        listed = jnp.any(lists[:, :, None] == me_col * blocks.shape[0] + blocks, axis=1)
        listed = unxor(jnp.repeat(listed, 128 // spans.shape[0], axis=0).astype(jnp.bfloat16), me_col, cols)
        allowed_cells = jnp.dot(
            jnp.repeat(listed, spans.shape[0], axis=0), in_block, preferred_element_type=jnp.float32
        )
        products = lax.dot_general(
            span_half, tile_centroids, (((1,), (1,)), ((), ())), preferred_element_type=jnp.float32
        )
        return jnp.where(allowed_cells > 0.5, products * logit_scale, floor_value)

    scores = [half_scores(pattern, span_halves[0]), half_scores(mate_pattern, span_halves[1])]

    def with_rows(row_pot):
        return [half + row_pot[n * row_count : (n + 1) * row_count, None] for n, half in enumerate(scores)]

    def row_sums(row_pot, col_pot):
        return jnp.concatenate([jnp.sum(jnp.exp(x + col_pot[None, :]), axis=1) for x in with_rows(row_pot)])

    def col_sums(row_pot, col_pot):
        return add([jnp.sum(jnp.exp(x + col_pot[None, :]), axis=0) for x in with_rows(row_pot)])

    def rounds():
        highs = [jnp.max(half, axis=1) for half in scores]
        totals = [jnp.sum(jnp.exp(half - high[:, None]), axis=1) for half, high in zip(scores, highs)]
        row_pot = -over_cols(log_sum, jnp.concatenate([high + jnp.log(total) for high, total in zip(highs, totals)]))
        high = tree(jnp.maximum, [jnp.max(x, axis=0) for x in with_rows(row_pot)])
        total = col_sums(row_pot, -high)
        col_pot = math.log(target) - over_rows(log_sum, high + jnp.log(total))
        for sweep in range(1, ITERS):
            row_pot = row_pot - jnp.log(over_cols(add, row_sums(row_pot, col_pot)))
            if sweep < ITERS - 1:
                mass = over_rows(add, col_sums(row_pot, col_pot))
                col_pot = col_pot + math.log(target) - jnp.log(mass)
        return jnp.concatenate([row_pot.reshape(-1, group_cols), col_pot[None]])

    def nothing():
        return jnp.zeros((2 * row_count // group_cols + 1, group_cols), jnp.float32)

    known = lax.cond(core == 1, rounds, nothing)
    got = swap(known, "row", 1)
    row_pot = jnp.where(core == 1, known[:-1].reshape(-1), reorder(got[:-1].reshape(-1), 2, 1))
    col_pot = jnp.where(core == 1, known[-1], reorder(got[-1], 2, 1))

    mass = col_sums(row_pot, col_pot)
    held = add(
        [
            lax.dot_general(
                jnp.exp(x[:, :half_cols] + col_pot[None, :half_cols]).astype(jnp.bfloat16),
                span_half,
                (((0,), (0,)), ((), ())),
                preferred_element_type=jnp.float32,
            )
            for x, span_half in zip(with_rows(row_pot), span_halves)
        ]
    ).reshape(chips, per, width)
    for at, size in stages("row"):
        me = digit("row", at, size)
        held = held.reshape((-1, size) + held.shape[1:])
        low = held.astype(jnp.bfloat16)
        note = in_thirds(mass, width)
        parts, masses = [lax.dynamic_index_in_dim(held, me, 1, keepdims=False)], [from_thirds(note, group_cols)]
        for d in range(1, size):
            block = lax.dynamic_index_in_dim(low, me ^ d, 1, keepdims=False).reshape(-1, width)
            got = swap(jnp.concatenate([block, note]), "row", d << at)
            if d << at == 2:
                row_out = after(row_pot[:row_count], got)
                row_out = jnp.concatenate(unxor_list(jnp.split(row_out, cols), me_col))
            parts.append(got[: block.shape[0]].astype(jnp.float32).reshape(parts[0].shape))
            masses.append(from_thirds(got[block.shape[0] :], group_cols))
        held, mass = add(parts), add(masses)
    own_mass = lax.dynamic_slice_in_dim(mass, me_row // 2 * per, per, 0)
    col_pots = (col_pot + math.log(target) - jnp.log(mass)).reshape(2, chips, per)
    col_pots = jnp.where(core == 1, col_pots[::-1], col_pots)
    return (
        (held.reshape(per, width) * (target * mass_ratio / own_mass)[:, None]).astype(jnp.bfloat16),
        row_out,
        col_pots.swapaxes(0, 1).reshape(-1),
    )


def solution(mesh):
    placed = (P(("row", "col"), None), P(("col", "row"), None), P("row", None))
    return jax.shard_map(
        per_device,
        mesh=mesh,
        in_specs=placed,
        out_specs=(P(("col", "row"), None), P("row"), P("col")),
        check_vma=False,
    )
```

```python
import math

import jax
import jax.numpy as jnp
from jax import lax
from jax.sharding import PartitionSpec as P

ITERS = 3


logit_scale = 0.0625
floor_value = -1e30


def swap(x, axis, k):
    return lax.ppermute(x, axis, [(i, i ^ k) for i in range(lax.axis_size(axis))])


def swap_by_core(x, axis, for_core):
    cols = lax.axis_size("col")
    scale = cols if axis == "row" else 1
    pairs = [(i, i ^ (for_core[i // cols & 1] * scale)) for i in range(lax.axis_size("row") * cols)]
    return lax.ppermute(x, ("row", "col"), pairs)


def stages(axis):
    low = 1 if axis == "row" else 0
    bits = (lax.axis_size(axis) - 1).bit_length()
    return [(at, 1 << min(2, bits - at)) for at in range(low, bits, 2)]


def digit(axis, at, size):
    return (lax.axis_index(axis) >> at) & (size - 1)


def gather_spans(x, core):
    parts = [x]
    ready = x
    for at, size in stages("col"):
        x = jnp.concatenate(parts)
        parts = [x] + [swap(x, "col", d << at) for d in range(1, min(size, 3))]
        near = parts
        if size == 4:
            passed_on = jnp.where(core == 1, parts[2], parts[1])
            near = lax.optimization_barrier((parts, passed_on))[0]
            ready = passed_on
            parts = parts + [swap_by_core(passed_on, "col", (2 << at, 1 << at))]
    mate = [swap(part, "row", 1) for part in [jnp.concatenate(near)] + parts[3:]]
    return parts, mate, ready


def after(x, other):
    return lax.optimization_barrier((x, other))[0]


def placed(parts, index):
    whole = jnp.zeros((len(parts),) + parts[0].shape, parts[0].dtype)
    for d, part in enumerate(parts):
        whole = lax.dynamic_update_index_in_dim(whole, part, index ^ d, 0)
    return whole.reshape((-1,) + parts[0].shape[1:])


def gather_centroids(x, first, arrived):
    for at, size in stages("row"):
        sent = after(x, first)
        parts = [sent] + [swap(sent, "row", d << at) for d in range(1, size)]
        parts = [after(part, arrived) for part in parts]
        mate = [swap(part, "row", 1) for part in parts]
        position = digit("row", at, size)
        x = placed(parts, position)
    return jnp.concatenate([x, placed(mate, position)])


def reorder(x, blocks, k):
    x = x.reshape((blocks, -1) + x.shape[1:])
    return jnp.concatenate([x[p ^ k] for p in range(blocks)])


def unxor(x, index, blocks):
    shape = x.shape
    bit = 1
    while bit < blocks:
        pairs = x.reshape((blocks // (2 * bit), 2, -1) + shape[1:])
        x = jnp.where((index & bit) != 0, pairs[:, ::-1], pairs).reshape(shape)
        bit *= 2
    return x


def unxor_list(parts, index):
    bit = 1
    while bit < len(parts):
        parts = [jnp.where((index & bit) != 0, parts[p ^ bit], part) for p, part in enumerate(parts)]
        bit *= 2
    return parts


def tree(op, parts):
    while len(parts) > 1:
        parts = [op(parts[i], parts[i + 1]) for i in range(0, len(parts), 2)]
    return parts[0]


def add(parts):
    return tree(jnp.add, parts)


def log_sum(parts):
    high = tree(jnp.maximum, parts)
    return high + jnp.log(add([jnp.exp(part - high) for part in parts]))


def over_rows(merge, x):
    for at, size in stages("row"):
        x = merge([x] + [swap(x, "row", d << at) for d in range(1, size)])
    return x


def over_cols(merge, x):
    cols = lax.axis_size("col")
    for at, size in stages("col"):
        parts = [x]
        for d in range(1, size):
            halves = swap(x, "col", d << at).reshape(2, -1)
            parts.append(jnp.concatenate([reorder(half, cols, d << at) for half in halves]))
        x = merge(parts)
    return x


def in_thirds(x, width):
    thirds = []
    for step in range(3):
        top = lax.reduce_precision(x, 8, 7)
        thirds.append(top.astype(jnp.bfloat16))
        x = x - top
    return jnp.pad(jnp.stack(thirds), ((0, 5), (0, width - x.shape[0])))


def from_thirds(rows, count):
    thirds = rows[:3, :count].astype(jnp.float32)
    return thirds[0] + thirds[1] + thirds[2]


def per_device(spans, centroids, pattern):
    rows, cols = lax.axis_size("row"), lax.axis_size("col")
    chips = rows // 2
    me_row, me_col = lax.axis_index("row"), lax.axis_index("col")
    core = me_row % 2
    per, width = centroids.shape
    half_cols = per * chips
    group_cols = 2 * half_cols
    row_count = spans.shape[0] * cols
    mass_ratio = group_cols * cols / (row_count * rows)
    target = 1 / mass_ratio

    mate_pattern = swap(pattern, "row", 1)
    own_parts, mate_parts, ready = gather_spans(spans, core)
    tile_centroids = gather_centroids(centroids, mate_pattern, mate_parts[0])
    own_parts = [after(own_parts[0], mate_parts[0])] + own_parts[1:]
    span_halves = [jnp.concatenate(own_parts), jnp.concatenate(mate_parts)]
    at = jnp.arange(group_cols)
    row_of = at % half_cols // per * 2 + (at // half_cols ^ core)
    blocks = jnp.arange(group_cols // 128)
    in_block = ((row_of * per + at % per) // 128 == blocks[:, None]).astype(jnp.bfloat16)

    def half_scores(lists, span_half):
        listed = jnp.any(lists[:, :, None] == me_col * blocks.shape[0] + blocks, axis=1)
        listed = unxor(jnp.repeat(listed, 128 // spans.shape[0], axis=0).astype(jnp.bfloat16), me_col, cols)
        allowed_cells = jnp.dot(
            jnp.repeat(listed, spans.shape[0], axis=0), in_block, preferred_element_type=jnp.float32
        )
        products = lax.dot_general(
            span_half, tile_centroids, (((1,), (1,)), ((), ())), preferred_element_type=jnp.float32
        )
        return jnp.where(allowed_cells > 0.5, products * logit_scale, floor_value)

    scores = [half_scores(pattern, span_halves[0]), half_scores(mate_pattern, span_halves[1])]

    def with_rows(row_pot):
        return [half + row_pot[n * row_count : (n + 1) * row_count, None] for n, half in enumerate(scores)]

    def row_sums(row_pot, col_pot):
        return jnp.concatenate([jnp.sum(jnp.exp(x + col_pot[None, :]), axis=1) for x in with_rows(row_pot)])

    def col_sums(row_pot, col_pot):
        return add([jnp.sum(jnp.exp(x + col_pot[None, :]), axis=0) for x in with_rows(row_pot)])

    def rounds():
        highs = [jnp.max(half, axis=1) for half in scores]
        totals = [jnp.sum(jnp.exp(half - high[:, None]), axis=1) for half, high in zip(scores, highs)]
        row_pot = -over_cols(log_sum, jnp.concatenate([high + jnp.log(total) for high, total in zip(highs, totals)]))
        high = tree(jnp.maximum, [jnp.max(x, axis=0) for x in with_rows(row_pot)])
        total = col_sums(row_pot, -high)
        col_pot = math.log(target) - over_rows(log_sum, high + jnp.log(total))
        for sweep in range(1, ITERS):
            row_pot = row_pot - jnp.log(over_cols(add, row_sums(row_pot, col_pot)))
            if sweep < ITERS - 1:
                mass = over_rows(add, col_sums(row_pot, col_pot))
                col_pot = col_pot + math.log(target) - jnp.log(mass)
        return jnp.concatenate([row_pot.reshape(-1, group_cols), col_pot[None]])

    def nothing():
        return jnp.zeros((2 * row_count // group_cols + 1, group_cols), jnp.float32)

    known = lax.cond(core == 1, rounds, nothing)
    got = swap(known, "row", 1)
    row_pot = jnp.where(core == 1, known[:-1].reshape(-1), reorder(got[:-1].reshape(-1), 2, 1))
    col_pot = jnp.where(core == 1, known[-1], reorder(got[-1], 2, 1))

    mass = col_sums(row_pot, col_pot)
    held = add(
        [
            lax.dot_general(
                jnp.exp(x[:, :half_cols] + col_pot[None, :half_cols]).astype(jnp.bfloat16),
                span_half,
                (((0,), (0,)), ((), ())),
                preferred_element_type=jnp.float32,
            )
            for x, span_half in zip(with_rows(row_pot), span_halves)
        ]
    ).reshape(chips, per, width)
    for at, size in stages("row"):
        me = digit("row", at, size)
        held = held.reshape((-1, size) + held.shape[1:])
        low = held.astype(jnp.bfloat16)
        note = in_thirds(mass, width)
        parts, masses = [lax.dynamic_index_in_dim(held, me, 1, keepdims=False)], [from_thirds(note, group_cols)]
        for d in range(1, size):
            block = lax.dynamic_index_in_dim(low, me ^ d, 1, keepdims=False).reshape(-1, width)
            message = jnp.concatenate([block, note])
            if at == 1 and d == size - 1:
                row_out = after(row_pot[:row_count], low)
                row_out = jnp.concatenate(unxor_list(jnp.split(row_out, cols), me_col))
                message, row_out = lax.optimization_barrier((message, row_out))
            got = swap(message, "row", d << at)
            parts.append(got[: block.shape[0]].astype(jnp.float32).reshape(parts[0].shape))
            masses.append(from_thirds(got[block.shape[0] :], group_cols))
        held, mass = add(parts), add(masses)
    own_mass = lax.dynamic_slice_in_dim(mass, me_row // 2 * per, per, 0)
    col_pots = (col_pot + math.log(target) - jnp.log(mass)).reshape(2, chips, per)
    col_pots = jnp.where(core == 1, col_pots[::-1], col_pots)
    return (
        (held.reshape(per, width) * (target * mass_ratio / own_mass)[:, None]).astype(jnp.bfloat16),
        row_out,
        col_pots.swapaxes(0, 1).reshape(-1),
    )


def solution(mesh):
    placed = (P(("row", "col"), None), P(("col", "row"), None), P("row", None))
    return jax.shard_map(
        per_device,
        mesh=mesh,
        in_specs=placed,
        out_specs=(P(("col", "row"), None), P("row"), P("col")),
        check_vma=False,
    )
```

```python
import math

import jax
import jax.numpy as jnp
from jax import lax
from jax.sharding import PartitionSpec as P

ITERS = 3


logit_scale = 0.0625
floor_value = -1e30


def swap(x, axis, k):
    return lax.ppermute(x, axis, [(i, i ^ k) for i in range(lax.axis_size(axis))])


def swap_by_core(x, axis, for_core):
    cols = lax.axis_size("col")
    scale = cols if axis == "row" else 1
    pairs = [(i, i ^ (for_core[i // cols & 1] * scale)) for i in range(lax.axis_size("row") * cols)]
    return lax.ppermute(x, ("row", "col"), pairs)


def stages(axis):
    low = 1 if axis == "row" else 0
    bits = (lax.axis_size(axis) - 1).bit_length()
    return [(at, 1 << min(2, bits - at)) for at in range(low, bits, 2)]


def digit(axis, at, size):
    return (lax.axis_index(axis) >> at) & (size - 1)


def gather_spans(x, core):
    parts = [x]
    ready = x
    for at, size in stages("col"):
        x = jnp.concatenate(parts)
        parts = [x] + [swap(x, "col", d << at) for d in range(1, min(size, 3))]
        near = parts
        if size == 4:
            passed_on = jnp.where(core == 1, parts[2], parts[1])
            near = lax.optimization_barrier((parts, passed_on))[0]
            ready = passed_on
            parts = parts + [swap_by_core(passed_on, "col", (2 << at, 1 << at))]
    got = swap(jnp.concatenate(near[1:]), "row", 1)
    mate = [swap(after(near[0], got), "row", 1), got] + [swap(part, "row", 1) for part in parts[3:]]
    return parts, mate, ready


def after(x, other):
    return lax.optimization_barrier((x, other))[0]


def placed(parts, index):
    whole = jnp.zeros((len(parts),) + parts[0].shape, parts[0].dtype)
    for d, part in enumerate(parts):
        whole = lax.dynamic_update_index_in_dim(whole, part, index ^ d, 0)
    return whole.reshape((-1,) + parts[0].shape[1:])


def gather_centroids(x, first, arrived):
    for at, size in stages("row"):
        sent = after(x, first)
        parts = [sent] + [swap(sent, "row", d << at) for d in range(1, size)]
        parts = [after(part, arrived) for part in parts]
        mate = [swap(part, "row", 1) for part in parts]
        position = digit("row", at, size)
        x = placed(parts, position)
    return jnp.concatenate([x, placed(mate, position)])


def reorder(x, blocks, k):
    x = x.reshape((blocks, -1) + x.shape[1:])
    return jnp.concatenate([x[p ^ k] for p in range(blocks)])


def unxor(x, index, blocks):
    shape = x.shape
    bit = 1
    while bit < blocks:
        pairs = x.reshape((blocks // (2 * bit), 2, -1) + shape[1:])
        x = jnp.where((index & bit) != 0, pairs[:, ::-1], pairs).reshape(shape)
        bit *= 2
    return x


def unxor_list(parts, index):
    bit = 1
    while bit < len(parts):
        parts = [jnp.where((index & bit) != 0, parts[p ^ bit], part) for p, part in enumerate(parts)]
        bit *= 2
    return parts


def tree(op, parts):
    while len(parts) > 1:
        parts = [op(parts[i], parts[i + 1]) for i in range(0, len(parts), 2)]
    return parts[0]


def add(parts):
    return tree(jnp.add, parts)


def log_sum(parts):
    high = tree(jnp.maximum, parts)
    return high + jnp.log(add([jnp.exp(part - high) for part in parts]))


def over_rows(merge, x):
    for at, size in stages("row"):
        x = merge([x] + [swap(x, "row", d << at) for d in range(1, size)])
    return x


def over_cols(merge, x):
    cols = lax.axis_size("col")
    for at, size in stages("col"):
        parts = [x]
        for d in range(1, size):
            halves = swap(x, "col", d << at).reshape(2, -1)
            parts.append(jnp.concatenate([reorder(half, cols, d << at) for half in halves]))
        x = merge(parts)
    return x


def in_thirds(x, width):
    thirds = []
    for step in range(3):
        top = lax.reduce_precision(x, 8, 7)
        thirds.append(top.astype(jnp.bfloat16))
        x = x - top
    return jnp.pad(jnp.stack(thirds), ((0, 5), (0, width - x.shape[0])))


def from_thirds(rows, count):
    thirds = rows[:3, :count].astype(jnp.float32)
    return thirds[0] + thirds[1] + thirds[2]


def per_device(spans, centroids, pattern):
    rows, cols = lax.axis_size("row"), lax.axis_size("col")
    chips = rows // 2
    me_row, me_col = lax.axis_index("row"), lax.axis_index("col")
    core = me_row % 2
    per, width = centroids.shape
    half_cols = per * chips
    group_cols = 2 * half_cols
    row_count = spans.shape[0] * cols
    mass_ratio = group_cols * cols / (row_count * rows)
    target = 1 / mass_ratio

    mate_pattern = swap(pattern, "row", 1)
    own_parts, mate_parts, ready = gather_spans(spans, core)
    tile_centroids = gather_centroids(centroids, mate_pattern, mate_parts[1])
    own_parts = [after(own_parts[0], mate_parts[1])] + own_parts[1:]
    span_halves = [jnp.concatenate(own_parts), jnp.concatenate(mate_parts)]
    at = jnp.arange(group_cols)
    row_of = at % half_cols // per * 2 + (at // half_cols ^ core)
    blocks = jnp.arange(group_cols // 128)
    in_block = ((row_of * per + at % per) // 128 == blocks[:, None]).astype(jnp.bfloat16)

    def half_scores(lists, span_half):
        listed = jnp.any(lists[:, :, None] == me_col * blocks.shape[0] + blocks, axis=1)
        listed = unxor(jnp.repeat(listed, 128 // spans.shape[0], axis=0).astype(jnp.bfloat16), me_col, cols)
        allowed_cells = jnp.dot(
            jnp.repeat(listed, spans.shape[0], axis=0), in_block, preferred_element_type=jnp.float32
        )
        products = lax.dot_general(
            span_half, tile_centroids, (((1,), (1,)), ((), ())), preferred_element_type=jnp.float32
        )
        return jnp.where(allowed_cells > 0.5, products * logit_scale, floor_value)

    scores = [half_scores(pattern, span_halves[0]), half_scores(mate_pattern, span_halves[1])]

    def with_rows(row_pot):
        return [half + row_pot[n * row_count : (n + 1) * row_count, None] for n, half in enumerate(scores)]

    def row_sums(row_pot, col_pot):
        return jnp.concatenate([jnp.sum(jnp.exp(x + col_pot[None, :]), axis=1) for x in with_rows(row_pot)])

    def col_sums(row_pot, col_pot):
        return add([jnp.sum(jnp.exp(x + col_pot[None, :]), axis=0) for x in with_rows(row_pot)])

    def rounds():
        highs = [jnp.max(half, axis=1) for half in scores]
        totals = [jnp.sum(jnp.exp(half - high[:, None]), axis=1) for half, high in zip(scores, highs)]
        row_pot = -over_cols(log_sum, jnp.concatenate([high + jnp.log(total) for high, total in zip(highs, totals)]))
        high = tree(jnp.maximum, [jnp.max(x, axis=0) for x in with_rows(row_pot)])
        total = col_sums(row_pot, -high)
        col_pot = math.log(target) - over_rows(log_sum, high + jnp.log(total))
        for sweep in range(1, ITERS):
            row_pot = row_pot - jnp.log(over_cols(add, row_sums(row_pot, col_pot)))
            if sweep < ITERS - 1:
                mass = over_rows(add, col_sums(row_pot, col_pot))
                col_pot = col_pot + math.log(target) - jnp.log(mass)
        return jnp.concatenate([row_pot.reshape(-1, group_cols), col_pot[None]])

    def nothing():
        return jnp.zeros((2 * row_count // group_cols + 1, group_cols), jnp.float32)

    known = lax.cond(core == 1, rounds, nothing)
    got = swap(known, "row", 1)
    row_pot = jnp.where(core == 1, known[:-1].reshape(-1), reorder(got[:-1].reshape(-1), 2, 1))
    col_pot = jnp.where(core == 1, known[-1], reorder(got[-1], 2, 1))

    mass = col_sums(row_pot, col_pot)
    held = add(
        [
            lax.dot_general(
                jnp.exp(x[:, :half_cols] + col_pot[None, :half_cols]).astype(jnp.bfloat16),
                span_half,
                (((0,), (0,)), ((), ())),
                preferred_element_type=jnp.float32,
            )
            for x, span_half in zip(with_rows(row_pot), span_halves)
        ]
    ).reshape(chips, per, width)
    for at, size in stages("row"):
        me = digit("row", at, size)
        held = held.reshape((-1, size) + held.shape[1:])
        low = held.astype(jnp.bfloat16)
        note = in_thirds(mass, width)
        parts, masses = [lax.dynamic_index_in_dim(held, me, 1, keepdims=False)], [from_thirds(note, group_cols)]
        for d in range(1, size):
            block = lax.dynamic_index_in_dim(low, me ^ d, 1, keepdims=False).reshape(-1, width)
            got = swap(jnp.concatenate([block, note]), "row", d << at)
            if d << at == 2:
                row_out = after(row_pot[:row_count], got)
                row_out = jnp.concatenate(unxor_list(jnp.split(row_out, cols), me_col))
            parts.append(got[: block.shape[0]].astype(jnp.float32).reshape(parts[0].shape))
            masses.append(from_thirds(got[block.shape[0] :], group_cols))
        held, mass = add(parts), add(masses)
    own_mass = lax.dynamic_slice_in_dim(mass, me_row // 2 * per, per, 0)
    col_pots = (col_pot + math.log(target) - jnp.log(mass)).reshape(2, chips, per)
    col_pots = jnp.where(core == 1, col_pots[::-1], col_pots)
    return (
        (held.reshape(per, width) * (target * mass_ratio / own_mass)[:, None]).astype(jnp.bfloat16),
        row_out,
        col_pots.swapaxes(0, 1).reshape(-1),
    )


def solution(mesh):
    placed = (P(("row", "col"), None), P(("col", "row"), None), P("row", None))
    return jax.shard_map(
        per_device,
        mesh=mesh,
        in_specs=placed,
        out_specs=(P(("col", "row"), None), P("row"), P("col")),
        check_vma=False,
    )
```

```python
import math

import jax
import jax.numpy as jnp
from jax import lax
from jax.sharding import PartitionSpec as P

ITERS = 3


logit_scale = 0.0625
floor_value = -1e30


def swap(x, axis, k):
    return lax.ppermute(x, axis, [(i, i ^ k) for i in range(lax.axis_size(axis))])


def swap_by_core(x, axis, for_core):
    cols = lax.axis_size("col")
    scale = cols if axis == "row" else 1
    pairs = [(i, i ^ (for_core[i // cols & 1] * scale)) for i in range(lax.axis_size("row") * cols)]
    return lax.ppermute(x, ("row", "col"), pairs)


def stages(axis):
    low = 1 if axis == "row" else 0
    bits = (lax.axis_size(axis) - 1).bit_length()
    return [(at, 1 << min(2, bits - at)) for at in range(low, bits, 2)]


def digit(axis, at, size):
    return (lax.axis_index(axis) >> at) & (size - 1)


def gather_spans(x, core):
    parts = [x]
    ready = x
    for at, size in stages("col"):
        x = jnp.concatenate(parts)
        parts = [x] + [swap(x, "col", d << at) for d in range(1, min(size, 3))]
        near = parts
        if size == 4:
            passed_on = jnp.where(core == 1, parts[2], parts[1])
            near = lax.optimization_barrier((parts, passed_on))[0]
            ready = passed_on
            parts = parts + [swap_by_core(passed_on, "col", (2 << at, 1 << at))]
    got = swap(jnp.concatenate(near[1:]), "row", 1)
    mate = [swap(after(near[0], got), "row", 1), got] + [swap(part, "row", 1) for part in parts[3:]]
    return parts, mate, ready


def after(x, other):
    return lax.optimization_barrier((x, other))[0]


def placed(parts, index):
    whole = jnp.zeros((len(parts),) + parts[0].shape, parts[0].dtype)
    for d, part in enumerate(parts):
        whole = lax.dynamic_update_index_in_dim(whole, part, index ^ d, 0)
    return whole.reshape((-1,) + parts[0].shape[1:])


def gather_centroids(x, first, arrived):
    for at, size in stages("row"):
        sent = after(x, first)
        parts = [sent] + [swap(sent, "row", d << at) for d in range(1, size)]
        parts = [after(part, arrived) for part in parts]
        mate = [swap(part, "row", 1) for part in parts]
        position = digit("row", at, size)
        x = placed(parts, position)
    return jnp.concatenate([x, placed(mate, position)])


def reorder(x, blocks, k):
    x = x.reshape((blocks, -1) + x.shape[1:])
    return jnp.concatenate([x[p ^ k] for p in range(blocks)])


def unxor(x, index, blocks):
    shape = x.shape
    bit = 1
    while bit < blocks:
        pairs = x.reshape((blocks // (2 * bit), 2, -1) + shape[1:])
        x = jnp.where((index & bit) != 0, pairs[:, ::-1], pairs).reshape(shape)
        bit *= 2
    return x


def unxor_list(parts, index):
    bit = 1
    while bit < len(parts):
        parts = [jnp.where((index & bit) != 0, parts[p ^ bit], part) for p, part in enumerate(parts)]
        bit *= 2
    return parts


def tree(op, parts):
    while len(parts) > 1:
        parts = [op(parts[i], parts[i + 1]) for i in range(0, len(parts), 2)]
    return parts[0]


def add(parts):
    return tree(jnp.add, parts)


def log_sum(parts):
    high = tree(jnp.maximum, parts)
    return high + jnp.log(add([jnp.exp(part - high) for part in parts]))


def over_rows(merge, x):
    for at, size in stages("row"):
        x = merge([x] + [swap(x, "row", d << at) for d in range(1, size)])
    return x


def over_cols(merge, x):
    cols = lax.axis_size("col")
    for at, size in stages("col"):
        parts = [x]
        for d in range(1, size):
            halves = swap(x, "col", d << at).reshape(2, -1)
            parts.append(jnp.concatenate([reorder(half, cols, d << at) for half in halves]))
        x = merge(parts)
    return x


def in_thirds(x, width):
    thirds = []
    for step in range(3):
        top = lax.reduce_precision(x, 8, 7)
        thirds.append(top.astype(jnp.bfloat16))
        x = x - top
    return jnp.pad(jnp.stack(thirds), ((0, 5), (0, width - x.shape[0])))


def from_thirds(rows, count):
    thirds = rows[:3, :count].astype(jnp.float32)
    return thirds[0] + thirds[1] + thirds[2]


def per_device(spans, centroids, pattern):
    rows, cols = lax.axis_size("row"), lax.axis_size("col")
    chips = rows // 2
    me_row, me_col = lax.axis_index("row"), lax.axis_index("col")
    core = me_row % 2
    per, width = centroids.shape
    half_cols = per * chips
    group_cols = 2 * half_cols
    row_count = spans.shape[0] * cols
    mass_ratio = group_cols * cols / (row_count * rows)
    target = 1 / mass_ratio

    mate_pattern = swap(pattern, "row", 1)
    own_parts, mate_parts, ready = gather_spans(spans, core)
    tile_centroids = gather_centroids(centroids, mate_pattern, mate_parts[1])
    own_parts = [after(own_parts[0], mate_parts[1])] + own_parts[1:]
    span_halves = [jnp.concatenate(own_parts), jnp.concatenate(mate_parts)]
    at = jnp.arange(group_cols)
    row_of = at % half_cols // per * 2 + (at // half_cols ^ core)
    blocks = jnp.arange(group_cols // 128)
    in_block = ((row_of * per + at % per) // 128 == blocks[:, None]).astype(jnp.bfloat16)

    def half_scores(lists, span_half):
        listed = jnp.any(lists[:, :, None] == me_col * blocks.shape[0] + blocks, axis=1)
        listed = unxor(jnp.repeat(listed, 128 // spans.shape[0], axis=0).astype(jnp.bfloat16), me_col, cols)
        allowed_cells = jnp.dot(
            jnp.repeat(listed, spans.shape[0], axis=0), in_block, preferred_element_type=jnp.float32
        )
        products = lax.dot_general(
            span_half, tile_centroids, (((1,), (1,)), ((), ())), preferred_element_type=jnp.float32
        )
        return jnp.where(allowed_cells > 0.5, products * logit_scale, floor_value)

    scores = [half_scores(pattern, span_halves[0]), half_scores(mate_pattern, span_halves[1])]

    def with_rows(row_pot):
        return [half + row_pot[n * row_count : (n + 1) * row_count, None] for n, half in enumerate(scores)]

    def row_sums(row_pot, col_pot):
        return jnp.concatenate([jnp.sum(jnp.exp(x + col_pot[None, :]), axis=1) for x in with_rows(row_pot)])

    def col_sums(row_pot, col_pot):
        return add([jnp.sum(jnp.exp(x + col_pot[None, :]), axis=0) for x in with_rows(row_pot)])

    def rounds():
        highs = [jnp.max(half, axis=1) for half in scores]
        totals = [jnp.sum(jnp.exp(half - high[:, None]), axis=1) for half, high in zip(scores, highs)]
        row_pot = -over_cols(log_sum, jnp.concatenate([high + jnp.log(total) for high, total in zip(highs, totals)]))
        high = tree(jnp.maximum, [jnp.max(x, axis=0) for x in with_rows(row_pot)])
        total = col_sums(row_pot, -high)
        col_pot = math.log(target) - over_rows(log_sum, high + jnp.log(total))
        for sweep in range(1, ITERS):
            row_pot = row_pot - jnp.log(over_cols(add, row_sums(row_pot, col_pot)))
            if sweep < ITERS - 1:
                mass = over_rows(add, col_sums(row_pot, col_pot))
                col_pot = col_pot + math.log(target) - jnp.log(mass)
        return jnp.concatenate([row_pot.reshape(-1, group_cols), col_pot[None]])

    def nothing():
        return jnp.zeros((2 * row_count // group_cols + 1, group_cols), jnp.float32)

    known = lax.cond(core == 1, rounds, nothing)
    got = swap(known, "row", 1)
    row_pot = jnp.where(core == 1, known[:-1].reshape(-1), reorder(got[:-1].reshape(-1), 2, 1))
    col_pot = jnp.where(core == 1, known[-1], reorder(got[-1], 2, 1))

    mass = col_sums(row_pot, col_pot)
    held = add(
        [
            lax.dot_general(
                jnp.exp(x[:, :half_cols] + col_pot[None, :half_cols]).astype(jnp.bfloat16),
                span_half,
                (((0,), (0,)), ((), ())),
                preferred_element_type=jnp.float32,
            )
            for x, span_half in zip(with_rows(row_pot), span_halves)
        ]
    ).reshape(chips, per, width)
    for at, size in stages("row"):
        me = digit("row", at, size)
        held = held.reshape((-1, size) + held.shape[1:])
        low = held.astype(jnp.bfloat16)
        note = in_thirds(mass, width)
        parts, masses = [lax.dynamic_index_in_dim(held, me, 1, keepdims=False)], [from_thirds(note, group_cols)]
        for d in range(1, size):
            block = lax.dynamic_index_in_dim(low, me ^ d, 1, keepdims=False).reshape(-1, width)
            got = swap(jnp.concatenate([block, note]), "row", d << at)
            if d << at == 2:
                row_out = after(row_pot[:row_count], got)
                row_out = jnp.concatenate(unxor_list(jnp.split(row_out, cols), me_col))
            parts.append(got[: block.shape[0]].astype(jnp.float32).reshape(parts[0].shape))
            masses.append(from_thirds(got[block.shape[0] :], group_cols))
        held, mass = add(parts), add(masses)
    own_mass = lax.dynamic_slice_in_dim(mass, me_row // 2 * per, per, 0)
    col_pots = col_pot + math.log(target) - jnp.log(mass)
    pieces = jnp.split(col_pots, 2 * chips)
    pieces = [jnp.where(core == 1, pieces[n - chips], piece) for n, piece in enumerate(pieces)]
    col_pots = jnp.concatenate([pieces[n] for chip in range(chips) for n in (chip, chips + chip)])
    return (
        (held.reshape(per, width) * (target * mass_ratio / own_mass)[:, None]).astype(jnp.bfloat16),
        row_out,
        col_pots,
    )


def solution(mesh):
    placed = (P(("row", "col"), None), P(("col", "row"), None), P("row", None))
    return jax.shard_map(
        per_device,
        mesh=mesh,
        in_specs=placed,
        out_specs=(P(("col", "row"), None), P("row"), P("col")),
        check_vma=False,
    )
```
